512 devices in a mesh: aux: 64 (over x, z, core), pair: 8 (over y).
Axes of the slice: x: 4, y: 8, z: 8, core: 2. Of those that a mesh axis runs over, the one named last changes fastest.
Arguments:
- three_index: bfloat16 [57344, 2048], P('aux', 'pair'), may hold values from -0.1875 to 0.1875
- occupied_energy: float32 [64], replicated, may hold values from -2 to -0.3
- virtual_energy: float32 [20096], replicated, may hold values from 0.5 to 4
- tile_occupied: int32 [16], replicated, may hold values from 0 to 63
- tile_virtual: int32 [16], replicated, may hold values from 0 to 156
- tile_exponent: int32 [16], replicated, may hold values from -1 to 1
Outputs:
- gamma_terms: bfloat16 [57344, 2048], P('aux', 'pair')
The draws below stay inside these ranges and needn't reach their ends.
All inputs are finite; a program needn't handle non-finite values.
Results may differ from the reference program's by a relative error of at most 0.0048.
Values may be sent and summed in bfloat16 or wider, within the bound.
No kernel may reach another device: no remote copies, remote signals or barrier semaphores. Data moves between devices by JAX's collectives and lax.ppermute only.
A program may use at most 64 MiB of HBM per device.

```python
import jax
import jax.numpy as jnp

TS = 128
NOCC = 64
VT = 157
NQ = 57344
NVIRT = 20096
NT = 16
NCOL = 2048


def plant(values, stream_key, least, largest):
    longest = values.shape.index(max(values.shape))
    spots = []
    for shift in (0, 1):
        where = [jax.random.randint(jax.random.fold_in(stream_key, axis), (), 0, length) for axis, length in enumerate(values.shape)]
        where[longest] = (where[longest] + shift) % values.shape[longest]
        spots.append(tuple(where))
    return values.at[spots[0]].set(least).at[spots[1]].set(largest)


def block_levels(own_key, shape, shards, smallest, high):
    level = 1.0
    for position, parts in shards:
        heights = jax.random.uniform(jax.random.fold_in(jax.random.fold_in(own_key, 6), position), (parts,), jnp.float32, smallest / len(shards), high / len(shards))
        level = level * jnp.repeat(jnp.exp(heights), shape[position] // parts).reshape((-1,) + (1,) * (len(shape) - 1 - position))
    return level


def gaussian(key, extent, scale, bound, shards=(), dtype=jnp.bfloat16):
    level = block_levels(key, extent, shards, -0.22, 0.18) if shards else 1.0
    values = jax.random.normal(key, extent, jnp.float32) * scale * level
    return jnp.minimum(jnp.maximum(values, -bound), bound).astype(dtype)


def setup_inputs(seed: int = 0) -> dict:
    key_of = jax.random.split(jax.random.key(seed), 7)
    return {
        "three_index": gaussian(key_of[0], (NQ, NCOL), (NQ // 64) ** -0.5, 0.1875, ((0, 64), (1, 8))),
        "occupied_energy": jnp.clip(jax.random.uniform(key_of[1], (NOCC,), jnp.float32, -2.0, -0.3), -2.0, -0.3),
        "virtual_energy": jnp.clip(jax.random.uniform(key_of[2], (NVIRT,), jnp.float32, 0.5, 4.0), 0.5, 4.0),
        "tile_occupied": plant(jax.random.randint(key_of[3], (NT,), 0, NOCC), jax.random.fold_in(key_of[3], 1), 0, NOCC - 1).astype(jnp.int32),
        "tile_virtual": plant(jax.random.randint(key_of[4], (NT,), 0, VT), jax.random.fold_in(key_of[4], 1), 0, VT - 1).astype(jnp.int32),
        "tile_exponent": plant(jax.random.randint(key_of[5], (NT,), -1, 2), jax.random.fold_in(key_of[5], 1), -1, 1).astype(jnp.int32),
    }


def column_scale(tile_exponent):
    factor = jnp.where(tile_exponent == -1, 0.5, jnp.where(tile_exponent == 1, 2.0, 1.0)).astype(jnp.float32)
    return jnp.repeat(factor, TS)


def column_energy(occupied_energy, virtual_energy, tile_occupied, tile_virtual):
    virtual_cols = virtual_energy.reshape(VT, TS)[tile_virtual].reshape(-1)
    occupied_cols = jnp.repeat(occupied_energy[tile_occupied], TS)
    return virtual_cols - occupied_cols


def reference(three_index, occupied_energy, virtual_energy, tile_occupied, tile_virtual, tile_exponent):
    col_scale = column_scale(tile_exponent)
    col_energy = column_energy(occupied_energy, virtual_energy, tile_occupied, tile_virtual)
    coulomb = jnp.dot(three_index.T, three_index, preferred_element_type=jnp.float32)
    amplitude = (coulomb * (col_scale * col_scale)[:, None] * col_scale[None, :]
                 / (col_energy[:, None] + col_energy[None, :])).astype(jnp.bfloat16)
    return jnp.dot(three_index, amplitude, preferred_element_type=jnp.float32).astype(jnp.bfloat16)
```

```python
import jax
import jax.numpy as jnp
from jax import lax
from jax.sharding import Mesh, PartitionSpec as P

TS = 128
VT = 157
NX, NZ, NCORE, NPAIR = 4, 8, 2, 8
NXZ = NX * NZ
AUX = ("x", "z", "core")
PAIRS = ((0, 0), (0, 1), (-1, 1), (-1, 2), (-2, 2))
PIECE = len(PAIRS) * 2 * TS // NXZ


def ring(size, step):
    return [(i, (i + step) % size) for i in range(size)]


def tile_scale(tile_exponent):
    return jnp.where(tile_exponent == -1, 0.5, jnp.where(tile_exponent == 1, 2.0, 1.0)).astype(
        jnp.float32
    )


def tile_energy(occupied_energy, virtual_energy, tile_occupied, tile_virtual):
    return virtual_energy.reshape(VT, TS)[tile_virtual] - occupied_energy[tile_occupied][:, None]


def full_block(tiles):
    return tiles.transpose(0, 2, 1, 3).reshape(2 * TS, 2 * TS)


def body(three_index, occupied_energy, virtual_energy, tile_occupied, tile_virtual, tile_exponent):
    bf16, f32 = jnp.bfloat16, jnp.float32
    me = lax.axis_index("pair")
    core = lax.axis_index("core")
    slot = lax.axis_index(("x", "z"))

    block = {0: three_index}
    for d in (1, 2, 3):
        block[-d] = lax.ppermute(block[1 - d], "pair", ring(NPAIR, 1))
        block[d] = lax.ppermute(block[d - 1], "pair", ring(NPAIR, -1))
    half = three_index.shape[0] // 2
    block[4] = jnp.concatenate(
        [
            lax.ppermute(block[-3][:half], "pair", ring(NPAIR, 1)),
            lax.ppermute(block[3][half:], "pair", ring(NPAIR, -1)),
        ]
    )

    energy = tile_energy(occupied_energy, virtual_energy, tile_occupied, tile_virtual)
    scale = tile_scale(tile_exponent)

    def tile_of(relative, part):
        return 2 * ((me + relative + NPAIR) % NPAIR) + part

    partial = []
    for r, c in PAIRS:
        product = lax.dot_general(
            block[r], block[c], (((0,), (0,)), ((), ())), preferred_element_type=f32
        )
        partial.append(product.reshape(2, TS, 2, TS).transpose(0, 2, 1, 3))
    partial = jnp.stack(partial, axis=1)
    own = jnp.where(core == 0, partial[0], partial[1])
    other = jnp.where(core == 0, partial[1], partial[0]).astype(bf16)
    summed = own + lax.ppermute(other, "core", ring(NCORE, 1)).astype(f32)
    pieces = lax.all_to_all(
        summed.astype(bf16).reshape(NXZ, PIECE, TS), ("x", "z"), 0, 0
    )
    coulomb = jnp.sum(pieces.astype(f32), axis=0)

    denominator = jnp.stack(
        [
            jnp.stack(
                [energy[tile_of(r, core)][:, None] + energy[tile_of(c, h)][None, :] for h in (0, 1)]
            )
            for r, c in PAIRS
        ]
    ).reshape(-1, TS)
    factor = jnp.stack(
        [jnp.stack([scale[tile_of(r, core)] * scale[tile_of(c, h)] for h in (0, 1)]) for r, c in PAIRS]
    ).reshape(-1)
    factor = jnp.repeat(factor, TS)[:, None]
    own_denominator = lax.dynamic_slice_in_dim(denominator, slot * PIECE, PIECE)
    own_factor = lax.dynamic_slice_in_dim(factor, slot * PIECE, PIECE)
    amplitude = (coulomb * own_factor / own_denominator).astype(bf16)
    halves = lax.all_to_all(
        jnp.broadcast_to(amplitude[None], (NXZ, PIECE, TS)), ("x", "z"), 0, 0
    ).reshape(-1, TS)

    width = 2 * TS
    lower1 = lax.ppermute(halves[1 * width : 3 * width], "pair", ring(NPAIR, 1))
    upper1 = lax.ppermute(halves[2 * width : 4 * width], "pair", ring(NPAIR, -1))
    lower2 = lax.ppermute(halves[3 * width : 5 * width], "pair", ring(NPAIR, 2))
    mine = jnp.concatenate([halves[: 2 * width], lower1, upper1, lower2])
    tiles = lax.all_gather(mine, "core").reshape(2, 8, 2, TS, TS)

    order = ((0, False), (1, True), (-1, False), (-2, False), (2, True), (3, True), (-3, False), (4, False))
    total = None
    for n, (q, transposed) in enumerate(order):
        matrix = full_block(tiles[:, n])
        row_scale = jnp.repeat(jnp.stack([scale[tile_of(q, 0)], scale[tile_of(q, 1)]]), TS).astype(bf16)
        if transposed:
            matrix = matrix * row_scale[None, :]
            dims = (((1,), (1,)), ((), ()))
        else:
            matrix = matrix * row_scale[:, None]
            dims = (((1,), (0,)), ((), ()))
        term = lax.dot_general(block[q], matrix, dims, preferred_element_type=f32)
        total = term if total is None else total + term
    return total.astype(bf16)


def solution(mesh):
    grid = Mesh(mesh.devices.reshape(NX, NZ, NCORE, NPAIR), AUX + ("pair",))
    placed = (P(AUX, "pair"), P(), P(), P(), P(), P())
    return jax.shard_map(
        body, mesh=grid, in_specs=placed, out_specs=P(AUX, "pair"), check_vma=False
    )
```

```python
import jax
import jax.numpy as jnp
from jax import lax
from jax.experimental import pallas as pl
from jax.experimental.pallas import tpu as pltpu
from jax.sharding import Mesh, PartitionSpec as P

TS = 128
VT = 157
NT = 16
NX, NZ, NCORE, NPAIR = 4, 8, 2, 8
NXZ = NX * NZ
AUX = ("x", "z", "core")
EARLY = ((0, 0), (0, 1), (-1, 1))
LATE = ((-1, 2), (-2, 2))
PAIRS = EARLY + LATE
WIDTH = 2 * TS
PIECE = len(PAIRS) * WIDTH // NXZ
ORDER = (
    (0, False, 0, 0),
    (1, True, 0, 1),
    (-1, False, 1, 0),
    (-2, False, 1, 1),
    (2, True, 2, 0),
    (3, True, 2, 1),
    (-3, False, 3, 0),
    (4, False, 3, 1),
)
ROWS = 128
VMEM_LIMIT = 48 * 1024 * 1024
bf16, f32 = jnp.bfloat16, jnp.float32
in_vmem = pl.BlockSpec(memory_space=pltpu.VMEM)
in_smem = pl.BlockSpec(memory_space=pltpu.SMEM)


def ring(size, step):
    return [(i, (i + step) % size) for i in range(size)]


def coulomb_pairs(blocks, pairs):
    names = sorted({d for pair in pairs for d in pair})

    def kernel(*refs):
        block = dict(zip(names, refs))
        own, other = refs[len(names) :]
        core = lax.axis_index("core")
        for k, (r, c) in enumerate(pairs):
            for out, part in ((own, core), (other, 1 - core)):
                left = block[r][:, pl.ds(pl.multiple_of(part * TS, TS), TS)]
                product = lax.dot_general(
                    left, block[c][...], (((0,), (0,)), ((), ())), preferred_element_type=f32
                )
                for h in (0, 1):
                    out[k, h] = product[:, h * TS : (h + 1) * TS].astype(out.dtype)

    shape = (len(pairs), 2, TS, TS)
    return pl.pallas_call(
        kernel,
        out_shape=(jax.ShapeDtypeStruct(shape, f32), jax.ShapeDtypeStruct(shape, bf16)),
        in_specs=[in_vmem] * len(names),
        out_specs=(in_vmem, in_vmem),
        compiler_params=pltpu.CompilerParams(vmem_limit_bytes=VMEM_LIMIT),
        name="coulomb_pairs",
    )(*[blocks[d] for d in names])


def sum_cores(own, received):
    def kernel(*refs):
        out = refs[-1]
        n = 0
        for mine, theirs in zip(refs[: len(own)], refs[len(own) : -1]):
            size = mine.shape[0]
            out[n : n + size] = (mine[...] + theirs[...].astype(f32)).astype(bf16)
            n += size

    total = sum(a.shape[0] for a in own)
    return pl.pallas_call(
        kernel,
        out_shape=jax.ShapeDtypeStruct((total,) + own[0].shape[1:], bf16),
        in_specs=[in_vmem] * (2 * len(own)),
        out_specs=in_vmem,
        compiler_params=pltpu.CompilerParams(vmem_limit_bytes=VMEM_LIMIT),
        name="sum_cores",
    )(*own, *received)


def amplitude_piece(pieces, denominator):
    def kernel(pieces_ref, denominator_ref, out):
        total = jnp.sum(pieces_ref[...].astype(f32), axis=0)
        out[...] = jnp.broadcast_to((total / denominator_ref[...]).astype(bf16)[None], out.shape)

    return pl.pallas_call(
        kernel,
        out_shape=jax.ShapeDtypeStruct(pieces.shape, bf16),
        in_specs=[in_vmem, in_vmem],
        out_specs=in_vmem,
        compiler_params=pltpu.CompilerParams(vmem_limit_bytes=VMEM_LIMIT),
        name="amplitude_piece",
    )(pieces, denominator)


def gamma_rows(blocks, last, mine, theirs, tile_exponent):
    rows, width = blocks[0].shape
    names = [q for q, *_ in ORDER if q != 4]
    steps = rows // ROWS

    def kernel(*refs):
        block = dict(zip(names, refs))
        block[4] = refs[len(names)]
        n = len(names) + 1
        own, other = refs[n : n + 4], refs[n + 4 : n + 8]
        exponent, out, matrix = refs[n + 8 :]
        me = lax.axis_index("pair")
        core = lax.axis_index("core")

        @pl.when(pl.program_id(0) == 0)
        def _():
            for i, (q, transposed, array, k) in enumerate(ORDER):
                for source, part in ((own, core), (other, 1 - core)):
                    for h in (0, 1):
                        tile = 2 * lax.rem(me + q + NPAIR, NPAIR) + (h if transposed else part)
                        level = exponent[tile]
                        scale = jnp.where(level == -1, 0.5, jnp.where(level == 1, 2.0, 1.0))
                        values = source[array][k, h].astype(f32) * scale.astype(f32)
                        row = pl.multiple_of(part * TS, TS)
                        matrix[i, pl.ds(row, TS), h * TS : (h + 1) * TS] = values.astype(bf16)

        total = None
        for i, (q, transposed, _, _) in enumerate(ORDER):
            dims = (((1,), (1 if transposed else 0,)), ((), ()))
            term = lax.dot_general(block[q][...], matrix[i], dims, preferred_element_type=f32)
            total = term if total is None else total + term
        out[...] = total.astype(bf16)

    row_block = pl.BlockSpec((ROWS, width), lambda i: (i, 0))
    return pl.pallas_call(
        kernel,
        grid=(steps,),
        out_shape=jax.ShapeDtypeStruct((rows, width), bf16),
        in_specs=[row_block] * 8 + [in_vmem] * 8 + [in_smem],
        out_specs=row_block,
        scratch_shapes=[pltpu.VMEM((len(ORDER), WIDTH, WIDTH), bf16)],
        compiler_params=pltpu.CompilerParams(vmem_limit_bytes=VMEM_LIMIT),
        name="gamma_rows",
    )(*[blocks[q] for q in names], last, *mine, *theirs, tile_exponent)


def body(three_index, occupied_energy, virtual_energy, tile_occupied, tile_virtual, tile_exponent):
    me = lax.axis_index("pair")
    core = lax.axis_index("core")
    slot = lax.axis_index(("x", "z"))
    up, down = ring(NPAIR, 1), ring(NPAIR, -1)
    swap = ring(NCORE, 1)

    block = {0: three_index}
    for d in (1, 2):
        block[-d] = lax.ppermute(block[1 - d], "pair", up)
        block[d] = lax.ppermute(block[d - 1], "pair", down)

    energy = virtual_energy.reshape(VT, TS)[tile_virtual] - occupied_energy[tile_occupied][:, None]
    scale = jnp.where(tile_exponent == -1, 0.5, jnp.where(tile_exponent == 1, 2.0, 1.0)).astype(f32)
    table = jnp.concatenate([energy, jnp.broadcast_to(scale[:, None], (NT, TS))], axis=1)
    table = jnp.concatenate([table, table, table])
    near = lax.dynamic_slice_in_dim(table, 2 * me + NT - 4, 10).reshape(5, 2, 2 * TS)
    row = lax.dynamic_index_in_dim(near, core, 1, keepdims=False)
    row_of = jnp.stack([row[r + 2] for r, _ in PAIRS])
    column_of = jnp.stack([near[c + 2] for _, c in PAIRS])
    denominator = (
        (row_of[:, None, :TS, None] + column_of[:, :, None, :TS])
        / (row_of[:, None, TS:, None] * column_of[:, :, None, TS:])
    ).reshape(-1, TS)
    own_denominator = lax.dynamic_slice_in_dim(denominator, slot * PIECE, PIECE)

    own_early, other_early = coulomb_pairs(block, EARLY)
    got_early = lax.ppermute(other_early, "core", swap)
    own_late, other_late = coulomb_pairs(block, LATE)
    got_late = lax.ppermute(other_late, "core", swap)
    summed = sum_cores((own_early, own_late), (got_early, got_late))

    block[-3] = lax.ppermute(block[-2], "pair", up)
    block[3] = lax.ppermute(block[2], "pair", down)
    pieces = lax.all_to_all(summed.reshape(NXZ, PIECE, TS), ("x", "z"), 0, 0)
    pieces, block[-3], block[3], own_denominator = lax.optimization_barrier(
        (pieces, block[-3], block[3], own_denominator)
    )

    half = three_index.shape[0] // 2
    last_upper = lax.ppermute(block[-3][:half], "pair", up)
    last_lower = lax.ppermute(block[3][half:], "pair", down)
    halves = lax.all_to_all(amplitude_piece(pieces, own_denominator), ("x", "z"), 0, 0)
    halves, last_upper, last_lower = lax.optimization_barrier((halves, last_upper, last_lower))
    last = jnp.concatenate([last_upper, last_lower])

    halves = halves.reshape(len(PAIRS), 2, TS, TS)
    mine = (
        halves[0:2],
        lax.ppermute(halves[1:3], "pair", up),
        lax.ppermute(halves[2:4], "pair", down),
        lax.ppermute(halves[3:5], "pair", ring(NPAIR, 2)),
    )
    theirs = lax.ppermute(jnp.concatenate(mine), "core", swap)
    theirs = tuple(theirs[2 * i : 2 * i + 2] for i in range(4))
    return gamma_rows(block, last, mine, theirs, tile_exponent)


def solution(mesh):
    grid = Mesh(mesh.devices.reshape(NX, NZ, NCORE, NPAIR), AUX + ("pair",))
    placed = (P(AUX, "pair"), P(), P(), P(), P(), P())
    return jax.shard_map(
        body, mesh=grid, in_specs=placed, out_specs=P(AUX, "pair"), check_vma=False
    )
```

```python
import jax
import jax.numpy as jnp
from jax import lax
from jax.experimental import pallas as pl
from jax.experimental.pallas import tpu as pltpu
from jax.sharding import Mesh, PartitionSpec as P

TS = 128
VT = 157
NT = 16
NX, NZ, NCORE, NPAIR = 4, 8, 2, 8
NXZ = NX * NZ
AUX = ("x", "z", "core")
EARLY = ((0, 0), (0, 1), (-1, 1))
LATE = ((-1, 2), (-2, 2))
PAIRS = EARLY + LATE
WIDTH = 2 * TS
PIECE = len(PAIRS) * WIDTH // NXZ
ORDER = (
    (0, False, 0, 0),
    (1, True, 0, 1),
    (-1, False, 1, 0),
    (-2, False, 1, 1),
    (2, True, 2, 0),
    (3, True, 2, 1),
    (-3, False, 3, 0),
    (4, False, 3, 1),
)
ROWS = 224
VMEM_LIMIT = 48 * 1024 * 1024
bf16, f32 = jnp.bfloat16, jnp.float32
in_vmem = pl.BlockSpec(memory_space=pltpu.VMEM)


def ring(size, step):
    return [(i, (i + step) % size) for i in range(size)]


def coulomb_pairs(blocks, pairs):
    names = sorted({d for pair in pairs for d in pair})

    def kernel(*refs):
        block = dict(zip(names, refs))
        own, other = refs[len(names) :]
        core = lax.axis_index("core")
        for k, (r, c) in enumerate(pairs):
            for out, part in ((own, core), (other, 1 - core)):
                left = block[r][:, pl.ds(pl.multiple_of(part * TS, TS), TS)]
                product = lax.dot_general(
                    left, block[c][...], (((0,), (0,)), ((), ())), preferred_element_type=f32
                )
                for h in (0, 1):
                    out[k, h] = product[:, h * TS : (h + 1) * TS].astype(out.dtype)

    shape = (len(pairs), 2, TS, TS)
    return pl.pallas_call(
        kernel,
        out_shape=(jax.ShapeDtypeStruct(shape, f32), jax.ShapeDtypeStruct(shape, bf16)),
        in_specs=[in_vmem] * len(names),
        out_specs=(in_vmem, in_vmem),
        compiler_params=pltpu.CompilerParams(vmem_limit_bytes=VMEM_LIMIT),
        name="coulomb_pairs",
    )(*[blocks[d] for d in names])


def sum_cores(own, received):
    def kernel(*refs):
        out = refs[-1]
        n = 0
        for mine, theirs in zip(refs[: len(own)], refs[len(own) : -1]):
            size = mine.shape[0]
            out[n : n + size] = (mine[...] + theirs[...].astype(f32)).astype(bf16)
            n += size

    total = sum(a.shape[0] for a in own)
    return pl.pallas_call(
        kernel,
        out_shape=jax.ShapeDtypeStruct((total,) + own[0].shape[1:], bf16),
        in_specs=[in_vmem] * (2 * len(own)),
        out_specs=in_vmem,
        compiler_params=pltpu.CompilerParams(vmem_limit_bytes=VMEM_LIMIT),
        name="sum_cores",
    )(*own, *received)


def amplitude_piece(pieces, denominator):
    def kernel(pieces_ref, denominator_ref, out):
        total = jnp.sum(pieces_ref[...].astype(f32), axis=0)
        out[...] = jnp.broadcast_to((total / denominator_ref[...]).astype(bf16)[None], out.shape)

    return pl.pallas_call(
        kernel,
        out_shape=jax.ShapeDtypeStruct(pieces.shape, bf16),
        in_specs=[in_vmem, in_vmem],
        out_specs=in_vmem,
        compiler_params=pltpu.CompilerParams(vmem_limit_bytes=VMEM_LIMIT),
        name="amplitude_piece",
    )(pieces, denominator)


def gamma_rows(blocks, last, mine, theirs, scales):
    rows, width = blocks[0].shape
    names = [q for q, *_ in ORDER if q != 4]
    half = rows // len(last)

    def kernel(*refs):
        block = dict(zip(names, refs))
        n = len(names)
        last_refs, refs = refs[n : n + len(last)], refs[n + len(last) :]
        own, other, scale, out, matrix = refs[:4], refs[4], refs[5], refs[6], refs[7]
        core = lax.axis_index("core")
        for i, (q, transposed, array, k) in enumerate(ORDER):
            for part, values in ((core, own[array].at[k]), (1 - core, other.at[2 * array + k])):
                place = pl.ds(pl.multiple_of(part * TS, TS), TS)
                for h in (0, 1):
                    tile = values[h].astype(f32)
                    if transposed:
                        tile = tile.T * scale[2 * i + h : 2 * i + h + 1]
                        matrix[i, h * TS : (h + 1) * TS, place] = tile.astype(bf16)
                    else:
                        tile = tile * scale[pl.ds(2 * i + part, 1)]
                        matrix[i, place, h * TS : (h + 1) * TS] = tile.astype(bf16)

        for start in range(0, rows, ROWS):
            total = None
            for i, (q, *_) in enumerate(ORDER):
                if q == 4:
                    left = [
                        last_refs[j][max(start - j * half, 0) : start + ROWS - j * half]
                        for j in range(len(last))
                        if start < (j + 1) * half and start + ROWS > j * half
                    ]
                    left = left[0] if len(left) == 1 else jnp.concatenate(left)
                else:
                    left = block[q][start : start + ROWS]
                term = jnp.dot(left, matrix[i], preferred_element_type=f32)
                total = term if total is None else total + term
            out[start : start + ROWS] = total.astype(bf16)

    return pl.pallas_call(
        kernel,
        out_shape=jax.ShapeDtypeStruct((rows, width), bf16),
        in_specs=[in_vmem] * (len(names) + len(last) + 6),
        out_specs=in_vmem,
        scratch_shapes=[pltpu.VMEM((len(ORDER), WIDTH, WIDTH), bf16)],
        compiler_params=pltpu.CompilerParams(vmem_limit_bytes=VMEM_LIMIT),
        name="gamma_rows",
    )(*[blocks[q] for q in names], *last, *mine, theirs, scales)


def body(three_index, occupied_energy, virtual_energy, tile_occupied, tile_virtual, tile_exponent):
    me = lax.axis_index("pair")
    core = lax.axis_index("core")
    slot = lax.axis_index(("x", "z"))
    up, down = ring(NPAIR, 1), ring(NPAIR, -1)
    swap = ring(NCORE, 1)

    block = {0: three_index}
    for d in (1, 2):
        block[-d] = lax.ppermute(block[1 - d], "pair", up)
        block[d] = lax.ppermute(block[d - 1], "pair", down)

    energy = virtual_energy.reshape(VT, TS)[tile_virtual] - occupied_energy[tile_occupied][:, None]
    scale = jnp.where(tile_exponent == -1, 0.5, jnp.where(tile_exponent == 1, 2.0, 1.0)).astype(f32)
    table = jnp.concatenate([energy, jnp.broadcast_to(scale[:, None], (NT, TS))], axis=1)
    table = jnp.concatenate([table, table, table])
    near = lax.dynamic_slice_in_dim(table, 2 * me + NT - 4, 10).reshape(5, 2, 2 * TS)
    row = lax.dynamic_index_in_dim(near, core, 1, keepdims=False)
    row_of = jnp.stack([row[r + 2] for r, _ in PAIRS])
    column_of = jnp.stack([near[c + 2] for _, c in PAIRS])
    denominator = (
        (row_of[:, None, :TS, None] + column_of[:, :, None, :TS])
        / (row_of[:, None, TS:, None] * column_of[:, :, None, TS:])
    ).reshape(-1, TS)
    own_denominator = lax.dynamic_slice_in_dim(denominator, slot * PIECE, PIECE)
    turned = lax.dynamic_slice_in_dim(table[:, TS:], 2 * me, NT).reshape(NPAIR, 2, TS)
    scales = jnp.concatenate([turned[q % NPAIR] for q, *_ in ORDER])

    own_early, other_early = coulomb_pairs(block, EARLY)
    got_early = lax.ppermute(other_early, "core", swap)
    own_late, other_late = coulomb_pairs(block, LATE)
    got_late = lax.ppermute(other_late, "core", swap)
    summed = sum_cores((own_early, own_late), (got_early, got_late))

    summed, block[-2], block[2], scales = lax.optimization_barrier(
        (summed, block[-2], block[2], scales)
    )
    block[-3] = lax.ppermute(block[-2], "pair", up)
    block[3] = lax.ppermute(block[2], "pair", down)
    pieces = lax.all_to_all(summed.reshape(NXZ, PIECE, TS), ("x", "z"), 0, 0)
    pieces, block[-3], block[3], own_denominator = lax.optimization_barrier(
        (pieces, block[-3], block[3], own_denominator)
    )

    half = three_index.shape[0] // 2
    last_upper = lax.ppermute(block[-3][:half], "pair", up)
    last_lower = lax.ppermute(block[3][half:], "pair", down)
    halves = lax.all_to_all(amplitude_piece(pieces, own_denominator), ("x", "z"), 0, 0)
    halves, last_upper, last_lower = lax.optimization_barrier((halves, last_upper, last_lower))

    halves = halves.reshape(len(PAIRS), 2, TS, TS)
    mine = (
        halves[0:2],
        lax.ppermute(halves[1:3], "pair", up),
        lax.ppermute(halves[2:4], "pair", down),
        lax.ppermute(halves[3:5], "pair", ring(NPAIR, 2)),
    )
    theirs = lax.ppermute(jnp.concatenate(mine), "core", swap)
    return gamma_rows(block, (last_upper, last_lower), mine, theirs, scales)


def solution(mesh):
    grid = Mesh(mesh.devices.reshape(NX, NZ, NCORE, NPAIR), AUX + ("pair",))
    placed = (P(AUX, "pair"), P(), P(), P(), P(), P())
    return jax.shard_map(
        body, mesh=grid, in_specs=placed, out_specs=P(AUX, "pair"), check_vma=False
    )
```

```python
import jax
import jax.numpy as jnp
from jax import lax
from jax.experimental import pallas as pl
from jax.experimental.pallas import tpu as pltpu
from jax.sharding import Mesh, PartitionSpec as P

TS = 128
VT = 157
NT = 16
NX, NZ, NCORE, NPAIR = 4, 8, 2, 8
NXZ = NX * NZ
AUX = ("x", "z", "core")
EARLY = ((0, 0), (0, 1), (-1, 1))
LATE = ((-1, 2), (-2, 2))
PAIRS = EARLY + LATE
WIDTH = 2 * TS
PIECE = WIDTH // NXZ
ORDER = (
    (0, False),
    (1, True),
    (-1, False),
    (-2, False),
    (2, True),
    (3, True),
    (-3, False),
    (4, False),
)
ROWS = 224
VMEM_LIMIT = 48 * 1024 * 1024
bf16, f32 = jnp.bfloat16, jnp.float32
in_vmem = pl.BlockSpec(memory_space=pltpu.VMEM)


def ring(size, step):
    return [(i, (i + step) % size) for i in range(size)]


def coulomb_pairs(blocks, pairs):
    names = sorted({d for pair in pairs for d in pair})

    def kernel(*refs):
        block = dict(zip(names, refs))
        own, other = refs[len(names) :]
        core = lax.axis_index("core")
        for k, (r, c) in enumerate(pairs):
            for out, part in ((own, core), (other, 1 - core)):
                left = block[r][:, pl.ds(pl.multiple_of(part * TS, TS), TS)]
                product = lax.dot_general(
                    left, block[c][...], (((0,), (0,)), ((), ())), preferred_element_type=f32
                )
                for h in (0, 1):
                    out[k, h] = product[:, h * TS : (h + 1) * TS].astype(out.dtype)

    shape = (len(pairs), 2, TS, TS)
    return pl.pallas_call(
        kernel,
        out_shape=(jax.ShapeDtypeStruct(shape, f32), jax.ShapeDtypeStruct(shape, bf16)),
        in_specs=[in_vmem] * len(names),
        out_specs=(in_vmem, in_vmem),
        compiler_params=pltpu.CompilerParams(vmem_limit_bytes=VMEM_LIMIT),
        name="coulomb_pairs",
    )(*[blocks[d] for d in names])


def sum_cores(own, received):
    pairs = own.shape[0]

    def kernel(mine, theirs, out):
        total = (mine[...] + theirs[...].astype(f32)).reshape(pairs, NXZ, PIECE, TS)
        out[...] = jnp.concatenate([total[k] for k in range(pairs)], axis=1).astype(bf16)

    return pl.pallas_call(
        kernel,
        out_shape=jax.ShapeDtypeStruct((NXZ, pairs * PIECE, TS), bf16),
        in_specs=[in_vmem] * 2,
        out_specs=in_vmem,
        compiler_params=pltpu.CompilerParams(vmem_limit_bytes=VMEM_LIMIT),
        name="sum_cores",
    )(own, received)


def early_piece(pieces, denominator):
    def kernel(pieces_ref, denominator_ref, kept, sent, second):
        total = jnp.sum(pieces_ref[...].astype(f32), axis=0) / denominator_ref[...]
        kept[...] = total[: 2 * PIECE].astype(bf16)
        sent[...] = total[PIECE:].astype(bf16)
        second[...] = total[2 * PIECE :]

    shape = jax.ShapeDtypeStruct((2 * PIECE, TS), bf16)
    return pl.pallas_call(
        kernel,
        out_shape=(shape, shape, jax.ShapeDtypeStruct((PIECE, TS), f32)),
        in_specs=[in_vmem] * 2,
        out_specs=(in_vmem,) * 3,
        compiler_params=pltpu.CompilerParams(vmem_limit_bytes=VMEM_LIMIT),
        name="early_piece",
    )(pieces, denominator)


def late_piece(pieces, denominator, second):
    def kernel(pieces_ref, denominator_ref, second_ref, down, up):
        total = jnp.sum(pieces_ref[...].astype(f32), axis=0) / denominator_ref[...]
        up[...] = total.astype(bf16)
        down[...] = jnp.concatenate([second_ref[...], total[:PIECE]]).astype(bf16)

    shape = jax.ShapeDtypeStruct((2 * PIECE, TS), bf16)
    return pl.pallas_call(
        kernel,
        out_shape=(shape, shape),
        in_specs=[in_vmem] * 3,
        out_specs=(in_vmem,) * 2,
        compiler_params=pltpu.CompilerParams(vmem_limit_bytes=VMEM_LIMIT),
        name="late_piece",
    )(pieces, denominator, second)


def spread(*pieces):
    rows = len(pieces) * 2 * PIECE

    def kernel(*refs):
        whole = jnp.concatenate([ref[...] for ref in refs[:-1]])
        refs[-1][...] = jnp.broadcast_to(whole[None], (NXZ, rows, TS))

    return pl.pallas_call(
        kernel,
        out_shape=jax.ShapeDtypeStruct((NXZ, rows, TS), bf16),
        in_specs=[in_vmem] * len(pieces),
        out_specs=in_vmem,
        compiler_params=pltpu.CompilerParams(vmem_limit_bytes=VMEM_LIMIT),
        name="spread",
    )(*pieces)


def gamma_rows(blocks, last, mine, theirs, scales):
    rows, width = blocks[0].shape
    names = [q for q, *_ in ORDER if q != 4]
    half = rows // len(last)

    def kernel(*refs):
        block = dict(zip(names, refs))
        n = len(names)
        last_refs, refs = refs[n : n + len(last)], refs[n + len(last) :]
        own, other, scale, out, matrix = refs
        core = lax.axis_index("core")
        for pair in range(0, len(ORDER), 2):
            for part, source in ((core, own), (1 - core, other)):
                place = pl.ds(pl.multiple_of(part * TS, TS), TS)
                both = source[:, pair * PIECE : (pair + 2) * PIECE].astype(f32)
                for k in (0, 1):
                    i = pair + k
                    tiles = both[:, k * PIECE : (k + 1) * PIECE].reshape(2, TS, TS)
                    for h in (0, 1):
                        if ORDER[i][1]:
                            tile = tiles[h].T * scale[2 * i + h : 2 * i + h + 1]
                            matrix[i, h * TS : (h + 1) * TS, place] = tile.astype(bf16)
                        else:
                            tile = tiles[h] * scale[pl.ds(2 * i + part, 1)]
                            matrix[i, place, h * TS : (h + 1) * TS] = tile.astype(bf16)

        for start in range(0, rows, ROWS):
            total = None
            for i, (q, *_) in enumerate(ORDER):
                if q == 4:
                    left = [
                        last_refs[j][max(start - j * half, 0) : start + ROWS - j * half]
                        for j in range(len(last))
                        if start < (j + 1) * half and start + ROWS > j * half
                    ]
                    left = left[0] if len(left) == 1 else jnp.concatenate(left)
                else:
                    left = block[q][start : start + ROWS]
                term = jnp.dot(left, matrix[i], preferred_element_type=f32)
                total = term if total is None else total + term
            out[start : start + ROWS] = total.astype(bf16)

    return pl.pallas_call(
        kernel,
        out_shape=jax.ShapeDtypeStruct((rows, width), bf16),
        in_specs=[in_vmem] * (len(names) + len(last) + 3),
        out_specs=in_vmem,
        scratch_shapes=[pltpu.VMEM((len(ORDER), WIDTH, WIDTH), bf16)],
        compiler_params=pltpu.CompilerParams(vmem_limit_bytes=VMEM_LIMIT),
        name="gamma_rows",
    )(*[blocks[q] for q in names], *last, mine, theirs, scales)


def body(three_index, occupied_energy, virtual_energy, tile_occupied, tile_virtual, tile_exponent):
    me = lax.axis_index("pair")
    core = lax.axis_index("core")
    slot = lax.axis_index(("x", "z"))
    up, down = ring(NPAIR, 1), ring(NPAIR, -1)
    swap = ring(NCORE, 1)

    block = {0: three_index}
    for d in (1, 2):
        block[-d] = lax.ppermute(block[1 - d], "pair", up)
        block[d] = lax.ppermute(block[d - 1], "pair", down)

    energy = virtual_energy.reshape(VT, TS)[tile_virtual] - occupied_energy[tile_occupied][:, None]
    scale = jnp.where(tile_exponent == -1, 0.5, jnp.where(tile_exponent == 1, 2.0, 1.0)).astype(f32)
    table = jnp.concatenate([energy, jnp.broadcast_to(scale[:, None], (NT, TS))], axis=1)
    table = jnp.concatenate([table, table, table])
    near = lax.dynamic_slice_in_dim(table, 2 * me + NT - 4, 10).reshape(5, 2, 2 * TS)
    row = lax.dynamic_index_in_dim(near, core, 1, keepdims=False)
    row_of = jnp.stack([row[r + 2] for r, _ in PAIRS])
    column_of = jnp.stack([near[c + 2] for _, c in PAIRS])
    denominator = (
        (row_of[:, None, :TS, None] + column_of[:, :, None, :TS])
        / (row_of[:, None, TS:, None] * column_of[:, :, None, TS:])
    ).reshape(len(PAIRS), NXZ, PIECE, TS)
    denominator = lax.dynamic_index_in_dim(denominator, slot, 1, keepdims=False).reshape(-1, TS)
    split = len(EARLY) * PIECE
    turned = lax.dynamic_slice_in_dim(table[:, TS:], 2 * me, NT).reshape(NPAIR, 2, TS)
    scales = jnp.concatenate([turned[q % NPAIR] for q, *_ in ORDER])

    own, other = coulomb_pairs(block, EARLY)
    early = sum_cores(own, lax.ppermute(other, "core", swap))
    early = lax.all_to_all(early, ("x", "z"), 0, 0)
    own, other = coulomb_pairs(block, LATE)
    late = sum_cores(own, lax.ppermute(other, "core", swap))
    late, block[-2], block[2] = lax.optimization_barrier((late, block[-2], block[2]))
    late = lax.all_to_all(late, ("x", "z"), 0, 0)
    block[-3] = lax.ppermute(block[-2], "pair", up)
    block[3] = lax.ppermute(block[2], "pair", down)

    kept, sent, second = early_piece(early, denominator[:split])
    lower1 = lax.ppermute(sent, "pair", up)
    sent, sent2 = late_piece(late, denominator[split:], second)
    upper1 = lax.ppermute(sent, "pair", down)
    lower2 = lax.ppermute(sent2, "pair", ring(NPAIR, 2))
    copies = spread(kept, lower1, upper1, lower2)
    copies, block[-3], block[3], scales = lax.optimization_barrier(
        (copies, block[-3], block[3], scales)
    )

    half = three_index.shape[0] // 2
    last_upper = lax.ppermute(block[-3][:half], "pair", up)
    last_lower = lax.ppermute(block[3][half:], "pair", down)
    mine = lax.all_to_all(copies, ("x", "z"), 0, 0)
    mine, last_upper, last_lower = lax.optimization_barrier((mine, last_upper, last_lower))
    theirs = lax.ppermute(mine, "core", swap)
    return gamma_rows(block, (last_upper, last_lower), mine, theirs, scales)


def solution(mesh):
    grid = Mesh(mesh.devices.reshape(NX, NZ, NCORE, NPAIR), AUX + ("pair",))
    placed = (P(AUX, "pair"), P(), P(), P(), P(), P())
    return jax.shard_map(
        body, mesh=grid, in_specs=placed, out_specs=P(AUX, "pair"), check_vma=False
    )
```

```python
import jax
import jax.numpy as jnp
from jax import lax
from jax.experimental import pallas as pl
from jax.experimental.pallas import tpu as pltpu
from jax.sharding import Mesh, PartitionSpec as P

TS = 128
VT = 157
NT = 16
NX, NZ, NCORE, NPAIR = 4, 8, 2, 8
NXZ = NX * NZ
AUX = ("x", "z", "core")
EARLY = ((0, 0), (0, 1), (-1, 1))
LATE = ((-1, 2), (-2, 2))
PAIRS = EARLY + LATE
WIDTH = 2 * TS
PIECE = WIDTH // NXZ
ORDER = (
    (0, False),
    (1, True),
    (-1, False),
    (-2, False),
    (2, True),
    (3, True),
    (-3, False),
    (4, False),
)
ROWS = 224
VMEM_LIMIT = 12 * 1024 * 1024
bf16, f32 = jnp.bfloat16, jnp.float32
in_vmem = pl.BlockSpec(memory_space=pltpu.VMEM)
in_smem = pl.BlockSpec(memory_space=pltpu.SMEM)


def ring(size, step):
    return [(i, (i + step) % size) for i in range(size)]


def tables(occupied_energy, virtual_energy, tile_occupied, tile_virtual, tile_exponent):
    def kernel(occupied, virtual, occupied_of, virtual_of, exponent, denominator, scales):
        me = lax.axis_index("pair")
        core = lax.axis_index("core")
        slot = lax.axis_index("x") * NZ + lax.axis_index("z")
        half, first = slot // (NXZ // 2), (slot % (NXZ // 2)) * PIECE

        def tile_of(relative, part):
            return lax.rem(2 * (me + relative + NPAIR) + part, NT)

        def energy(tile):
            return virtual[pl.ds(virtual_of[tile], 1)] - occupied[occupied_of[tile]]

        def scale(tile):
            level = exponent[tile]
            return jnp.where(level == -1, 0.5, jnp.where(level == 1, 2.0, 1.0)).astype(f32)

        lane = lax.broadcasted_iota(jnp.int32, (PIECE, TS), 1)
        chosen = lane == first + lax.broadcasted_iota(jnp.int32, (PIECE, TS), 0)
        for k, (r, c) in enumerate(PAIRS):
            row, column = tile_of(r, core), tile_of(c, half)
            of_row = jnp.sum(jnp.where(chosen, energy(row), 0.0), axis=1, keepdims=True)
            level = jnp.full((PIECE, TS), scale(row) * scale(column), f32)
            denominator[k * PIECE : (k + 1) * PIECE] = (of_row + energy(column)) / level
        for i, (q, _) in enumerate(ORDER):
            for part in (0, 1):
                n = 2 * i + part
                scales[n : n + 1] = jnp.full((1, TS), scale(tile_of(q, part)), f32)

    return pl.pallas_call(
        kernel,
        out_shape=(
            jax.ShapeDtypeStruct((len(PAIRS) * PIECE, TS), f32),
            jax.ShapeDtypeStruct((2 * len(ORDER), TS), f32),
        ),
        in_specs=[in_smem, in_vmem, in_smem, in_smem, in_smem],
        out_specs=(in_vmem, in_vmem),
        compiler_params=pltpu.CompilerParams(vmem_limit_bytes=VMEM_LIMIT),
        name="tables",
    )(occupied_energy, virtual_energy.reshape(VT, TS), tile_occupied, tile_virtual, tile_exponent)


def coulomb_pairs(blocks, pairs):
    names = sorted({d for pair in pairs for d in pair})

    def kernel(*refs):
        block = dict(zip(names, refs))
        own, other = refs[len(names) :]
        core = lax.axis_index("core")
        for k, (r, c) in enumerate(pairs):
            for out, part in ((own, core), (other, 1 - core)):
                left = block[r][:, pl.ds(pl.multiple_of(part * TS, TS), TS)]
                product = lax.dot_general(
                    left, block[c][...], (((0,), (0,)), ((), ())), preferred_element_type=f32
                )
                for h in (0, 1):
                    out[k, h] = product[:, h * TS : (h + 1) * TS].astype(out.dtype)

    shape = (len(pairs), 2, TS, TS)
    return pl.pallas_call(
        kernel,
        out_shape=(jax.ShapeDtypeStruct(shape, f32), jax.ShapeDtypeStruct(shape, bf16)),
        in_specs=[in_vmem] * len(names),
        out_specs=(in_vmem, in_vmem),
        compiler_params=pltpu.CompilerParams(vmem_limit_bytes=VMEM_LIMIT),
        name="coulomb_pairs",
    )(*[blocks[d] for d in names])


def sum_cores(own, received):
    pairs = sum(a.shape[0] for a in own)

    def kernel(*refs):
        parts = []
        for mine, theirs in zip(refs[: len(own)], refs[len(own) : -1]):
            count = mine.shape[0]
            total = (mine[...] + theirs[...].astype(f32)).reshape(count, NXZ, PIECE, TS)
            parts += [total[k] for k in range(count)]
        refs[-1][...] = jnp.concatenate(parts, axis=1).astype(bf16)

    return pl.pallas_call(
        kernel,
        out_shape=jax.ShapeDtypeStruct((NXZ, pairs * PIECE, TS), bf16),
        in_specs=[in_vmem] * (2 * len(own)),
        out_specs=in_vmem,
        compiler_params=pltpu.CompilerParams(vmem_limit_bytes=VMEM_LIMIT),
        name="sum_cores",
    )(*own, *received)


def amplitude_pieces(pieces, denominator):
    def kernel(pieces_ref, denominator_ref, *outs):
        total = jnp.sum(pieces_ref[...].astype(f32), axis=0) / denominator_ref[...]
        for k, out in enumerate(outs):
            out[...] = total[k * PIECE : (k + 2) * PIECE].astype(bf16)

    shape = jax.ShapeDtypeStruct((2 * PIECE, TS), bf16)
    return pl.pallas_call(
        kernel,
        out_shape=(shape,) * 4,
        in_specs=[in_vmem] * 2,
        out_specs=(in_vmem,) * 4,
        compiler_params=pltpu.CompilerParams(vmem_limit_bytes=VMEM_LIMIT),
        name="amplitude_pieces",
    )(pieces, denominator)


def spread(*pieces):
    rows = len(pieces) * 2 * PIECE

    def kernel(*refs):
        whole = jnp.concatenate([ref[...] for ref in refs[:-1]])
        refs[-1][...] = jnp.broadcast_to(whole[None], (NXZ, rows, TS))

    return pl.pallas_call(
        kernel,
        out_shape=jax.ShapeDtypeStruct((NXZ, rows, TS), bf16),
        in_specs=[in_vmem] * len(pieces),
        out_specs=in_vmem,
        compiler_params=pltpu.CompilerParams(vmem_limit_bytes=VMEM_LIMIT),
        name="spread",
    )(*pieces)


def gamma_rows(blocks, mine, theirs, scales):
    rows, width = blocks[0].shape
    names = [q for q, _ in ORDER]

    def kernel(*refs):
        block = dict(zip(names, refs))
        own, other, scale, out, matrix = refs[len(names) :]
        core = lax.axis_index("core")
        for pair in range(0, len(ORDER), 2):
            for part, source in ((core, own), (1 - core, other)):
                place = pl.ds(pl.multiple_of(part * TS, TS), TS)
                both = source[:, pair * PIECE : (pair + 2) * PIECE].astype(f32)
                for k in (0, 1):
                    i = pair + k
                    tiles = both[:, k * PIECE : (k + 1) * PIECE].reshape(2, TS, TS)
                    for h in (0, 1):
                        if ORDER[i][1]:
                            tile = tiles[h].T * scale[2 * i + h : 2 * i + h + 1]
                            matrix[i, h * TS : (h + 1) * TS, place] = tile.astype(bf16)
                        else:
                            tile = tiles[h] * scale[pl.ds(2 * i + part, 1)]
                            matrix[i, place, h * TS : (h + 1) * TS] = tile.astype(bf16)

        for start in range(0, rows, ROWS):
            total = None
            for i, (q, *_) in enumerate(ORDER):
                left = block[q][start : start + ROWS]
                term = jnp.dot(left, matrix[i], preferred_element_type=f32)
                total = term if total is None else total + term
            out[start : start + ROWS] = total.astype(bf16)

    return pl.pallas_call(
        kernel,
        out_shape=jax.ShapeDtypeStruct((rows, width), bf16),
        in_specs=[in_vmem] * (len(names) + 3),
        out_specs=in_vmem,
        scratch_shapes=[pltpu.VMEM((len(ORDER), WIDTH, WIDTH), bf16)],
        compiler_params=pltpu.CompilerParams(vmem_limit_bytes=VMEM_LIMIT),
        name="gamma_rows",
    )(*[blocks[q] for q in names], mine, theirs, scales)


def body(three_index, *energies):
    up, down = ring(NPAIR, 1), ring(NPAIR, -1)
    swap = ring(NCORE, 1)

    block = {0: three_index}
    block[-1] = lax.ppermute(block[0], "pair", up)
    block[1] = lax.ppermute(block[0], "pair", down)
    denominator, scales = tables(*energies)
    block[-1], denominator, scales = lax.optimization_barrier((block[-1], denominator, scales))
    block[-2] = lax.ppermute(block[-1], "pair", up)
    block[2] = lax.ppermute(block[1], "pair", down)

    early, other_early = coulomb_pairs(block, EARLY)
    got_early = lax.ppermute(other_early, "core", swap)
    late, other_late = coulomb_pairs(block, LATE)
    got_late = lax.ppermute(other_late, "core", swap)
    summed = sum_cores((early, late), (got_early, got_late))

    summed, block[-2] = lax.optimization_barrier((summed, block[-2]))
    block[-3] = lax.ppermute(block[-2], "pair", up)
    pieces = lax.all_to_all(summed, ("x", "z"), 0, 0)
    pieces, block[-3] = lax.optimization_barrier((pieces, block[-3]))

    kept, send_up, send_down, send_far = amplitude_pieces(pieces, denominator)
    lower2 = lax.ppermute(send_far, "pair", ring(NPAIR, 2))
    lower1 = lax.ppermute(send_up, "pair", up)
    upper1 = lax.ppermute(send_down, "pair", down)
    copies = spread(kept, lower1, upper1, lower2)

    copies, block[-3], block[2] = lax.optimization_barrier((copies, block[-3], block[2]))
    block[4] = lax.ppermute(block[-3], "pair", up)
    block[3] = lax.ppermute(block[2], "pair", down)
    mine = lax.all_to_all(copies, ("x", "z"), 0, 0)
    mine, block[3], block[4] = lax.optimization_barrier((mine, block[3], block[4]))
    theirs = lax.ppermute(mine, "core", swap)
    return gamma_rows(block, mine, theirs, scales)


def solution(mesh):
    grid = Mesh(mesh.devices.reshape(NX, NZ, NCORE, NPAIR), AUX + ("pair",))
    placed = (P(AUX, "pair"), P(), P(), P(), P(), P())
    return jax.shard_map(
        body, mesh=grid, in_specs=placed, out_specs=P(AUX, "pair"), check_vma=False
    )
```

```python
import jax
import jax.numpy as jnp
from jax import lax
from jax.experimental import pallas as pl
from jax.experimental.pallas import tpu as pltpu
from jax.sharding import Mesh, PartitionSpec as P

TS = 128
VT = 157
NT = 16
NX, NZ, NCORE, NPAIR = 4, 8, 2, 8
NXZ = NX * NZ
AUX = ("x", "z", "core")
EARLY = ((0, 0), (0, 1), (-1, 1))
LATE = ((-1, 2), (-2, 2))
PAIRS = EARLY + LATE
WIDTH = 2 * TS
PIECE = WIDTH // NXZ
ORDER = (
    (0, False),
    (1, True),
    (-1, False),
    (-2, False),
    (2, True),
    (3, True),
    (-3, False),
    (4, False),
)
ROWS = 224
VMEM_LIMIT = 12 * 1024 * 1024
bf16, f32 = jnp.bfloat16, jnp.float32
in_vmem = pl.BlockSpec(memory_space=pltpu.VMEM)
in_smem = pl.BlockSpec(memory_space=pltpu.SMEM)


def ring(size, step):
    return [(i, (i + step) % size) for i in range(size)]


def tables(occupied_energy, virtual_energy, tile_occupied, tile_virtual, tile_exponent):
    def kernel(occupied, virtual, occupied_of, virtual_of, exponent, denominator, scales):
        me = lax.axis_index("pair")
        core = lax.axis_index("core")
        slot = lax.axis_index("x") * NZ + lax.axis_index("z")
        half, first = slot // (NXZ // 2), (slot % (NXZ // 2)) * PIECE

        def tile_of(relative, part):
            return lax.rem(2 * (me + relative + NPAIR) + part, NT)

        def energy(tile):
            return virtual[pl.ds(virtual_of[tile], 1)] - occupied[occupied_of[tile]]

        def scale(tile):
            level = exponent[tile]
            return jnp.where(level == -1, 0.5, jnp.where(level == 1, 2.0, 1.0)).astype(f32)

        lane = lax.broadcasted_iota(jnp.int32, (PIECE, TS), 1)
        chosen = lane == first + lax.broadcasted_iota(jnp.int32, (PIECE, TS), 0)
        for k, (r, c) in enumerate(PAIRS):
            row, column = tile_of(r, core), tile_of(c, half)
            of_row = jnp.sum(jnp.where(chosen, energy(row), 0.0), axis=1, keepdims=True)
            level = jnp.full((PIECE, TS), scale(row) * scale(column), f32)
            denominator[k * PIECE : (k + 1) * PIECE] = (of_row + energy(column)) / level
        for i, (q, _) in enumerate(ORDER):
            for part in (0, 1):
                n = 2 * i + part
                scales[n : n + 1] = jnp.full((1, TS), scale(tile_of(q, part)), f32)

    return pl.pallas_call(
        kernel,
        out_shape=(
            jax.ShapeDtypeStruct((len(PAIRS) * PIECE, TS), f32),
            jax.ShapeDtypeStruct((2 * len(ORDER), TS), f32),
        ),
        in_specs=[in_smem, in_vmem, in_smem, in_smem, in_smem],
        out_specs=(in_vmem, in_vmem),
        compiler_params=pltpu.CompilerParams(vmem_limit_bytes=VMEM_LIMIT),
        name="tables",
    )(occupied_energy, virtual_energy.reshape(VT, TS), tile_occupied, tile_virtual, tile_exponent)


def coulomb_pairs(blocks, pairs):
    names = sorted({d for pair in pairs for d in pair})

    def kernel(*refs):
        block = dict(zip(names, refs))
        own, other = refs[len(names) :]
        core = lax.axis_index("core")
        for k, (r, c) in enumerate(pairs):
            for out, part in ((own, core), (other, 1 - core)):
                left = block[r][:, pl.ds(pl.multiple_of(part * TS, TS), TS)]
                product = lax.dot_general(
                    left, block[c][...], (((0,), (0,)), ((), ())), preferred_element_type=f32
                )
                for h in (0, 1):
                    out[k, h] = product[:, h * TS : (h + 1) * TS].astype(out.dtype)

    shape = (len(pairs), 2, TS, TS)
    return pl.pallas_call(
        kernel,
        out_shape=(jax.ShapeDtypeStruct(shape, f32), jax.ShapeDtypeStruct(shape, bf16)),
        in_specs=[in_vmem] * len(names),
        out_specs=(in_vmem, in_vmem),
        compiler_params=pltpu.CompilerParams(vmem_limit_bytes=VMEM_LIMIT),
        name="coulomb_pairs",
    )(*[blocks[d] for d in names])


def sum_cores(own, received):
    pairs = sum(a.shape[0] for a in own)

    def kernel(*refs):
        parts = []
        for mine, theirs in zip(refs[: len(own)], refs[len(own) : -1]):
            count = mine.shape[0]
            total = (mine[...] + theirs[...].astype(f32)).reshape(count, NXZ, PIECE, TS)
            parts += [total[k] for k in range(count)]
        refs[-1][...] = jnp.concatenate(parts, axis=1).astype(bf16)

    return pl.pallas_call(
        kernel,
        out_shape=jax.ShapeDtypeStruct((NXZ, pairs * PIECE, TS), bf16),
        in_specs=[in_vmem] * (2 * len(own)),
        out_specs=in_vmem,
        compiler_params=pltpu.CompilerParams(vmem_limit_bytes=VMEM_LIMIT),
        name="sum_cores",
    )(*own, *received)


def amplitude_pieces(pieces, denominator):
    def kernel(pieces_ref, denominator_ref, *outs):
        total = jnp.sum(pieces_ref[...].astype(f32), axis=0) / denominator_ref[...]
        for k, out in enumerate(outs):
            out[...] = total[k * PIECE : (k + 2) * PIECE].astype(bf16)

    shape = jax.ShapeDtypeStruct((2 * PIECE, TS), bf16)
    return pl.pallas_call(
        kernel,
        out_shape=(shape,) * 4,
        in_specs=[in_vmem] * 2,
        out_specs=(in_vmem,) * 4,
        compiler_params=pltpu.CompilerParams(vmem_limit_bytes=VMEM_LIMIT),
        name="amplitude_pieces",
    )(pieces, denominator)


def spread(*pieces):
    rows = len(pieces) * 2 * PIECE

    def kernel(*refs):
        whole = jnp.concatenate([ref[...] for ref in refs[:-1]])
        refs[-1][...] = jnp.broadcast_to(whole[None], (NXZ, rows, TS))

    return pl.pallas_call(
        kernel,
        out_shape=jax.ShapeDtypeStruct((NXZ, rows, TS), bf16),
        in_specs=[in_vmem] * len(pieces),
        out_specs=in_vmem,
        compiler_params=pltpu.CompilerParams(vmem_limit_bytes=VMEM_LIMIT),
        name="spread",
    )(*pieces)


def gamma_rows(blocks, mine, theirs, scales):
    rows, width = blocks[0].shape
    names = [q for q, _ in ORDER]

    def kernel(*refs):
        block = dict(zip(names, refs))
        own, other, scale, out, matrix = refs[len(names) :]
        core = lax.axis_index("core")
        for pair in range(0, len(ORDER), 2):
            for part, source in ((core, own), (1 - core, other)):
                place = pl.ds(pl.multiple_of(part * TS, TS), TS)
                both = source[:, pair * PIECE : (pair + 2) * PIECE].astype(f32)
                for k in (0, 1):
                    i = pair + k
                    tiles = both[:, k * PIECE : (k + 1) * PIECE].reshape(2, TS, TS)
                    for h in (0, 1):
                        if ORDER[i][1]:
                            tile = tiles[h].T * scale[2 * i + h : 2 * i + h + 1]
                            matrix[i, h * TS : (h + 1) * TS, place] = tile.astype(bf16)
                        else:
                            tile = tiles[h] * scale[pl.ds(2 * i + part, 1)]
                            matrix[i, place, h * TS : (h + 1) * TS] = tile.astype(bf16)

        for start in range(0, rows, ROWS):
            total = None
            for i, (q, *_) in enumerate(ORDER):
                left = block[q][start : start + ROWS]
                term = jnp.dot(left, matrix[i], preferred_element_type=f32)
                total = term if total is None else total + term
            out[start : start + ROWS] = total.astype(bf16)

    return pl.pallas_call(
        kernel,
        out_shape=jax.ShapeDtypeStruct((rows, width), bf16),
        in_specs=[in_vmem] * (len(names) + 3),
        out_specs=in_vmem,
        scratch_shapes=[pltpu.VMEM((len(ORDER), WIDTH, WIDTH), bf16)],
        compiler_params=pltpu.CompilerParams(vmem_limit_bytes=VMEM_LIMIT),
        name="gamma_rows",
    )(*[blocks[q] for q in names], mine, theirs, scales)


def body(three_index, *energies):
    up, down = ring(NPAIR, 1), ring(NPAIR, -1)
    swap = ring(NCORE, 1)

    block = {0: three_index}
    block[-1] = lax.ppermute(block[0], "pair", up)
    block[1] = lax.ppermute(block[0], "pair", down)
    denominator, scales = tables(*energies)
    block[-1], denominator, scales = lax.optimization_barrier((block[-1], denominator, scales))
    block[-2] = lax.ppermute(block[-1], "pair", up)
    block[2] = lax.ppermute(block[1], "pair", down)

    early, other_early = coulomb_pairs(block, EARLY)
    got_early = lax.ppermute(other_early, "core", swap)
    late, other_late = coulomb_pairs(block, LATE)
    got_late = lax.ppermute(other_late, "core", swap)
    summed = sum_cores((early, late), (got_early, got_late))

    summed, block[-2], block[2] = lax.optimization_barrier((summed, block[-2], block[2]))
    block[-3] = lax.ppermute(block[-2], "pair", up)
    block[3] = lax.ppermute(block[2], "pair", down)
    pieces = lax.all_to_all(summed, ("x", "z"), 0, 0)
    pieces, block[-3] = lax.optimization_barrier((pieces, block[-3]))

    kept, send_up, send_down, send_far = amplitude_pieces(pieces, denominator)
    block[4] = lax.ppermute(block[-3], "pair", up)
    lower2 = lax.ppermute(send_far, "pair", ring(NPAIR, 2))
    lower1 = lax.ppermute(send_up, "pair", up)
    upper1 = lax.ppermute(send_down, "pair", down)
    copies = spread(kept, lower1, upper1, lower2)
    copies, block[3], block[4] = lax.optimization_barrier((copies, block[3], block[4]))
    mine = lax.all_to_all(copies, ("x", "z"), 0, 0)
    theirs = lax.ppermute(mine, "core", swap)
    return gamma_rows(block, mine, theirs, scales)


def solution(mesh):
    grid = Mesh(mesh.devices.reshape(NX, NZ, NCORE, NPAIR), AUX + ("pair",))
    placed = (P(AUX, "pair"), P(), P(), P(), P(), P())
    return jax.shard_map(
        body, mesh=grid, in_specs=placed, out_specs=P(AUX, "pair"), check_vma=False
    )
```

```python
import jax
import jax.numpy as jnp
from jax import lax
from jax.experimental import pallas as pl
from jax.experimental.pallas import tpu as pltpu
from jax.sharding import Mesh, PartitionSpec as P

TS = 128
VT = 157
NT = 16
NX, NZ, NCORE, NPAIR = 4, 8, 2, 8
NXZ = NX * NZ
AUX = ("x", "z", "core")
EARLY = ((0, 0), (0, 1), (-1, 1))
LATE = ((-1, 2), (-2, 2))
PAIRS = EARLY + LATE
WIDTH = 2 * TS
PIECE = WIDTH // NXZ
SENDS = ((0, (0, 1)), (1, (1, 2)), (-1, (2, 3)), (2, (3, 4)))
GETS = tuple((PAIRS[k][0] - d, PAIRS[k][1] - d) for d, pairs in SENDS for k in pairs)
ORDER = tuple((r, False) if c == 0 else (c, True) for r, c in GETS)
ROWS = 224
VMEM_LIMIT = 12 * 1024 * 1024
bf16, f32 = jnp.bfloat16, jnp.float32
in_vmem = pl.BlockSpec(memory_space=pltpu.VMEM)
in_smem = pl.BlockSpec(memory_space=pltpu.SMEM)


def ring(size, step):
    return [(i, (i + step) % size) for i in range(size)]


def tables(occupied_energy, virtual_energy, tile_occupied, tile_virtual, tile_exponent):
    def kernel(occupied, virtual, occupied_of, virtual_of, exponent, denominator, scales):
        me = lax.axis_index("pair")
        core = lax.axis_index("core")
        slot = lax.axis_index("z") * NX + lax.axis_index("x")
        half, first = slot // (NXZ // 2), (slot % (NXZ // 2)) * PIECE

        def tile_of(relative, part):
            return lax.rem(2 * (me + relative + NPAIR) + part, NT)

        def energy(tile):
            return virtual[pl.ds(virtual_of[tile], 1)] - occupied[occupied_of[tile]]

        def scale(tile):
            level = exponent[tile]
            return jnp.where(level == -1, 0.5, jnp.where(level == 1, 2.0, 1.0)).astype(f32)

        lane = lax.broadcasted_iota(jnp.int32, (PIECE, TS), 1)
        chosen = lane == first + lax.broadcasted_iota(jnp.int32, (PIECE, TS), 0)
        for k, (r, c) in enumerate(GETS):
            row, column = tile_of(r, core), tile_of(c, half)
            of_row = jnp.sum(jnp.where(chosen, energy(row), 0.0), axis=1, keepdims=True)
            level = jnp.full((PIECE, TS), scale(row) * scale(column), f32)
            denominator[k * PIECE : (k + 1) * PIECE] = (of_row + energy(column)) / level
        for i, (q, _) in enumerate(ORDER):
            for part in (0, 1):
                n = 2 * i + part
                scales[n : n + 1] = jnp.full((1, TS), scale(tile_of(q, part)), f32)

    return pl.pallas_call(
        kernel,
        out_shape=(
            jax.ShapeDtypeStruct((len(GETS) * PIECE, TS), f32),
            jax.ShapeDtypeStruct((2 * len(ORDER), TS), f32),
        ),
        in_specs=[in_smem, in_vmem, in_smem, in_smem, in_smem],
        out_specs=(in_vmem, in_vmem),
        compiler_params=pltpu.CompilerParams(vmem_limit_bytes=VMEM_LIMIT),
        name="tables",
    )(occupied_energy, virtual_energy.reshape(VT, TS), tile_occupied, tile_virtual, tile_exponent)


def coulomb_pairs(blocks, pairs):
    names = sorted({d for pair in pairs for d in pair})

    def kernel(*refs):
        block = dict(zip(names, refs))
        own, other = refs[len(names) :]
        core = lax.axis_index("core")
        for k, (r, c) in enumerate(pairs):
            for out, part in ((own, core), (other, 1 - core)):
                left = block[r][:, pl.ds(pl.multiple_of(part * TS, TS), TS)]
                product = lax.dot_general(
                    left, block[c][...], (((0,), (0,)), ((), ())), preferred_element_type=f32
                )
                for h in (0, 1):
                    out[k, h] = product[:, h * TS : (h + 1) * TS].astype(out.dtype)

    shape = (len(pairs), 2, TS, TS)
    return pl.pallas_call(
        kernel,
        out_shape=(jax.ShapeDtypeStruct(shape, f32), jax.ShapeDtypeStruct(shape, bf16)),
        in_specs=[in_vmem] * len(names),
        out_specs=(in_vmem, in_vmem),
        compiler_params=pltpu.CompilerParams(vmem_limit_bytes=VMEM_LIMIT),
        name="coulomb_pairs",
    )(*[blocks[d] for d in names])


def sum_cores(own, received):
    pairs = sum(a.shape[0] for a in own)
    rows = WIDTH // NZ

    def kernel(*refs):
        out = refs[-1]
        n = 0
        for mine, theirs in zip(refs[: len(own)], refs[len(own) : -1]):
            count = mine.shape[0]
            total = (mine[...] + theirs[...].astype(f32)).astype(bf16).reshape(count, NZ, rows, TS)
            for k in range(count):
                out[:, (n + k) * rows : (n + k + 1) * rows] = total[k]
            n += count

    return pl.pallas_call(
        kernel,
        out_shape=jax.ShapeDtypeStruct((NZ, pairs * rows, TS), bf16),
        in_specs=[in_vmem] * (2 * len(own)),
        out_specs=in_vmem,
        compiler_params=pltpu.CompilerParams(vmem_limit_bytes=VMEM_LIMIT),
        name="sum_cores",
    )(*own, *received)


def sum_z(parts):
    def kernel(parts_ref, out):
        me = lax.axis_index("pair")
        total = jnp.sum(parts_ref[...].astype(f32), axis=0).reshape(len(PAIRS), NX, PIECE, TS)
        out[...] = jnp.zeros_like(out)
        for d, (first, second) in SENDS:
            both = jnp.concatenate([total[first], total[second]], axis=1)
            out[pl.ds(NX * lax.rem(me + d + NPAIR, NPAIR), NX)] = both.astype(bf16)

    return pl.pallas_call(
        kernel,
        out_shape=jax.ShapeDtypeStruct((NPAIR * NX, 2 * PIECE, TS), bf16),
        in_specs=[in_vmem],
        out_specs=in_vmem,
        compiler_params=pltpu.CompilerParams(vmem_limit_bytes=VMEM_LIMIT),
        name="sum_z",
    )(parts)


def amplitude_copies(parts, denominator):
    rows = len(GETS) * PIECE

    def kernel(parts_ref, denominator_ref, out):
        me = lax.axis_index("pair")
        total = jnp.concatenate(
            [
                jnp.sum(parts_ref[pl.ds(NX * lax.rem(me - d + NPAIR, NPAIR), NX)].astype(f32), axis=0)
                for d, _ in SENDS
            ]
        )
        amplitude = (total / denominator_ref[...]).astype(bf16)
        out[...] = jnp.broadcast_to(amplitude[None], out.shape)

    return pl.pallas_call(
        kernel,
        out_shape=jax.ShapeDtypeStruct((NXZ, rows, TS), bf16),
        in_specs=[in_vmem] * 2,
        out_specs=in_vmem,
        compiler_params=pltpu.CompilerParams(vmem_limit_bytes=VMEM_LIMIT),
        name="amplitude_copies",
    )(parts, denominator)


def gamma_rows(blocks, last, mine, theirs, scales):
    rows, width = blocks[0].shape
    names = [q for q, _ in ORDER[:-1]]

    def kernel(*refs):
        block = dict(zip(names, refs))
        n = len(names)
        own, other, scale, out, matrix = refs[n + len(last) :]
        core = lax.axis_index("core")
        for pair in range(0, len(ORDER), 2):
            for part, source in ((core, own), (1 - core, other)):
                place = pl.ds(pl.multiple_of(part * TS, TS), TS)
                both = source[:, pair * PIECE : (pair + 2) * PIECE].astype(f32)
                for k in (0, 1):
                    i = pair + k
                    tiles = both[:, k * PIECE : (k + 1) * PIECE].reshape(2, TS, TS)
                    for h in (0, 1):
                        if ORDER[i][1]:
                            tile = tiles[h].T * scale[2 * i + h : 2 * i + h + 1]
                            matrix[i, h * TS : (h + 1) * TS, place] = tile.astype(bf16)
                        else:
                            tile = tiles[h] * scale[pl.ds(2 * i + part, 1)]
                            matrix[i, place, h * TS : (h + 1) * TS] = tile.astype(bf16)

        height = rows // len(last)
        for start in range(0, rows, ROWS):
            part, offset = divmod(start, height)
            total = jnp.dot(
                refs[n + part][offset : offset + ROWS], matrix[n], preferred_element_type=f32
            )
            for i, q in enumerate(names):
                total += jnp.dot(block[q][start : start + ROWS], matrix[i], preferred_element_type=f32)
            out[start : start + ROWS] = total.astype(bf16)

    return pl.pallas_call(
        kernel,
        out_shape=jax.ShapeDtypeStruct((rows, width), bf16),
        in_specs=[in_vmem] * (len(names) + len(last) + 3),
        out_specs=in_vmem,
        scratch_shapes=[pltpu.VMEM((len(ORDER), WIDTH, WIDTH), bf16)],
        compiler_params=pltpu.CompilerParams(vmem_limit_bytes=VMEM_LIMIT),
        name="gamma_rows",
    )(*[blocks[q] for q in names], *last, mine, theirs, scales)


def body(three_index, *energies):
    up, down = ring(NPAIR, 1), ring(NPAIR, -1)
    swap = ring(NCORE, 1)

    block = {0: three_index}
    block[-1] = lax.ppermute(block[0], "pair", up)
    block[1] = lax.ppermute(block[0], "pair", down)
    denominator, scales = tables(*energies)
    block[-1], denominator, scales = lax.optimization_barrier((block[-1], denominator, scales))
    block[-2] = lax.ppermute(block[-1], "pair", up)
    block[2] = lax.ppermute(block[1], "pair", down)

    early, other_early = coulomb_pairs(block, EARLY)
    got_early = lax.ppermute(other_early, "core", swap)
    late, other_late = coulomb_pairs(block, LATE)
    got_late = lax.ppermute(other_late, "core", swap)
    summed = sum_cores((early, late), (got_early, got_late))

    summed, block[-2], block[2] = lax.optimization_barrier((summed, block[-2], block[2]))
    block[-3] = lax.ppermute(block[-2], "pair", up)
    block[3] = lax.ppermute(block[2], "pair", down)
    parts = lax.all_to_all(summed, "z", 0, 0)
    parts = lax.all_to_all(sum_z(parts), ("pair", "x"), 0, 0)
    copies = amplitude_copies(parts, denominator)

    copies, block[-3], block[3] = lax.optimization_barrier((copies, block[-3], block[3]))
    last = (lax.ppermute(block[-3], "pair", up),)
    mine = lax.all_to_all(copies, ("z", "x"), 0, 0)
    mine, last = lax.optimization_barrier((mine, last))
    theirs = lax.ppermute(mine, "core", swap)
    return gamma_rows(block, last, mine, theirs, scales)


def solution(mesh):
    grid = Mesh(mesh.devices.reshape(NX, NZ, NCORE, NPAIR), AUX + ("pair",))
    placed = (P(AUX, "pair"), P(), P(), P(), P(), P())
    return jax.shard_map(
        body, mesh=grid, in_specs=placed, out_specs=P(AUX, "pair"), check_vma=False
    )
```

```python
import jax
import jax.numpy as jnp
from jax import lax
from jax.experimental import pallas as pl
from jax.experimental.pallas import tpu as pltpu
from jax.sharding import Mesh, PartitionSpec as P

TS = 128
VT = 157
NT = 16
NX, NZ, NCORE, NPAIR = 4, 8, 2, 8
NXZ = NX * NZ
AUX = ("x", "z", "core")
EARLY = ((0, 0), (0, 1), (-1, 1))
LATE = ((-1, 2), (-2, 2))
PAIRS = EARLY + LATE
WIDTH = 2 * TS
PIECE = WIDTH // NXZ
SENDS = ((0, (0, 1)), (1, (1, 2)), (-1, (2, 3)), (2, (3, 4)))
GETS = tuple((PAIRS[k][0] - d, PAIRS[k][1] - d) for d, pairs in SENDS for k in pairs)
ORDER = tuple((r, False) if c == 0 else (c, True) for r, c in GETS)
ROWS = 224
VMEM_LIMIT = 12 * 1024 * 1024
bf16, f32 = jnp.bfloat16, jnp.float32
in_vmem = pl.BlockSpec(memory_space=pltpu.VMEM)
in_smem = pl.BlockSpec(memory_space=pltpu.SMEM)


def ring(size, step):
    return [(i, (i + step) % size) for i in range(size)]


def tables(occupied_energy, virtual_energy, tile_occupied, tile_virtual, tile_exponent):
    def kernel(occupied, virtual, occupied_of, virtual_of, exponent, denominator, scales):
        me = lax.axis_index("pair")
        core = lax.axis_index("core")
        slot = lax.axis_index("z") * NX + lax.axis_index("x")
        half, first = slot // (NXZ // 2), (slot % (NXZ // 2)) * PIECE

        def tile_of(relative, part):
            return lax.rem(2 * (me + relative + NPAIR) + part, NT)

        def energy(tile):
            return virtual[pl.ds(virtual_of[tile], 1)] - occupied[occupied_of[tile]]

        def scale(tile):
            level = exponent[tile]
            return jnp.where(level == -1, 0.5, jnp.where(level == 1, 2.0, 1.0)).astype(f32)

        lane = lax.broadcasted_iota(jnp.int32, (PIECE, TS), 1)
        chosen = lane == first + lax.broadcasted_iota(jnp.int32, (PIECE, TS), 0)
        for k, (r, c) in enumerate(GETS):
            row, column = tile_of(r, core), tile_of(c, half)
            of_row = jnp.sum(jnp.where(chosen, energy(row), 0.0), axis=1, keepdims=True)
            level = jnp.full((PIECE, TS), scale(row) * scale(column), f32)
            denominator[k * PIECE : (k + 1) * PIECE] = (of_row + energy(column)) / level
        for i, (q, _) in enumerate(ORDER):
            for part in (0, 1):
                n = 2 * i + part
                scales[n : n + 1] = jnp.full((1, TS), scale(tile_of(q, part)), f32)

    return pl.pallas_call(
        kernel,
        out_shape=(
            jax.ShapeDtypeStruct((len(GETS) * PIECE, TS), f32),
            jax.ShapeDtypeStruct((2 * len(ORDER), TS), f32),
        ),
        in_specs=[in_smem, in_vmem, in_smem, in_smem, in_smem],
        out_specs=(in_vmem, in_vmem),
        compiler_params=pltpu.CompilerParams(vmem_limit_bytes=VMEM_LIMIT),
        name="tables",
    )(occupied_energy, virtual_energy.reshape(VT, TS), tile_occupied, tile_virtual, tile_exponent)


def coulomb_pairs(blocks, pairs):
    names = sorted({d for pair in pairs for d in pair})

    def kernel(*refs):
        block = dict(zip(names, refs))
        own, other = refs[len(names) :]
        core = lax.axis_index("core")
        for k, (r, c) in enumerate(pairs):
            for out, part in ((own, core), (other, 1 - core)):
                left = block[r][:, pl.ds(pl.multiple_of(part * TS, TS), TS)]
                product = lax.dot_general(
                    left, block[c][...], (((0,), (0,)), ((), ())), preferred_element_type=f32
                )
                for h in (0, 1):
                    out[k, h] = product[:, h * TS : (h + 1) * TS].astype(out.dtype)

    shape = (len(pairs), 2, TS, TS)
    return pl.pallas_call(
        kernel,
        out_shape=(jax.ShapeDtypeStruct(shape, f32), jax.ShapeDtypeStruct(shape, bf16)),
        in_specs=[in_vmem] * len(names),
        out_specs=(in_vmem, in_vmem),
        compiler_params=pltpu.CompilerParams(vmem_limit_bytes=VMEM_LIMIT),
        name="coulomb_pairs",
    )(*[blocks[d] for d in names])


def sum_cores(own, received):
    pairs = sum(a.shape[0] for a in own)
    rows = WIDTH // NZ

    def kernel(*refs):
        out = refs[-1]
        n = 0
        for mine, theirs in zip(refs[: len(own)], refs[len(own) : -1]):
            count = mine.shape[0]
            total = (mine[...] + theirs[...].astype(f32)).astype(bf16).reshape(count, NZ, rows, TS)
            for k in range(count):
                out[:, (n + k) * rows : (n + k + 1) * rows] = total[k]
            n += count

    return pl.pallas_call(
        kernel,
        out_shape=jax.ShapeDtypeStruct((NZ, pairs * rows, TS), bf16),
        in_specs=[in_vmem] * (2 * len(own)),
        out_specs=in_vmem,
        compiler_params=pltpu.CompilerParams(vmem_limit_bytes=VMEM_LIMIT),
        name="sum_cores",
    )(*own, *received)


def sum_z(parts):
    def kernel(parts_ref, out):
        me = lax.axis_index("pair")
        total = jnp.sum(parts_ref[...].astype(f32), axis=0).reshape(len(PAIRS), NX, PIECE, TS)
        out[...] = jnp.zeros_like(out)
        for d, (first, second) in SENDS:
            both = jnp.concatenate([total[first], total[second]], axis=1)
            out[pl.ds(NX * lax.rem(me + d + NPAIR, NPAIR), NX)] = both.astype(bf16)

    return pl.pallas_call(
        kernel,
        out_shape=jax.ShapeDtypeStruct((NPAIR * NX, 2 * PIECE, TS), bf16),
        in_specs=[in_vmem],
        out_specs=in_vmem,
        compiler_params=pltpu.CompilerParams(vmem_limit_bytes=VMEM_LIMIT),
        name="sum_z",
    )(parts)


def amplitude_copies(parts, denominator):
    rows = len(GETS) * PIECE

    def kernel(parts_ref, denominator_ref, out):
        me = lax.axis_index("pair")
        total = jnp.concatenate(
            [
                jnp.sum(parts_ref[pl.ds(NX * lax.rem(me - d + NPAIR, NPAIR), NX)].astype(f32), axis=0)
                for d, _ in SENDS
            ]
        )
        amplitude = (total / denominator_ref[...]).astype(bf16)
        out[...] = jnp.broadcast_to(amplitude[None], out.shape)

    return pl.pallas_call(
        kernel,
        out_shape=jax.ShapeDtypeStruct((NXZ, rows, TS), bf16),
        in_specs=[in_vmem] * 2,
        out_specs=in_vmem,
        compiler_params=pltpu.CompilerParams(vmem_limit_bytes=VMEM_LIMIT),
        name="amplitude_copies",
    )(parts, denominator)


def gamma_rows(blocks, mine, theirs, scales):
    rows, width = blocks[0].shape
    names = [q for q, _ in ORDER]

    def kernel(*refs):
        block = refs[: len(names)]
        own, other, scale, out, matrix = refs[len(names) :]
        core = lax.axis_index("core")
        for pair in range(0, len(ORDER), 2):
            for part, source in ((core, own), (1 - core, other)):
                place = pl.ds(pl.multiple_of(part * TS, TS), TS)
                both = source[:, pair * PIECE : (pair + 2) * PIECE].astype(f32)
                for k in (0, 1):
                    i = pair + k
                    tiles = both[:, k * PIECE : (k + 1) * PIECE].reshape(2, TS, TS)
                    for h in (0, 1):
                        if ORDER[i][1]:
                            tile = tiles[h].T * scale[2 * i + h : 2 * i + h + 1]
                            matrix[i, h * TS : (h + 1) * TS, place] = tile.astype(bf16)
                        else:
                            tile = tiles[h] * scale[pl.ds(2 * i + part, 1)]
                            matrix[i, place, h * TS : (h + 1) * TS] = tile.astype(bf16)

        for start in range(0, rows, ROWS):
            total = None
            for i, ref in enumerate(block):
                term = jnp.dot(ref[start : start + ROWS], matrix[i], preferred_element_type=f32)
                total = term if total is None else total + term
            out[start : start + ROWS] = total.astype(bf16)

    return pl.pallas_call(
        kernel,
        out_shape=jax.ShapeDtypeStruct((rows, width), bf16),
        in_specs=[in_vmem] * (len(names) + 3),
        out_specs=in_vmem,
        scratch_shapes=[pltpu.VMEM((len(ORDER), WIDTH, WIDTH), bf16)],
        compiler_params=pltpu.CompilerParams(vmem_limit_bytes=VMEM_LIMIT),
        name="gamma_rows",
    )(*[blocks[q] for q in names], mine, theirs, scales)


def body(three_index, *energies):
    up, down = ring(NPAIR, 1), ring(NPAIR, -1)
    swap = ring(NCORE, 1)

    block = {0: three_index}
    block[-1] = lax.ppermute(block[0], "pair", up)
    block[1] = lax.ppermute(block[0], "pair", down)
    denominator, scales = tables(*energies)
    block[-1], denominator, scales = lax.optimization_barrier((block[-1], denominator, scales))
    block[-2] = lax.ppermute(block[-1], "pair", up)
    block[2] = lax.ppermute(block[1], "pair", down)

    early, other_early = coulomb_pairs(block, EARLY)
    got_early = lax.ppermute(other_early, "core", swap)
    late, other_late = coulomb_pairs(block, LATE)
    got_late = lax.ppermute(other_late, "core", swap)
    summed = sum_cores((early, late), (got_early, got_late))

    summed, block[-2], block[2] = lax.optimization_barrier((summed, block[-2], block[2]))
    block[-3] = lax.ppermute(block[-2], "pair", up)
    block[3] = lax.ppermute(block[2], "pair", down)
    block[-4] = lax.ppermute(block[-2], "pair", ring(NPAIR, 2))
    parts = lax.all_to_all(summed, "z", 0, 0)
    parts = lax.all_to_all(sum_z(parts), ("pair", "x"), 0, 0)
    copies = amplitude_copies(parts, denominator)
    copies, block[-3], block[3], block[-4] = lax.optimization_barrier(
        (copies, block[-3], block[3], block[-4])
    )
    mine = lax.all_to_all(copies, ("z", "x"), 0, 0)
    theirs = lax.ppermute(mine, "core", swap)
    return gamma_rows(block, mine, theirs, scales)


def solution(mesh):
    grid = Mesh(mesh.devices.reshape(NX, NZ, NCORE, NPAIR), AUX + ("pair",))
    placed = (P(AUX, "pair"), P(), P(), P(), P(), P())
    return jax.shard_map(
        body, mesh=grid, in_specs=placed, out_specs=P(AUX, "pair"), check_vma=False
    )
```

```python
import jax
import jax.numpy as jnp
from jax import lax
from jax.experimental import pallas as pl
from jax.experimental.pallas import tpu as pltpu
from jax.sharding import Mesh, PartitionSpec as P

TS = 128
VT = 157
NT = 16
NX, NZ, NCORE, NPAIR = 4, 8, 2, 8
NXZ = NX * NZ
AUX = ("x", "z", "core")
EARLY = ((0, 0), (0, 1), (-1, 1))
LATE = ((-1, 2), (-2, 2))
PAIRS = EARLY + LATE
WIDTH = 2 * TS
PIECE = WIDTH // NXZ
SENDS = ((0, (0, 1)), (1, (1, 2)), (-1, (2, 3)), (2, (3, 4)))
GETS = tuple((PAIRS[k][0] - d, PAIRS[k][1] - d) for d, pairs in SENDS for k in pairs)
ORDER = tuple((r, False) if c == 0 else (c, True) for r, c in GETS)
ROWS = 224
VMEM_LIMIT = 12 * 1024 * 1024
bf16, f32 = jnp.bfloat16, jnp.float32
in_vmem = pl.BlockSpec(memory_space=pltpu.VMEM)
in_smem = pl.BlockSpec(memory_space=pltpu.SMEM)


SWAP_A = [(i, i ^ 1) for i in range(NPAIR)]
SWAP_B = [(i, (i + (-1 if i % 2 == 0 else 1)) % NPAIR) for i in range(NPAIR)]
SWAP_CORES = [(0, 1), (1, 0)]
HELD = (0, ("A", 1), ("B", 1), ("A", 2), ("B", 2), ("A", 3), ("B", 3), ("B", 4))


def held_name(relative, parity):
    if relative == 0:
        return 0
    if abs(relative) == 4:
        return ("B", 4)
    return ("A" if (relative > 0) == (parity == 0) else "B", abs(relative))


def tables(occupied_energy, virtual_energy, tile_occupied, tile_virtual, tile_exponent):
    def kernel(occupied, virtual, occupied_of, virtual_of, exponent, denominator, scales):
        me = lax.axis_index("pair")
        core = lax.axis_index("core")
        slot = lax.axis_index("z") * NX + lax.axis_index("x")
        half, first = slot // (NXZ // 2), (slot % (NXZ // 2)) * PIECE

        def tile_of(relative, part):
            return lax.rem(2 * (me + relative + NPAIR) + part, NT)

        def energy(tile):
            return virtual[pl.ds(virtual_of[tile], 1)] - occupied[occupied_of[tile]]

        def scale(tile):
            level = exponent[tile]
            return jnp.where(level == -1, 0.5, jnp.where(level == 1, 2.0, 1.0)).astype(f32)

        lane = lax.broadcasted_iota(jnp.int32, (PIECE, TS), 1)
        chosen = lane == first + lax.broadcasted_iota(jnp.int32, (PIECE, TS), 0)
        for k, (r, c) in enumerate(GETS):
            row, column = tile_of(r, core), tile_of(c, half)
            of_row = jnp.sum(jnp.where(chosen, energy(row), 0.0), axis=1, keepdims=True)
            level = jnp.full((PIECE, TS), scale(row) * scale(column), f32)
            denominator[k * PIECE : (k + 1) * PIECE] = (of_row + energy(column)) / level
        for i, (q, _) in enumerate(ORDER):
            for part in (0, 1):
                n = 2 * i + part
                scales[n : n + 1] = jnp.full((1, TS), scale(tile_of(q, part)), f32)

    return pl.pallas_call(
        kernel,
        out_shape=(
            jax.ShapeDtypeStruct((len(GETS) * PIECE, TS), f32),
            jax.ShapeDtypeStruct((2 * len(ORDER), TS), f32),
        ),
        in_specs=[in_smem, in_vmem, in_smem, in_smem, in_smem],
        out_specs=(in_vmem, in_vmem),
        compiler_params=pltpu.CompilerParams(vmem_limit_bytes=VMEM_LIMIT),
        name="tables",
    )(occupied_energy, virtual_energy.reshape(VT, TS), tile_occupied, tile_virtual, tile_exponent)


def coulomb_pairs(blocks, pairs):
    names = [
        n for n in HELD if n in {held_name(d, parity) for pair in pairs for d in pair for parity in (0, 1)}
    ]

    def kernel(*refs):
        block = dict(zip(names, refs))
        own, other = refs[len(names) :]
        core = lax.axis_index("core")
        me = lax.axis_index("pair")
        for parity in (0, 1):

            @pl.when(lax.rem(me, 2) == parity)
            def _(parity=parity):
                for k, (r, c) in enumerate(pairs):
                    rows, columns = block[held_name(r, parity)], block[held_name(c, parity)]
                    for out, part in ((own, core), (other, 1 - core)):
                        left = rows[:, pl.ds(pl.multiple_of(part * TS, TS), TS)]
                        product = lax.dot_general(
                            left, columns[...], (((0,), (0,)), ((), ())), preferred_element_type=f32
                        )
                        for h in (0, 1):
                            out[k, h] = product[:, h * TS : (h + 1) * TS].astype(out.dtype)

    shape = (len(pairs), 2, TS, TS)
    return pl.pallas_call(
        kernel,
        out_shape=(jax.ShapeDtypeStruct(shape, f32), jax.ShapeDtypeStruct(shape, bf16)),
        in_specs=[in_vmem] * len(names),
        out_specs=(in_vmem, in_vmem),
        compiler_params=pltpu.CompilerParams(vmem_limit_bytes=VMEM_LIMIT),
        name="coulomb_pairs",
    )(*[blocks[n] for n in names])


def sum_cores(own, received):
    pairs = sum(a.shape[0] for a in own)
    rows = WIDTH // NZ

    def kernel(*refs):
        out = refs[-1]
        n = 0
        for mine, theirs in zip(refs[: len(own)], refs[len(own) : -1]):
            count = mine.shape[0]
            total = (mine[...] + theirs[...].astype(f32)).astype(bf16).reshape(count, NZ, rows, TS)
            for k in range(count):
                out[:, (n + k) * rows : (n + k + 1) * rows] = total[k]
            n += count

    return pl.pallas_call(
        kernel,
        out_shape=jax.ShapeDtypeStruct((NZ, pairs * rows, TS), bf16),
        in_specs=[in_vmem] * (2 * len(own)),
        out_specs=in_vmem,
        compiler_params=pltpu.CompilerParams(vmem_limit_bytes=VMEM_LIMIT),
        name="sum_cores",
    )(*own, *received)


def sum_z(parts):
    def kernel(parts_ref, out):
        me = lax.axis_index("pair")
        total = jnp.sum(parts_ref[...].astype(f32), axis=0).reshape(len(PAIRS), NX, PIECE, TS)
        out[...] = jnp.zeros_like(out)
        for d, (first, second) in SENDS:
            both = jnp.concatenate([total[first], total[second]], axis=1)
            out[pl.ds(NX * lax.rem(me + d + NPAIR, NPAIR), NX)] = both.astype(bf16)

    return pl.pallas_call(
        kernel,
        out_shape=jax.ShapeDtypeStruct((NPAIR * NX, 2 * PIECE, TS), bf16),
        in_specs=[in_vmem],
        out_specs=in_vmem,
        compiler_params=pltpu.CompilerParams(vmem_limit_bytes=VMEM_LIMIT),
        name="sum_z",
    )(parts)


def amplitude_copies(parts, denominator):
    rows = len(GETS) * PIECE

    def kernel(parts_ref, denominator_ref, out):
        me = lax.axis_index("pair")
        total = jnp.concatenate(
            [
                jnp.sum(parts_ref[pl.ds(NX * lax.rem(me - d + NPAIR, NPAIR), NX)].astype(f32), axis=0)
                for d, _ in SENDS
            ]
        )
        amplitude = (total / denominator_ref[...]).astype(bf16)
        out[...] = jnp.broadcast_to(amplitude[None], out.shape)

    return pl.pallas_call(
        kernel,
        out_shape=jax.ShapeDtypeStruct((NXZ, rows, TS), bf16),
        in_specs=[in_vmem] * 2,
        out_specs=in_vmem,
        compiler_params=pltpu.CompilerParams(vmem_limit_bytes=VMEM_LIMIT),
        name="amplitude_copies",
    )(parts, denominator)


def gamma_rows(blocks, mine, theirs, scales):
    rows, width = blocks[0].shape

    def kernel(*refs):
        block = refs[: len(HELD)]
        own, other, scale, out, matrix = refs[len(HELD) :]
        core = lax.axis_index("core")
        even = lax.rem(lax.axis_index("pair"), 2) == 0
        for pair in range(0, len(ORDER), 2):
            for part, source in ((core, own), (1 - core, other)):
                place = pl.ds(pl.multiple_of(part * TS, TS), TS)
                both = source[:, pair * PIECE : (pair + 2) * PIECE].astype(f32)
                for k in (0, 1):
                    i = pair + k
                    q, transposed = ORDER[i]
                    held = jnp.where(even, HELD.index(held_name(q, 0)), HELD.index(held_name(q, 1)))
                    tiles = both[:, k * PIECE : (k + 1) * PIECE].reshape(2, TS, TS)
                    for h in (0, 1):
                        if transposed:
                            tile = tiles[h].T * scale[2 * i + h : 2 * i + h + 1]
                            matrix[held, h * TS : (h + 1) * TS, place] = tile.astype(bf16)
                        else:
                            tile = tiles[h] * scale[pl.ds(2 * i + part, 1)]
                            matrix[held, place, h * TS : (h + 1) * TS] = tile.astype(bf16)

        for start in range(0, rows, ROWS):
            total = None
            for i, ref in enumerate(block):
                term = jnp.dot(ref[start : start + ROWS], matrix[i], preferred_element_type=f32)
                total = term if total is None else total + term
            out[start : start + ROWS] = total.astype(bf16)

    return pl.pallas_call(
        kernel,
        out_shape=jax.ShapeDtypeStruct((rows, width), bf16),
        in_specs=[in_vmem] * (len(HELD) + 3),
        out_specs=in_vmem,
        scratch_shapes=[pltpu.VMEM((len(HELD), WIDTH, WIDTH), bf16)],
        compiler_params=pltpu.CompilerParams(vmem_limit_bytes=VMEM_LIMIT),
        name="gamma_rows",
    )(*[blocks[n] for n in HELD], mine, theirs, scales)


def body(three_index, *energies):
    def swap_a(x):
        return lax.ppermute(x, "pair", SWAP_A)

    def swap_b(x):
        return lax.ppermute(x, "pair", SWAP_B)

    def swap_cores(x):
        return lax.ppermute(x, "core", SWAP_CORES)

    block = {0: three_index}
    block["A", 1] = swap_a(block[0])
    block["B", 1] = swap_b(block[0])
    denominator, scales = tables(*energies)
    block["B", 1], denominator, scales = lax.optimization_barrier(
        (block["B", 1], denominator, scales)
    )
    block["B", 2] = swap_b(block["A", 1])
    block["A", 2] = swap_a(block["B", 1])

    early, other_early = coulomb_pairs(block, EARLY)
    got_early = swap_cores(other_early)
    late, other_late = coulomb_pairs(block, LATE)
    got_late = swap_cores(other_late)
    summed = sum_cores((early, late), (got_early, got_late))

    summed, block["A", 2], block["B", 2] = lax.optimization_barrier(
        (summed, block["A", 2], block["B", 2])
    )
    block["A", 3] = swap_a(block["B", 2])
    block["B", 3] = swap_b(block["A", 2])
    parts = lax.all_to_all(summed, "z", 0, 0)
    parts = lax.all_to_all(sum_z(parts), ("pair", "x"), 0, 0)
    copies = amplitude_copies(parts, denominator)

    copies, block["A", 3], block["B", 3] = lax.optimization_barrier(
        (copies, block["A", 3], block["B", 3])
    )
    block["B", 4] = swap_b(block["A", 3])
    mine = lax.all_to_all(copies, ("z", "x"), 0, 0)
    mine, block["B", 4] = lax.optimization_barrier((mine, block["B", 4]))
    return gamma_rows(block, mine, swap_cores(mine), scales)


def solution(mesh):
    grid = Mesh(mesh.devices.reshape(NX, NZ, NCORE, NPAIR), AUX + ("pair",))
    placed = (P(AUX, "pair"), P(), P(), P(), P(), P())
    return jax.shard_map(
        body, mesh=grid, in_specs=placed, out_specs=P(AUX, "pair"), check_vma=False
    )
```

```python
import jax
import jax.numpy as jnp
from jax import lax
from jax.experimental import pallas as pl
from jax.experimental.pallas import tpu as pltpu
from jax.sharding import Mesh, PartitionSpec as P

TS = 128
VT = 157
NT = 16
NX, NZ, NCORE, NPAIR = 4, 8, 2, 8
NXZ = NX * NZ
AUX = ("x", "z", "core")
EARLY = ((0, 0), (0, 1), (-1, 1))
LATE = ((-1, 2), (-2, 2))
PAIRS = EARLY + LATE
WIDTH = 2 * TS
PIECE = WIDTH // NXZ
SENDS = ((0, (0, 1)), (1, (1, 2)), (-1, (2, 3)), (2, (3, 4)))
GETS = tuple((PAIRS[k][0] - d, PAIRS[k][1] - d) for d, pairs in SENDS for k in pairs)
ORDER = tuple((r, False) if c == 0 else (c, True) for r, c in GETS)
ROWS = 224
VMEM_LIMIT = 12 * 1024 * 1024
bf16, f32 = jnp.bfloat16, jnp.float32
in_vmem = pl.BlockSpec(memory_space=pltpu.VMEM)
in_smem = pl.BlockSpec(memory_space=pltpu.SMEM)


def ring(size, step):
    return [(i, (i + step) % size) for i in range(size)]


def tables(occupied_energy, virtual_energy, tile_occupied, tile_virtual, tile_exponent):
    def kernel(occupied, virtual, occupied_of, virtual_of, exponent, denominator, scales):
        me = lax.axis_index("pair")
        core = lax.axis_index("core")
        slot = lax.axis_index("z") * NX + lax.axis_index("x")
        half, first = slot // (NXZ // 2), (slot % (NXZ // 2)) * PIECE

        def tile_of(relative, part):
            return lax.rem(2 * (me + relative + NPAIR) + part, NT)

        def energy(tile):
            return virtual[pl.ds(virtual_of[tile], 1)] - occupied[occupied_of[tile]]

        def scale(tile):
            level = exponent[tile]
            return jnp.where(level == -1, 0.5, jnp.where(level == 1, 2.0, 1.0)).astype(f32)

        lane = lax.broadcasted_iota(jnp.int32, (PIECE, TS), 1)
        chosen = lane == first + lax.broadcasted_iota(jnp.int32, (PIECE, TS), 0)
        for k, (r, c) in enumerate(GETS):
            row, column = tile_of(r, core), tile_of(c, half)
            of_row = jnp.sum(jnp.where(chosen, energy(row), 0.0), axis=1, keepdims=True)
            level = jnp.full((PIECE, TS), scale(row) * scale(column), f32)
            denominator[k * PIECE : (k + 1) * PIECE] = (of_row + energy(column)) / level
        for i, (q, _) in enumerate(ORDER):
            for part in (0, 1):
                n = 2 * i + part
                scales[n : n + 1] = jnp.full((1, TS), scale(tile_of(q, part)), f32)

    return pl.pallas_call(
        kernel,
        out_shape=(
            jax.ShapeDtypeStruct((len(GETS) * PIECE, TS), f32),
            jax.ShapeDtypeStruct((2 * len(ORDER), TS), f32),
        ),
        in_specs=[in_smem, in_vmem, in_smem, in_smem, in_smem],
        out_specs=(in_vmem, in_vmem),
        compiler_params=pltpu.CompilerParams(vmem_limit_bytes=VMEM_LIMIT),
        name="tables",
    )(occupied_energy, virtual_energy.reshape(VT, TS), tile_occupied, tile_virtual, tile_exponent)


def coulomb_pairs(blocks, pairs):
    names = sorted({d for pair in pairs for d in pair})

    def kernel(*refs):
        block = dict(zip(names, refs))
        own, other = refs[len(names) :]
        core = lax.axis_index("core")
        for k, (r, c) in enumerate(pairs):
            for out, part in ((own, core), (other, 1 - core)):
                left = block[r][:, pl.ds(pl.multiple_of(part * TS, TS), TS)]
                product = lax.dot_general(
                    left, block[c][...], (((0,), (0,)), ((), ())), preferred_element_type=f32
                )
                for h in (0, 1):
                    out[k, h] = product[:, h * TS : (h + 1) * TS].astype(out.dtype)

    shape = (len(pairs), 2, TS, TS)
    return pl.pallas_call(
        kernel,
        out_shape=(jax.ShapeDtypeStruct(shape, f32), jax.ShapeDtypeStruct(shape, bf16)),
        in_specs=[in_vmem] * len(names),
        out_specs=(in_vmem, in_vmem),
        compiler_params=pltpu.CompilerParams(vmem_limit_bytes=VMEM_LIMIT),
        name="coulomb_pairs",
    )(*[blocks[d] for d in names])


def sum_cores(own, received):
    pairs = sum(a.shape[0] for a in own)
    rows = WIDTH // NZ

    def kernel(*refs):
        out = refs[-1]
        n = 0
        for mine, theirs in zip(refs[: len(own)], refs[len(own) : -1]):
            count = mine.shape[0]
            total = (mine[...] + theirs[...].astype(f32)).astype(bf16).reshape(count, NZ, rows, TS)
            for k in range(count):
                out[:, (n + k) * rows : (n + k + 1) * rows] = total[k]
            n += count

    return pl.pallas_call(
        kernel,
        out_shape=jax.ShapeDtypeStruct((NZ, pairs * rows, TS), bf16),
        in_specs=[in_vmem] * (2 * len(own)),
        out_specs=in_vmem,
        compiler_params=pltpu.CompilerParams(vmem_limit_bytes=VMEM_LIMIT),
        name="sum_cores",
    )(*own, *received)


def sum_z(parts):
    def kernel(parts_ref, out):
        me = lax.axis_index("pair")
        total = jnp.sum(parts_ref[...].astype(f32), axis=0).reshape(len(PAIRS), NX, PIECE, TS)
        out[...] = jnp.zeros_like(out)
        for d, (first, second) in SENDS:
            both = jnp.concatenate([total[first], total[second]], axis=1)
            out[pl.ds(NX * lax.rem(me + d + NPAIR, NPAIR), NX)] = both.astype(bf16)

    return pl.pallas_call(
        kernel,
        out_shape=jax.ShapeDtypeStruct((NPAIR * NX, 2 * PIECE, TS), bf16),
        in_specs=[in_vmem],
        out_specs=in_vmem,
        compiler_params=pltpu.CompilerParams(vmem_limit_bytes=VMEM_LIMIT),
        name="sum_z",
    )(parts)


def amplitude_copies(parts, denominator):
    rows = len(GETS) * PIECE

    def kernel(parts_ref, denominator_ref, out):
        me = lax.axis_index("pair")
        total = jnp.concatenate(
            [
                jnp.sum(parts_ref[pl.ds(NX * lax.rem(me - d + NPAIR, NPAIR), NX)].astype(f32), axis=0)
                for d, _ in SENDS
            ]
        )
        amplitude = (total / denominator_ref[...]).astype(bf16)
        out[...] = jnp.broadcast_to(amplitude[None], out.shape)

    return pl.pallas_call(
        kernel,
        out_shape=jax.ShapeDtypeStruct((NXZ, rows, TS), bf16),
        in_specs=[in_vmem] * 2,
        out_specs=in_vmem,
        compiler_params=pltpu.CompilerParams(vmem_limit_bytes=VMEM_LIMIT),
        name="amplitude_copies",
    )(parts, denominator)


def gamma_rows(blocks, last, mine, theirs, scales):
    rows, width = blocks[0].shape
    names = [q for q, _ in ORDER[:-1]]

    def kernel(*refs):
        block = dict(zip(names, refs))
        n = len(names)
        own, other, scale, out, matrix = refs[n + len(last) :]
        core = lax.axis_index("core")
        for pair in range(0, len(ORDER), 2):
            for part, source in ((core, own), (1 - core, other)):
                place = pl.ds(pl.multiple_of(part * TS, TS), TS)
                both = source[:, pair * PIECE : (pair + 2) * PIECE].astype(f32)
                for k in (0, 1):
                    i = pair + k
                    tiles = both[:, k * PIECE : (k + 1) * PIECE].reshape(2, TS, TS)
                    for h in (0, 1):
                        if ORDER[i][1]:
                            tile = tiles[h].T * scale[2 * i + h : 2 * i + h + 1]
                            matrix[i, h * TS : (h + 1) * TS, place] = tile.astype(bf16)
                        else:
                            tile = tiles[h] * scale[pl.ds(2 * i + part, 1)]
                            matrix[i, place, h * TS : (h + 1) * TS] = tile.astype(bf16)

        height = rows // len(last)
        for start in range(0, rows, ROWS):
            part, offset = divmod(start, height)
            total = jnp.dot(
                refs[n + part][offset : offset + ROWS], matrix[n], preferred_element_type=f32
            )
            for i, q in enumerate(names):
                total += jnp.dot(block[q][start : start + ROWS], matrix[i], preferred_element_type=f32)
            out[start : start + ROWS] = total.astype(bf16)

    return pl.pallas_call(
        kernel,
        out_shape=jax.ShapeDtypeStruct((rows, width), bf16),
        in_specs=[in_vmem] * (len(names) + len(last) + 3),
        out_specs=in_vmem,
        scratch_shapes=[pltpu.VMEM((len(ORDER), WIDTH, WIDTH), bf16)],
        compiler_params=pltpu.CompilerParams(vmem_limit_bytes=VMEM_LIMIT),
        name="gamma_rows",
    )(*[blocks[q] for q in names], *last, mine, theirs, scales)


def body(three_index, *energies):
    up, down = ring(NPAIR, 1), ring(NPAIR, -1)
    swap = ring(NCORE, 1)

    block = {0: three_index}
    block[-1] = lax.ppermute(block[0], "pair", up)
    block[1] = lax.ppermute(block[0], "pair", down)
    denominator, scales = tables(*energies)
    block[-1], denominator, scales = lax.optimization_barrier((block[-1], denominator, scales))
    block[-2] = lax.ppermute(block[-1], "pair", up)
    block[2] = lax.ppermute(block[1], "pair", down)

    early, other_early = coulomb_pairs(block, EARLY)
    got_early = lax.ppermute(other_early, "core", swap)
    late, other_late = coulomb_pairs(block, LATE)
    got_late = lax.ppermute(other_late, "core", swap)
    summed = sum_cores((early, late), (got_early, got_late))

    block[-3] = lax.ppermute(block[-2], "pair", up)
    parts = lax.all_to_all(summed, "z", 0, 0)
    parts, block[-3], block[2] = lax.optimization_barrier((parts, block[-3], block[2]))
    parts = lax.all_to_all(sum_z(parts), ("pair", "x"), 0, 0)
    copies = amplitude_copies(parts, denominator)
    copies, block[-3], block[2] = lax.optimization_barrier((copies, block[-3], block[2]))
    block[3] = lax.ppermute(block[2], "pair", down)
    last = (lax.ppermute(block[-3], "pair", up),)
    mine = lax.all_to_all(copies, ("z", "x"), 0, 0)
    mine, last, block[3] = lax.optimization_barrier((mine, last, block[3]))
    theirs = lax.ppermute(mine, "core", swap)
    return gamma_rows(block, last, mine, theirs, scales)


def solution(mesh):
    grid = Mesh(mesh.devices.reshape(NX, NZ, NCORE, NPAIR), AUX + ("pair",))
    placed = (P(AUX, "pair"), P(), P(), P(), P(), P())
    return jax.shard_map(
        body, mesh=grid, in_specs=placed, out_specs=P(AUX, "pair"), check_vma=False
    )
```

```python
import jax
import jax.numpy as jnp
from jax import lax
from jax.experimental import pallas as pl
from jax.experimental.pallas import tpu as pltpu
from jax.sharding import Mesh, PartitionSpec as P

TS = 128
VT = 157
NT = 16
NX, NZ, NCORE, NPAIR = 4, 8, 2, 8
NXZ = NX * NZ
AUX = ("x", "z", "core")
WIDTH = 2 * TS
PIECE = WIDTH // NXZ
CHUNKS = 2
SWAP_A = [(i, i ^ 1) for i in range(NPAIR)]
SWAP_B = [(i, (i + (-1 if i % 2 == 0 else 1)) % NPAIR) for i in range(NPAIR)]
SWAP_CORES = [(0, 1), (1, 0)]
HELD = (0, 1, -1, 2, -2, 3, -3, 4)
EARLY = 5
ROWS = 224
VMEM_LIMIT = 12 * 1024 * 1024
bf16, f32 = jnp.bfloat16, jnp.float32
in_vmem = pl.BlockSpec(memory_space=pltpu.VMEM)
in_smem = pl.BlockSpec(memory_space=pltpu.SMEM)
PARAMS = pltpu.CompilerParams(vmem_limit_bytes=VMEM_LIMIT)


def denominators(occupied_energy, virtual_energy, tile_occupied, tile_virtual, tile_exponent):
    def kernel(occupied, virtual, occupied_of, virtual_of, exponent, out):
        me = lax.axis_index("pair")
        core = lax.axis_index("core")
        side = 1 - 2 * lax.rem(me, 2)
        slot = lax.axis_index("z") * NX + lax.axis_index("x")
        half, first = slot // (NXZ // 2), (slot % (NXZ // 2)) * PIECE

        def tile_of(relative, part):
            return lax.rem(2 * (me + relative + NPAIR) + part, NT)

        def energy(tile):
            return virtual[pl.ds(virtual_of[tile], 1)] - occupied[occupied_of[tile]]

        def scale(tile):
            level = exponent[tile]
            return jnp.where(level == -1, 0.5, jnp.where(level == 1, 2.0, 1.0)).astype(f32)

        lane = lax.broadcasted_iota(jnp.int32, (PIECE, TS), 1)
        chosen = lane == first + lax.broadcasted_iota(jnp.int32, (PIECE, TS), 0)
        column = tile_of(0, half)
        for k, distance in enumerate(HELD):
            row = tile_of(side * distance, core)
            of_row = jnp.sum(jnp.where(chosen, energy(row), 0.0), axis=1, keepdims=True)
            level = jnp.full((PIECE, TS), scale(row) * scale(row) * scale(column), f32)
            out[k * PIECE : (k + 1) * PIECE] = (of_row + energy(column)) / level

    return pl.pallas_call(
        kernel,
        out_shape=jax.ShapeDtypeStruct((len(HELD) * PIECE, TS), f32),
        in_specs=[in_smem, in_vmem, in_smem, in_smem, in_smem],
        out_specs=in_vmem,
        compiler_params=PARAMS,
        name="denominators",
    )(occupied_energy, virtual_energy.reshape(VT, TS), tile_occupied, tile_virtual, tile_exponent)


def coulomb_blocks(own, blocks):
    height = own.shape[0] // CHUNKS
    given = [block for block in blocks if block is not None]

    def kernel(own_ref, *refs):
        mine, other = refs[-2:]
        core = lax.axis_index("core")
        n = 0
        for k, block in enumerate(blocks):
            if block is None:
                parts = [own_ref.at[i * height : (i + 1) * height] for i in range(CHUNKS)]
            else:
                parts = refs[n : n + CHUNKS]
                n += CHUNKS
            for out, part in ((mine, core), (other, 1 - core)):
                total = None
                for i, rows in enumerate(parts):
                    left = rows[:, pl.ds(pl.multiple_of(part * TS, TS), TS)]
                    right = own_ref[i * height : (i + 1) * height]
                    term = lax.dot_general(left, right, (((0,), (0,)), ((), ())), preferred_element_type=f32)
                    total = term if total is None else total + term
                for h in (0, 1):
                    out[k, h] = total[:, h * TS : (h + 1) * TS].astype(out.dtype)

    shape = (len(blocks), 2, TS, TS)
    return pl.pallas_call(
        kernel,
        out_shape=(jax.ShapeDtypeStruct(shape, f32), jax.ShapeDtypeStruct(shape, bf16)),
        in_specs=[in_vmem] * (1 + CHUNKS * len(given)),
        out_specs=(in_vmem, in_vmem),
        compiler_params=PARAMS,
        name="coulomb_blocks",
    )(own, *[part for block in given for part in block])


def sum_cores(own, received):
    count = sum(a.shape[0] for a in own)

    def kernel(*refs):
        parts = []
        for mine, theirs in zip(refs[: len(own)], refs[len(own) : -1]):
            total = (mine[...] + theirs[...].astype(f32)).reshape(-1, NXZ, PIECE, TS)
            parts += [total[k] for k in range(total.shape[0])]
        refs[-1][...] = jnp.concatenate(parts, axis=1).astype(bf16)

    return pl.pallas_call(
        kernel,
        out_shape=jax.ShapeDtypeStruct((NXZ, count * PIECE, TS), bf16),
        in_specs=[in_vmem] * (2 * len(own)),
        out_specs=in_vmem,
        compiler_params=PARAMS,
        name="sum_cores",
    )(*own, *received)


def amplitude_copies(parts, denominator):
    def kernel(parts_ref, denominator_ref, out):
        total = jnp.sum(parts_ref[...].astype(f32), axis=0)
        out[...] = jnp.broadcast_to((total / denominator_ref[...]).astype(bf16)[None], out.shape)

    return pl.pallas_call(
        kernel,
        out_shape=jax.ShapeDtypeStruct(parts.shape, bf16),
        in_specs=[in_vmem] * 2,
        out_specs=in_vmem,
        compiler_params=PARAMS,
        name="amplitude_copies",
    )(parts, denominator)


def gamma_rows(own, blocks, mine, theirs):
    rows, width = own.shape
    height = rows // CHUNKS

    def kernel(own_ref, *refs):
        block = refs[: CHUNKS * len(blocks)]
        mine_ref, theirs_ref, out, matrix = refs[CHUNKS * len(blocks) :]
        core = lax.axis_index("core")
        for pair in range(0, len(HELD), 2):
            for part, source in ((core, mine_ref), (1 - core, theirs_ref)):
                place = pl.ds(pl.multiple_of(part * TS, TS), TS)
                both = source[:, pair * PIECE : (pair + 2) * PIECE].astype(f32)
                for k in (0, 1):
                    tiles = both[:, k * PIECE : (k + 1) * PIECE].reshape(2, TS, TS).astype(bf16)
                    for h in (0, 1):
                        matrix[pair + k, place, h * TS : (h + 1) * TS] = tiles[h]

        for start in range(0, rows, ROWS):
            part, offset = divmod(start, height)
            total = jnp.dot(own_ref[start : start + ROWS], matrix[0], preferred_element_type=f32)
            for k in range(len(blocks)):
                left = block[CHUNKS * k + part][offset : offset + ROWS]
                total += jnp.dot(left, matrix[k + 1], preferred_element_type=f32)
            out[start : start + ROWS] = total.astype(bf16)

    return pl.pallas_call(
        kernel,
        out_shape=jax.ShapeDtypeStruct((rows, width), bf16),
        in_specs=[in_vmem] * (3 + CHUNKS * len(blocks)),
        out_specs=in_vmem,
        scratch_shapes=[pltpu.VMEM((len(HELD), WIDTH, WIDTH), bf16)],
        compiler_params=PARAMS,
        name="gamma_rows",
    )(own, *[part for block in blocks for part in block], mine, theirs)


def body(three_index, *energies):
    def swap_a(x):
        return lax.ppermute(x, "pair", SWAP_A)

    def swap_b(x):
        return lax.ppermute(x, "pair", SWAP_B)

    def swap_cores(x):
        return lax.ppermute(x, "core", SWAP_CORES)

    height = three_index.shape[0] // CHUNKS
    own = [three_index[i * height : (i + 1) * height] for i in range(CHUNKS)]
    a1, b1, a2, b2, a3, b3 = ([None] * CHUNKS for _ in range(6))
    for i in range(CHUNKS):
        a1[i], b1[i] = swap_a(own[i]), swap_b(own[i])
    denominator = denominators(*energies)
    a1[0], denominator = lax.optimization_barrier((a1[0], denominator))
    for i in range(CHUNKS):
        b2[i], a2[i] = swap_b(a1[i]), swap_a(b1[i])
    for i in range(CHUNKS):
        a3[i], b3[i] = swap_a(b2[i]), swap_b(a2[i])
    opposite = [swap_b(a3[0]), swap_a(b3[1])]
    blocks = [a1, b1, a2, b2, a3, b3, opposite]

    early, other_early = coulomb_blocks(three_index, [None] + blocks[: EARLY - 1])
    got_early = swap_cores(other_early)
    late, other_late = coulomb_blocks(three_index, blocks[EARLY - 1 :])
    got_late = swap_cores(other_late)
    parts = lax.all_to_all(sum_cores((early, late), (got_early, got_late)), ("z", "x"), 0, 0)
    mine = lax.all_to_all(amplitude_copies(parts, denominator), ("z", "x"), 0, 0)
    return gamma_rows(three_index, blocks, mine, swap_cores(mine))


def solution(mesh):
    grid = Mesh(mesh.devices.reshape(NX, NZ, NCORE, NPAIR), AUX + ("pair",))
    placed = (P(AUX, "pair"), P(), P(), P(), P(), P())
    return jax.shard_map(
        body, mesh=grid, in_specs=placed, out_specs=P(AUX, "pair"), check_vma=False
    )
```

```python
import jax
import jax.numpy as jnp
from jax import lax
from jax.experimental import pallas as pl
from jax.experimental.pallas import tpu as pltpu
from jax.sharding import Mesh, PartitionSpec as P

TS = 128
VT = 157
NT = 16
NX, NZ, NCORE, NPAIR = 4, 8, 2, 8
NXZ = NX * NZ
AUX = ("x", "z", "core")
EARLY = ((0, 0), (0, 1), (-1, 1))
LATE = ((-1, 2), (-2, 2))
PAIRS = EARLY + LATE
WIDTH = 2 * TS
PIECE = WIDTH // NXZ
SENDS = ((0, (0, 1)), (1, (1, 2)), (-1, (2, 3)), (2, (3, 4)))
GETS = tuple((PAIRS[k][0] - d, PAIRS[k][1] - d) for d, pairs in SENDS for k in pairs)
ORDER = tuple((r, False) if c == 0 else (c, True) for r, c in GETS)
ROWS = 224
VMEM_LIMIT = 12 * 1024 * 1024
bf16, f32 = jnp.bfloat16, jnp.float32
in_vmem = pl.BlockSpec(memory_space=pltpu.VMEM)
in_smem = pl.BlockSpec(memory_space=pltpu.SMEM)


SWAP_A = [(i, i ^ 1) for i in range(NPAIR)]
SWAP_B = [(i, (i + (-1 if i % 2 == 0 else 1)) % NPAIR) for i in range(NPAIR)]
SWAP_CORES = [(0, 1), (1, 0)]
HELD = (0, ("A", 1), ("B", 1), ("A", 2), ("B", 2), ("A", 3), ("B", 3), ("B", 4))


def held_name(relative, parity):
    if relative == 0:
        return 0
    if abs(relative) == 4:
        return ("B", 4)
    return ("A" if (relative > 0) == (parity == 0) else "B", abs(relative))


def tables(occupied_energy, virtual_energy, tile_occupied, tile_virtual, tile_exponent):
    def kernel(occupied, virtual, occupied_of, virtual_of, exponent, denominator, scales):
        me = lax.axis_index("pair")
        core = lax.axis_index("core")
        slot = lax.axis_index("z") * NX + lax.axis_index("x")
        half, first = slot // (NXZ // 2), (slot % (NXZ // 2)) * PIECE

        def tile_of(relative, part):
            return lax.rem(2 * (me + relative + NPAIR) + part, NT)

        def energy(tile):
            return virtual[pl.ds(virtual_of[tile], 1)] - occupied[occupied_of[tile]]

        def scale(tile):
            level = exponent[tile]
            return jnp.where(level == -1, 0.5, jnp.where(level == 1, 2.0, 1.0)).astype(f32)

        lane = lax.broadcasted_iota(jnp.int32, (PIECE, TS), 1)
        chosen = lane == first + lax.broadcasted_iota(jnp.int32, (PIECE, TS), 0)
        for k, (r, c) in enumerate(PAIRS):
            row, column = tile_of(r, core), tile_of(c, half)
            of_row = jnp.sum(jnp.where(chosen, energy(row), 0.0), axis=1, keepdims=True)
            level = jnp.full((PIECE, TS), scale(row) * scale(column), f32)
            denominator[k * PIECE : (k + 1) * PIECE] = (of_row + energy(column)) / level
        for i, (q, _) in enumerate(ORDER):
            for part in (0, 1):
                n = 2 * i + part
                scales[n : n + 1] = jnp.full((1, TS), scale(tile_of(q, part)), f32)

    return pl.pallas_call(
        kernel,
        out_shape=(
            jax.ShapeDtypeStruct((len(PAIRS) * PIECE, TS), f32),
            jax.ShapeDtypeStruct((2 * len(ORDER), TS), f32),
        ),
        in_specs=[in_smem, in_vmem, in_smem, in_smem, in_smem],
        out_specs=(in_vmem, in_vmem),
        compiler_params=pltpu.CompilerParams(vmem_limit_bytes=VMEM_LIMIT),
        name="tables",
    )(occupied_energy, virtual_energy.reshape(VT, TS), tile_occupied, tile_virtual, tile_exponent)


def coulomb_pairs(blocks, pairs):
    names = [
        n for n in HELD if n in {held_name(d, parity) for pair in pairs for d in pair for parity in (0, 1)}
    ]

    def kernel(*refs):
        block = dict(zip(names, refs))
        own, other = refs[len(names) :]
        core = lax.axis_index("core")
        me = lax.axis_index("pair")
        for parity in (0, 1):

            @pl.when(lax.rem(me, 2) == parity)
            def _(parity=parity):
                for k, (r, c) in enumerate(pairs):
                    rows, columns = block[held_name(r, parity)], block[held_name(c, parity)]
                    for out, part in ((own, core), (other, 1 - core)):
                        left = rows[:, pl.ds(pl.multiple_of(part * TS, TS), TS)]
                        product = lax.dot_general(
                            left, columns[...], (((0,), (0,)), ((), ())), preferred_element_type=f32
                        )
                        for h in (0, 1):
                            out[k, h] = product[:, h * TS : (h + 1) * TS].astype(out.dtype)

    shape = (len(pairs), 2, TS, TS)
    return pl.pallas_call(
        kernel,
        out_shape=(jax.ShapeDtypeStruct(shape, f32), jax.ShapeDtypeStruct(shape, bf16)),
        in_specs=[in_vmem] * len(names),
        out_specs=(in_vmem, in_vmem),
        compiler_params=pltpu.CompilerParams(vmem_limit_bytes=VMEM_LIMIT),
        name="coulomb_pairs",
    )(*[blocks[n] for n in names])


def sum_cores(own, received):
    count = sum(a.shape[0] for a in own)

    def kernel(*refs):
        parts = []
        for mine, theirs in zip(refs[: len(own)], refs[len(own) : -1]):
            total = (mine[...] + theirs[...].astype(f32)).reshape(-1, NXZ, PIECE, TS)
            parts += [total[k] for k in range(total.shape[0])]
        refs[-1][...] = jnp.concatenate(parts, axis=1).astype(bf16)

    return pl.pallas_call(
        kernel,
        out_shape=jax.ShapeDtypeStruct((NXZ, count * PIECE, TS), bf16),
        in_specs=[in_vmem] * (2 * len(own)),
        out_specs=in_vmem,
        compiler_params=pltpu.CompilerParams(vmem_limit_bytes=VMEM_LIMIT),
        name="sum_cores",
    )(*own, *received)


def amplitude_sends(parts, denominator):
    def kernel(parts_ref, denominator_ref, out):
        me = lax.axis_index("pair")
        total = jnp.sum(parts_ref[...].astype(f32), axis=0) / denominator_ref[...]
        out[...] = jnp.zeros_like(out)
        for d, (first, second) in SENDS:
            both = total[first * PIECE : (second + 1) * PIECE]
            out[lax.rem(me + d + NPAIR, NPAIR)] = both.astype(bf16)

    return pl.pallas_call(
        kernel,
        out_shape=jax.ShapeDtypeStruct((NPAIR, 2 * PIECE, TS), bf16),
        in_specs=[in_vmem] * 2,
        out_specs=in_vmem,
        compiler_params=pltpu.CompilerParams(vmem_limit_bytes=VMEM_LIMIT),
        name="amplitude_sends",
    )(parts, denominator)


def amplitude_copies(received):
    rows = len(GETS) * PIECE

    def kernel(received_ref, out):
        me = lax.axis_index("pair")
        pieces = [received_ref[lax.rem(me - d + NPAIR, NPAIR)] for d, _ in SENDS]
        out[...] = jnp.broadcast_to(jnp.concatenate(pieces)[None], out.shape)

    return pl.pallas_call(
        kernel,
        out_shape=jax.ShapeDtypeStruct((NXZ, rows, TS), bf16),
        in_specs=[in_vmem],
        out_specs=in_vmem,
        compiler_params=pltpu.CompilerParams(vmem_limit_bytes=VMEM_LIMIT),
        name="amplitude_copies",
    )(received)


def gamma_rows(blocks, mine, theirs, scales):
    rows, width = blocks[0].shape

    def kernel(*refs):
        block = refs[: len(HELD)]
        own, other, scale, out, matrix = refs[len(HELD) :]
        core = lax.axis_index("core")
        even = lax.rem(lax.axis_index("pair"), 2) == 0
        for pair in range(0, len(ORDER), 2):
            for part, source in ((core, own), (1 - core, other)):
                place = pl.ds(pl.multiple_of(part * TS, TS), TS)
                both = source[:, pair * PIECE : (pair + 2) * PIECE].astype(f32)
                for k in (0, 1):
                    i = pair + k
                    q, transposed = ORDER[i]
                    held = jnp.where(even, HELD.index(held_name(q, 0)), HELD.index(held_name(q, 1)))
                    tiles = both[:, k * PIECE : (k + 1) * PIECE].reshape(2, TS, TS)
                    for h in (0, 1):
                        if transposed:
                            tile = tiles[h].T * scale[2 * i + h : 2 * i + h + 1]
                            matrix[held, h * TS : (h + 1) * TS, place] = tile.astype(bf16)
                        else:
                            tile = tiles[h] * scale[pl.ds(2 * i + part, 1)]
                            matrix[held, place, h * TS : (h + 1) * TS] = tile.astype(bf16)

        for start in range(0, rows, ROWS):
            total = None
            for i, ref in enumerate(block):
                term = jnp.dot(ref[start : start + ROWS], matrix[i], preferred_element_type=f32)
                total = term if total is None else total + term
            out[start : start + ROWS] = total.astype(bf16)

    return pl.pallas_call(
        kernel,
        out_shape=jax.ShapeDtypeStruct((rows, width), bf16),
        in_specs=[in_vmem] * (len(HELD) + 3),
        out_specs=in_vmem,
        scratch_shapes=[pltpu.VMEM((len(HELD), WIDTH, WIDTH), bf16)],
        compiler_params=pltpu.CompilerParams(vmem_limit_bytes=VMEM_LIMIT),
        name="gamma_rows",
    )(*[blocks[n] for n in HELD], mine, theirs, scales)


def body(three_index, *energies):
    def swap_a(x):
        return lax.ppermute(x, "pair", SWAP_A)

    def swap_b(x):
        return lax.ppermute(x, "pair", SWAP_B)

    def swap_cores(x):
        return lax.ppermute(x, "core", SWAP_CORES)

    block = {0: three_index}
    block["A", 1] = swap_a(block[0])
    block["B", 1] = swap_b(block[0])
    denominator, scales = tables(*energies)
    block["B", 1], denominator, scales = lax.optimization_barrier(
        (block["B", 1], denominator, scales)
    )
    block["B", 2] = swap_b(block["A", 1])
    block["A", 2] = swap_a(block["B", 1])

    early, other_early = coulomb_pairs(block, EARLY)
    got_early = swap_cores(other_early)
    late, other_late = coulomb_pairs(block, LATE)
    got_late = swap_cores(other_late)
    summed = sum_cores((early, late), (got_early, got_late))

    summed, block["A", 2], block["B", 2] = lax.optimization_barrier(
        (summed, block["A", 2], block["B", 2])
    )
    block["A", 3] = swap_a(block["B", 2])
    block["B", 3] = swap_b(block["A", 2])
    parts = lax.all_to_all(summed, ("z", "x"), 0, 0)
    block["B", 4] = swap_b(block["A", 3])
    received = lax.all_to_all(amplitude_sends(parts, denominator), "pair", 0, 0)
    copies = amplitude_copies(received)
    copies, block["B", 3], block["B", 4] = lax.optimization_barrier((copies, block["B", 3], block["B", 4]))
    mine = lax.all_to_all(copies, ("z", "x"), 0, 0)
    return gamma_rows(block, mine, swap_cores(mine), scales)


def solution(mesh):
    grid = Mesh(mesh.devices.reshape(NX, NZ, NCORE, NPAIR), AUX + ("pair",))
    placed = (P(AUX, "pair"), P(), P(), P(), P(), P())
    return jax.shard_map(
        body, mesh=grid, in_specs=placed, out_specs=P(AUX, "pair"), check_vma=False
    )
```

```python
import jax
import jax.numpy as jnp
from jax import lax
from jax.experimental import pallas as pl
from jax.experimental.pallas import tpu as pltpu
from jax.sharding import Mesh, PartitionSpec as P

TS = 128
VT = 157
NT = 16
NX, NZ, NCORE, NPAIR = 4, 8, 2, 8
NXZ = NX * NZ
AUX = ("x", "z", "core")
EARLY = ((0, 0), (0, 1), (-1, 1))
LATE = ((-1, 2), (-2, 2))
PAIRS = EARLY + LATE
WIDTH = 2 * TS
PIECE = WIDTH // NXZ
SENDS = ((0, (0, 1)), (1, (1, 2)), (-1, (2, 3)), (2, (3, 4)))
GETS = tuple((PAIRS[k][0] - d, PAIRS[k][1] - d) for d, pairs in SENDS for k in pairs)
ORDER = tuple((r, False) if c == 0 else (c, True) for r, c in GETS)
ROWS = 224
VMEM_LIMIT = 12 * 1024 * 1024
bf16, f32 = jnp.bfloat16, jnp.float32
in_vmem = pl.BlockSpec(memory_space=pltpu.VMEM)
in_smem = pl.BlockSpec(memory_space=pltpu.SMEM)


SWAP_A = [(i, i ^ 1) for i in range(NPAIR)]
SWAP_B = [(i, (i + (-1 if i % 2 == 0 else 1)) % NPAIR) for i in range(NPAIR)]
SWAP_CORES = [(0, 1), (1, 0)]
HELD = (0, ("A", 1), ("B", 1), ("A", 2), ("B", 2), ("A", 3), ("B", 3), ("B", 4))


def held_name(relative, parity):
    if relative == 0:
        return 0
    if abs(relative) == 4:
        return ("B", 4)
    return ("A" if (relative > 0) == (parity == 0) else "B", abs(relative))


def tables(occupied_energy, virtual_energy, tile_occupied, tile_virtual, tile_exponent):
    def kernel(occupied, virtual, occupied_of, virtual_of, exponent, denominator, scales):
        me = lax.axis_index("pair")
        core = lax.axis_index("core")
        slot = lax.axis_index("z") * NX + lax.axis_index("x")
        half, first = slot // (NXZ // 2), (slot % (NXZ // 2)) * PIECE

        def tile_of(relative, part):
            return lax.rem(2 * (me + relative + NPAIR) + part, NT)

        def energy(tile):
            return virtual[pl.ds(virtual_of[tile], 1)] - occupied[occupied_of[tile]]

        def scale(tile):
            level = exponent[tile]
            return jnp.where(level == -1, 0.5, jnp.where(level == 1, 2.0, 1.0)).astype(f32)

        lane = lax.broadcasted_iota(jnp.int32, (PIECE, TS), 1)
        chosen = lane == first + lax.broadcasted_iota(jnp.int32, (PIECE, TS), 0)
        for k, (r, c) in enumerate(GETS):
            row, column = tile_of(r, core), tile_of(c, half)
            of_row = jnp.sum(jnp.where(chosen, energy(row), 0.0), axis=1, keepdims=True)
            level = jnp.full((PIECE, TS), scale(row) * scale(column), f32)
            denominator[k * PIECE : (k + 1) * PIECE] = (of_row + energy(column)) / level
        for i, (q, _) in enumerate(ORDER):
            for part in (0, 1):
                n = 2 * i + part
                scales[n : n + 1] = jnp.full((1, TS), scale(tile_of(q, part)), f32)

    return pl.pallas_call(
        kernel,
        out_shape=(
            jax.ShapeDtypeStruct((len(GETS) * PIECE, TS), f32),
            jax.ShapeDtypeStruct((2 * len(ORDER), TS), f32),
        ),
        in_specs=[in_smem, in_vmem, in_smem, in_smem, in_smem],
        out_specs=(in_vmem, in_vmem),
        compiler_params=pltpu.CompilerParams(vmem_limit_bytes=VMEM_LIMIT),
        name="tables",
    )(occupied_energy, virtual_energy.reshape(VT, TS), tile_occupied, tile_virtual, tile_exponent)


def coulomb_pairs(blocks, pairs):
    names = [
        n for n in HELD if n in {held_name(d, parity) for pair in pairs for d in pair for parity in (0, 1)}
    ]

    def kernel(*refs):
        block = dict(zip(names, refs))
        own, other = refs[len(names) :]
        core = lax.axis_index("core")
        me = lax.axis_index("pair")
        for parity in (0, 1):

            @pl.when(lax.rem(me, 2) == parity)
            def _(parity=parity):
                for k, (r, c) in enumerate(pairs):
                    rows, columns = block[held_name(r, parity)], block[held_name(c, parity)]
                    for out, part in ((own, core), (other, 1 - core)):
                        left = rows[:, pl.ds(pl.multiple_of(part * TS, TS), TS)]
                        product = lax.dot_general(
                            left, columns[...], (((0,), (0,)), ((), ())), preferred_element_type=f32
                        )
                        for h in (0, 1):
                            out[k, h] = product[:, h * TS : (h + 1) * TS].astype(out.dtype)

    shape = (len(pairs), 2, TS, TS)
    return pl.pallas_call(
        kernel,
        out_shape=(jax.ShapeDtypeStruct(shape, f32), jax.ShapeDtypeStruct(shape, bf16)),
        in_specs=[in_vmem] * len(names),
        out_specs=(in_vmem, in_vmem),
        compiler_params=pltpu.CompilerParams(vmem_limit_bytes=VMEM_LIMIT),
        name="coulomb_pairs",
    )(*[blocks[n] for n in names])


def sum_cores(own, received):
    pairs = sum(a.shape[0] for a in own)
    rows = WIDTH // NZ

    def kernel(*refs):
        out = refs[-1]
        n = 0
        for mine, theirs in zip(refs[: len(own)], refs[len(own) : -1]):
            count = mine.shape[0]
            total = (mine[...] + theirs[...].astype(f32)).astype(bf16).reshape(count, NZ, rows, TS)
            for k in range(count):
                out[:, (n + k) * rows : (n + k + 1) * rows] = total[k]
            n += count

    return pl.pallas_call(
        kernel,
        out_shape=jax.ShapeDtypeStruct((NZ, pairs * rows, TS), bf16),
        in_specs=[in_vmem] * (2 * len(own)),
        out_specs=in_vmem,
        compiler_params=pltpu.CompilerParams(vmem_limit_bytes=VMEM_LIMIT),
        name="sum_cores",
    )(*own, *received)


def sum_z(parts):
    def kernel(parts_ref, out):
        me = lax.axis_index("pair")
        total = jnp.sum(parts_ref[...].astype(f32), axis=0).reshape(len(PAIRS), NX, PIECE, TS)
        out[...] = jnp.zeros_like(out)
        for d, (first, second) in SENDS:
            both = jnp.concatenate([total[first], total[second]], axis=1)
            out[pl.ds(NX * lax.rem(me + d + NPAIR, NPAIR), NX)] = both.astype(bf16)

    return pl.pallas_call(
        kernel,
        out_shape=jax.ShapeDtypeStruct((NPAIR * NX, 2 * PIECE, TS), bf16),
        in_specs=[in_vmem],
        out_specs=in_vmem,
        compiler_params=pltpu.CompilerParams(vmem_limit_bytes=VMEM_LIMIT),
        name="sum_z",
    )(parts)


def amplitude_copies(parts, denominator):
    rows = len(GETS) * PIECE

    def kernel(parts_ref, denominator_ref, out):
        me = lax.axis_index("pair")
        total = jnp.concatenate(
            [
                jnp.sum(parts_ref[pl.ds(NX * lax.rem(me - d + NPAIR, NPAIR), NX)].astype(f32), axis=0)
                for d, _ in SENDS
            ]
        )
        amplitude = (total / denominator_ref[...]).astype(bf16)
        out[...] = jnp.broadcast_to(amplitude[None], out.shape)

    return pl.pallas_call(
        kernel,
        out_shape=jax.ShapeDtypeStruct((NXZ, rows, TS), bf16),
        in_specs=[in_vmem] * 2,
        out_specs=in_vmem,
        compiler_params=pltpu.CompilerParams(vmem_limit_bytes=VMEM_LIMIT),
        name="amplitude_copies",
    )(parts, denominator)


def gamma_rows(blocks, mine, theirs, scales):
    rows, width = blocks[0].shape

    def kernel(*refs):
        block = refs[: len(HELD)]
        own, other, scale, out, matrix = refs[len(HELD) :]
        core = lax.axis_index("core")
        even = lax.rem(lax.axis_index("pair"), 2) == 0
        for pair in range(0, len(ORDER), 2):
            for part, source in ((core, own), (1 - core, other)):
                place = pl.ds(pl.multiple_of(part * TS, TS), TS)
                both = source[:, pair * PIECE : (pair + 2) * PIECE].astype(f32)
                for k in (0, 1):
                    i = pair + k
                    q, transposed = ORDER[i]
                    held = jnp.where(even, HELD.index(held_name(q, 0)), HELD.index(held_name(q, 1)))
                    tiles = both[:, k * PIECE : (k + 1) * PIECE].reshape(2, TS, TS)
                    for h in (0, 1):
                        if transposed:
                            tile = tiles[h].T * scale[2 * i + h : 2 * i + h + 1]
                            matrix[held, h * TS : (h + 1) * TS, place] = tile.astype(bf16)
                        else:
                            tile = tiles[h] * scale[pl.ds(2 * i + part, 1)]
                            matrix[held, place, h * TS : (h + 1) * TS] = tile.astype(bf16)

        for start in range(0, rows, ROWS):
            total = None
            for i, ref in enumerate(block):
                term = jnp.dot(ref[start : start + ROWS], matrix[i], preferred_element_type=f32)
                total = term if total is None else total + term
            out[start : start + ROWS] = total.astype(bf16)

    return pl.pallas_call(
        kernel,
        out_shape=jax.ShapeDtypeStruct((rows, width), bf16),
        in_specs=[in_vmem] * (len(HELD) + 3),
        out_specs=in_vmem,
        scratch_shapes=[pltpu.VMEM((len(HELD), WIDTH, WIDTH), bf16)],
        compiler_params=pltpu.CompilerParams(vmem_limit_bytes=VMEM_LIMIT),
        name="gamma_rows",
    )(*[blocks[n] for n in HELD], mine, theirs, scales)


def body(three_index, *energies):
    def swap_a(x):
        return lax.ppermute(x, "pair", SWAP_A)

    def swap_b(x):
        return lax.ppermute(x, "pair", SWAP_B)

    def swap_cores(x):
        return lax.ppermute(x, "core", SWAP_CORES)

    block = {0: three_index}
    block["A", 1] = swap_a(block[0])
    block["B", 1] = swap_b(block[0])
    denominator, scales = tables(*energies)
    block["B", 1], denominator, scales = lax.optimization_barrier(
        (block["B", 1], denominator, scales)
    )
    block["B", 2] = swap_b(block["A", 1])
    block["A", 2] = swap_a(block["B", 1])

    early, other_early = coulomb_pairs(block, EARLY)
    got_early = swap_cores(other_early)
    late, other_late = coulomb_pairs(block, LATE)
    got_late = swap_cores(other_late)
    summed = sum_cores((early, late), (got_early, got_late))

    summed, block["A", 2], block["B", 2] = lax.optimization_barrier(
        (summed, block["A", 2], block["B", 2])
    )
    block["A", 3] = swap_a(block["B", 2])
    block["B", 3] = swap_b(block["A", 2])
    parts = lax.all_to_all(summed, "z", 0, 0)
    slots = sum_z(parts)
    parts = lax.all_to_all(slots, ("pair", "x"), 0, 0)
    block["B", 4] = swap_b(block["A", 3])
    copies = amplitude_copies(parts, denominator)
    copies, block["B", 3], block["B", 4] = lax.optimization_barrier((copies, block["B", 3], block["B", 4]))
    mine = lax.all_to_all(copies, ("z", "x"), 0, 0)
    return gamma_rows(block, mine, swap_cores(mine), scales)


def solution(mesh):
    grid = Mesh(mesh.devices.reshape(NX, NZ, NCORE, NPAIR), AUX + ("pair",))
    placed = (P(AUX, "pair"), P(), P(), P(), P(), P())
    return jax.shard_map(
        body, mesh=grid, in_specs=placed, out_specs=P(AUX, "pair"), check_vma=False
    )
```

```python
import jax
import jax.numpy as jnp
from jax import lax
from jax.experimental import pallas as pl
from jax.experimental.pallas import tpu as pltpu
from jax.sharding import Mesh, PartitionSpec as P

TS = 128
VT = 157
NT = 16
NX, NZ, NCORE, NPAIR = 4, 8, 2, 8
NXZ = NX * NZ
AUX = ("x", "z", "core")
EARLY = ((0, 0), (0, 1), (-1, 1))
LATE = ((-1, 2), (-2, 2))
PAIRS = EARLY + LATE
WIDTH = 2 * TS
PIECE = WIDTH // NXZ
SENDS = ((0, (0, 1)), (1, (1, 2)), (-1, (2, 3)), (2, (3, 4)))
GETS = tuple((PAIRS[k][0] - d, PAIRS[k][1] - d) for d, pairs in SENDS for k in pairs)
ORDER = tuple((r, False) if c == 0 else (c, True) for r, c in GETS)
ROWS = 224
VMEM_LIMIT = 12 * 1024 * 1024
bf16, f32 = jnp.bfloat16, jnp.float32
in_vmem = pl.BlockSpec(memory_space=pltpu.VMEM)
in_smem = pl.BlockSpec(memory_space=pltpu.SMEM)


SWAP_A = [(i, i ^ 1) for i in range(NPAIR)]
SWAP_B = [(i, (i + (-1 if i % 2 == 0 else 1)) % NPAIR) for i in range(NPAIR)]
SWAP_CORES = [(0, 1), (1, 0)]
HELD = (0, ("A", 1), ("B", 1), ("A", 2), ("B", 2), ("A", 3), ("B", 3), ("B", 4))


def held_name(relative, parity):
    if relative == 0:
        return 0
    if abs(relative) == 4:
        return ("B", 4)
    return ("A" if (relative > 0) == (parity == 0) else "B", abs(relative))


def tables(occupied_energy, virtual_energy, tile_occupied, tile_virtual, tile_exponent):
    def kernel(occupied, virtual, occupied_of, virtual_of, exponent, denominator, scales):
        me = lax.axis_index("pair")
        core = lax.axis_index("core")
        slot = lax.axis_index("z") * NX + lax.axis_index("x")
        half, first = slot // (NXZ // 2), (slot % (NXZ // 2)) * PIECE

        def tile_of(relative, part):
            return lax.rem(2 * (me + relative + NPAIR) + part, NT)

        def energy(tile):
            return virtual[pl.ds(virtual_of[tile], 1)] - occupied[occupied_of[tile]]

        def scale(tile):
            level = exponent[tile]
            return jnp.where(level == -1, 0.5, jnp.where(level == 1, 2.0, 1.0)).astype(f32)

        lane = lax.broadcasted_iota(jnp.int32, (PIECE, TS), 1)
        chosen = lane == first + lax.broadcasted_iota(jnp.int32, (PIECE, TS), 0)
        for k, (r, c) in enumerate(GETS):
            row, column = tile_of(r, core), tile_of(c, half)
            of_row = jnp.sum(jnp.where(chosen, energy(row), 0.0), axis=1, keepdims=True)
            level = jnp.full((PIECE, TS), scale(row) * scale(column), f32)
            denominator[k * PIECE : (k + 1) * PIECE] = (of_row + energy(column)) / level
        for i, (q, _) in enumerate(ORDER):
            for part in (0, 1):
                n = 2 * i + part
                scales[n : n + 1] = jnp.full((1, TS), scale(tile_of(q, part)), f32)

    return pl.pallas_call(
        kernel,
        out_shape=(
            jax.ShapeDtypeStruct((len(GETS) * PIECE, TS), f32),
            jax.ShapeDtypeStruct((2 * len(ORDER), TS), f32),
        ),
        in_specs=[in_smem, in_vmem, in_smem, in_smem, in_smem],
        out_specs=(in_vmem, in_vmem),
        compiler_params=pltpu.CompilerParams(vmem_limit_bytes=VMEM_LIMIT),
        name="tables",
    )(occupied_energy, virtual_energy.reshape(VT, TS), tile_occupied, tile_virtual, tile_exponent)


def coulomb_pairs(blocks, pairs, joined=None):
    names = [
        n for n in HELD if n in {held_name(d, parity) for pair in pairs for d in pair for parity in (0, 1)}
    ]
    counts = [len(blocks[n]) for n in names]
    rows = sum(part.shape[0] for part in blocks[names[0]])
    most = max(counts)
    height = rows // most

    def kernel(*refs):
        parts = {}
        given = list(refs[: sum(counts)])
        for n, count in zip(names, counts):
            mine, given = given[:count], given[count:]
            parts[n] = mine if count == most else [
                mine[0].at[i * height : (i + 1) * height] for i in range(most)
            ]
        own, other, *whole = refs[sum(counts) :]
        core = lax.axis_index("core")
        me = lax.axis_index("pair")
        for parity in (0, 1):

            @pl.when(lax.rem(me, 2) == parity)
            def _(parity=parity):
                for k, (r, c) in enumerate(pairs):
                    for out, part in ((own, core), (other, 1 - core)):
                        place = pl.ds(pl.multiple_of(part * TS, TS), TS)
                        total = None
                        for left, right in zip(parts[held_name(r, parity)], parts[held_name(c, parity)]):
                            term = lax.dot_general(
                                left[:, place], right[...], (((0,), (0,)), ((), ())), preferred_element_type=f32
                            )
                            total = term if total is None else total + term
                        for h in (0, 1):
                            out[k, h] = total[:, h * TS : (h + 1) * TS].astype(out.dtype)

        for ref in whole:
            for i, part in enumerate(parts[joined]):
                ref[i * height : (i + 1) * height] = part[...]

    shape = (len(pairs), 2, TS, TS)
    out_shape = [jax.ShapeDtypeStruct(shape, f32), jax.ShapeDtypeStruct(shape, bf16)]
    if joined is not None:
        out_shape.append(jax.ShapeDtypeStruct((rows, WIDTH), bf16))
    return pl.pallas_call(
        kernel,
        out_shape=out_shape,
        in_specs=[in_vmem] * sum(counts),
        out_specs=[in_vmem] * len(out_shape),
        compiler_params=pltpu.CompilerParams(vmem_limit_bytes=VMEM_LIMIT),
        name="coulomb_pairs",
    )(*[part for n in names for part in blocks[n]])


def sum_cores(own, received):
    pairs = sum(a.shape[0] for a in own)
    rows = WIDTH // NZ

    def kernel(*refs):
        out = refs[-1]
        n = 0
        for mine, theirs in zip(refs[: len(own)], refs[len(own) : -1]):
            count = mine.shape[0]
            total = (mine[...] + theirs[...].astype(f32)).astype(bf16).reshape(count, NZ, rows, TS)
            for k in range(count):
                out[:, (n + k) * rows : (n + k + 1) * rows] = total[k]
            n += count

    return pl.pallas_call(
        kernel,
        out_shape=jax.ShapeDtypeStruct((NZ, pairs * rows, TS), bf16),
        in_specs=[in_vmem] * (2 * len(own)),
        out_specs=in_vmem,
        compiler_params=pltpu.CompilerParams(vmem_limit_bytes=VMEM_LIMIT),
        name="sum_cores",
    )(*own, *received)


def sum_z(parts):
    def kernel(parts_ref, out):
        me = lax.axis_index("pair")
        total = jnp.sum(parts_ref[...].astype(f32), axis=0).reshape(len(PAIRS), NX, PIECE, TS)
        out[...] = jnp.zeros_like(out)
        for d, (first, second) in SENDS:
            both = jnp.concatenate([total[first], total[second]], axis=1)
            out[pl.ds(NX * lax.rem(me + d + NPAIR, NPAIR), NX)] = both.astype(bf16)

    return pl.pallas_call(
        kernel,
        out_shape=jax.ShapeDtypeStruct((NPAIR * NX, 2 * PIECE, TS), bf16),
        in_specs=[in_vmem],
        out_specs=in_vmem,
        compiler_params=pltpu.CompilerParams(vmem_limit_bytes=VMEM_LIMIT),
        name="sum_z",
    )(parts)


def amplitude_copies(parts, denominator):
    rows = len(GETS) * PIECE

    def kernel(parts_ref, denominator_ref, out):
        me = lax.axis_index("pair")
        total = jnp.concatenate(
            [
                jnp.sum(parts_ref[pl.ds(NX * lax.rem(me - d + NPAIR, NPAIR), NX)].astype(f32), axis=0)
                for d, _ in SENDS
            ]
        )
        amplitude = (total / denominator_ref[...]).astype(bf16)
        out[...] = jnp.broadcast_to(amplitude[None], out.shape)

    return pl.pallas_call(
        kernel,
        out_shape=jax.ShapeDtypeStruct((NXZ, rows, TS), bf16),
        in_specs=[in_vmem] * 2,
        out_specs=in_vmem,
        compiler_params=pltpu.CompilerParams(vmem_limit_bytes=VMEM_LIMIT),
        name="amplitude_copies",
    )(parts, denominator)


def gamma_rows(blocks, mine, theirs, scales):
    rows, width = blocks[0][0].shape
    counts = [len(blocks[n]) for n in HELD]

    def kernel(*refs):
        given = list(refs[: sum(counts)])
        block = []
        for count in counts:
            block.append(given[:count])
            given = given[count:]
        own, other, scale, out, matrix = refs[sum(counts) :]
        core = lax.axis_index("core")
        even = lax.rem(lax.axis_index("pair"), 2) == 0
        for pair in range(0, len(ORDER), 2):
            for part, source in ((core, own), (1 - core, other)):
                place = pl.ds(pl.multiple_of(part * TS, TS), TS)
                both = source[:, pair * PIECE : (pair + 2) * PIECE].astype(f32)
                for k in (0, 1):
                    i = pair + k
                    q, transposed = ORDER[i]
                    held = jnp.where(even, HELD.index(held_name(q, 0)), HELD.index(held_name(q, 1)))
                    tiles = both[:, k * PIECE : (k + 1) * PIECE].reshape(2, TS, TS)
                    for h in (0, 1):
                        if transposed:
                            tile = tiles[h].T * scale[2 * i + h : 2 * i + h + 1]
                            matrix[held, h * TS : (h + 1) * TS, place] = tile.astype(bf16)
                        else:
                            tile = tiles[h] * scale[pl.ds(2 * i + part, 1)]
                            matrix[held, place, h * TS : (h + 1) * TS] = tile.astype(bf16)

        for start in range(0, rows, ROWS):
            total = None
            for i, parts in enumerate(block):
                part, offset = divmod(start, rows // len(parts))
                left = parts[part][offset : offset + ROWS]
                term = jnp.dot(left, matrix[i], preferred_element_type=f32)
                total = term if total is None else total + term
            out[start : start + ROWS] = total.astype(bf16)

    return pl.pallas_call(
        kernel,
        out_shape=jax.ShapeDtypeStruct((rows, width), bf16),
        in_specs=[in_vmem] * (sum(counts) + 3),
        out_specs=in_vmem,
        scratch_shapes=[pltpu.VMEM((len(HELD), WIDTH, WIDTH), bf16)],
        compiler_params=pltpu.CompilerParams(vmem_limit_bytes=VMEM_LIMIT),
        name="gamma_rows",
    )(*[part for n in HELD for part in blocks[n]], mine, theirs, scales)


def body(three_index, *energies):
    def swap_a(x):
        return lax.ppermute(x, "pair", SWAP_A)

    def swap_b(x):
        return lax.ppermute(x, "pair", SWAP_B)

    def swap_cores(x):
        return lax.ppermute(x, "core", SWAP_CORES)

    half = three_index.shape[0] // 2
    block = {0: [three_index]}
    block["A", 1] = [swap_a(three_index)]
    block["B", 1] = [swap_b(three_index[:half]), swap_b(three_index[half:])]
    denominator, scales = tables(*energies)
    block["B", 1][1], denominator, scales = lax.optimization_barrier(
        (block["B", 1][1], denominator, scales)
    )
    block["B", 2] = [swap_b(block["A", 1][0])]
    block["A", 2] = [swap_a(part) for part in block["B", 1]]

    early, other_early = coulomb_pairs(block, EARLY)
    got_early = swap_cores(other_early)
    late, other_late, joined = coulomb_pairs(block, LATE, ("A", 2))
    got_late = swap_cores(other_late)
    summed = sum_cores((early, late), (got_early, got_late))
    block["A", 2] = [joined]

    b2, a2 = block["B", 2][0], joined
    summed, b2, a2 = lax.optimization_barrier((summed, b2, a2))
    a3, b3 = swap_a(b2), swap_b(a2)
    parts = lax.all_to_all(summed, "z", 0, 0)
    parts = lax.all_to_all(sum_z(parts), ("pair", "x"), 0, 0)
    copies = amplitude_copies(parts, denominator)

    copies, a3, b3 = lax.optimization_barrier((copies, a3, b3))
    b4 = swap_b(a3)
    mine = lax.all_to_all(copies, ("z", "x"), 0, 0)
    mine, b4 = lax.optimization_barrier((mine, b4))
    block.update({("B", 2): [b2], ("A", 2): [a2], ("A", 3): [a3], ("B", 3): [b3], ("B", 4): [b4]})
    return gamma_rows(block, mine, swap_cores(mine), scales)


def solution(mesh):
    grid = Mesh(mesh.devices.reshape(NX, NZ, NCORE, NPAIR), AUX + ("pair",))
    placed = (P(AUX, "pair"), P(), P(), P(), P(), P())
    return jax.shard_map(
        body, mesh=grid, in_specs=placed, out_specs=P(AUX, "pair"), check_vma=False
    )
```

```python
import jax
import jax.numpy as jnp
from jax import lax
from jax.experimental import pallas as pl
from jax.experimental.pallas import tpu as pltpu
from jax.sharding import Mesh, PartitionSpec as P

TS = 128
VT = 157
NT = 16
NX, NZ, NCORE, NPAIR = 4, 8, 2, 8
NXZ = NX * NZ
AUX = ("x", "z", "core")
EARLY = ((0, 0), (0, 1), (-1, 1))
LATE = ((-1, 2), (-2, 2))
PAIRS = EARLY + LATE
WIDTH = 2 * TS
PIECE = WIDTH // NXZ
SENDS = ((0, (0, 1)), (1, (1, 2)), (-1, (2, 3)), (2, (3, 4)))
GETS = tuple((PAIRS[k][0] - d, PAIRS[k][1] - d) for d, pairs in SENDS for k in pairs)
ORDER = tuple((r, False) if c == 0 else (c, True) for r, c in GETS)
ROWS = 224
VMEM_LIMIT = 12 * 1024 * 1024
bf16, f32 = jnp.bfloat16, jnp.float32
in_vmem = pl.BlockSpec(memory_space=pltpu.VMEM)
in_smem = pl.BlockSpec(memory_space=pltpu.SMEM)


SWAP_A = [(i, i ^ 1) for i in range(NPAIR)]
SWAP_B = [(i, (i + (-1 if i % 2 == 0 else 1)) % NPAIR) for i in range(NPAIR)]
SWAP_CORES = [(0, 1), (1, 0)]
HELD = (0, ("A", 1), ("B", 1), ("A", 2), ("B", 2), ("A", 3), ("B", 3), ("B", 4))


def held_name(relative, parity):
    if relative == 0:
        return 0
    if abs(relative) == 4:
        return ("B", 4)
    return ("A" if (relative > 0) == (parity == 0) else "B", abs(relative))


def tables(occupied_energy, virtual_energy, tile_occupied, tile_virtual, tile_exponent):
    def kernel(occupied, virtual, occupied_of, virtual_of, exponent, denominator, scales):
        me = lax.axis_index("pair")
        core = lax.axis_index("core")
        slot = lax.axis_index("z") * NX + lax.axis_index("x")
        half, first = slot // (NXZ // 2), (slot % (NXZ // 2)) * PIECE

        def tile_of(relative, part):
            return lax.rem(2 * (me + relative + NPAIR) + part, NT)

        def energy(tile):
            return virtual[pl.ds(virtual_of[tile], 1)] - occupied[occupied_of[tile]]

        def scale(tile):
            level = exponent[tile]
            return jnp.where(level == -1, 0.5, jnp.where(level == 1, 2.0, 1.0)).astype(f32)

        lane = lax.broadcasted_iota(jnp.int32, (PIECE, TS), 1)
        chosen = lane == first + lax.broadcasted_iota(jnp.int32, (PIECE, TS), 0)
        for k, (r, c) in enumerate(GETS):
            row, column = tile_of(r, core), tile_of(c, half)
            of_row = jnp.sum(jnp.where(chosen, energy(row), 0.0), axis=1, keepdims=True)
            level = jnp.full((PIECE, TS), scale(row) * scale(column), f32)
            denominator[k * PIECE : (k + 1) * PIECE] = (of_row + energy(column)) / level
        for i, (q, _) in enumerate(ORDER):
            for part in (0, 1):
                n = 2 * i + part
                scales[n : n + 1] = jnp.full((1, TS), scale(tile_of(q, part)), f32)

    return pl.pallas_call(
        kernel,
        out_shape=(
            jax.ShapeDtypeStruct((len(GETS) * PIECE, TS), f32),
            jax.ShapeDtypeStruct((2 * len(ORDER), TS), f32),
        ),
        in_specs=[in_smem, in_vmem, in_smem, in_smem, in_smem],
        out_specs=(in_vmem, in_vmem),
        compiler_params=pltpu.CompilerParams(vmem_limit_bytes=VMEM_LIMIT),
        name="tables",
    )(occupied_energy, virtual_energy.reshape(VT, TS), tile_occupied, tile_virtual, tile_exponent)


def coulomb_pairs(blocks, pairs, joined=None):
    names = [
        n for n in HELD if n in {held_name(d, parity) for pair in pairs for d in pair for parity in (0, 1)}
    ]
    counts = [len(blocks[n]) for n in names]
    rows = sum(part.shape[0] for part in blocks[names[0]])
    most = max(counts)
    height = rows // most

    def kernel(*refs):
        parts = {}
        given = list(refs[: sum(counts)])
        for n, count in zip(names, counts):
            mine, given = given[:count], given[count:]
            parts[n] = mine if count == most else [
                mine[0].at[i * height : (i + 1) * height] for i in range(most)
            ]
        own, other, *whole = refs[sum(counts) :]
        core = lax.axis_index("core")
        me = lax.axis_index("pair")
        for parity in (0, 1):

            @pl.when(lax.rem(me, 2) == parity)
            def _(parity=parity):
                for k, (r, c) in enumerate(pairs):
                    for out, part in ((own, core), (other, 1 - core)):
                        place = pl.ds(pl.multiple_of(part * TS, TS), TS)
                        total = None
                        for left, right in zip(parts[held_name(r, parity)], parts[held_name(c, parity)]):
                            term = lax.dot_general(
                                left[:, place], right[...], (((0,), (0,)), ((), ())), preferred_element_type=f32
                            )
                            total = term if total is None else total + term
                        for h in (0, 1):
                            out[k, h] = total[:, h * TS : (h + 1) * TS].astype(out.dtype)

        for ref in whole:
            for i, part in enumerate(parts[joined]):
                ref[i * height : (i + 1) * height] = part[...]

    shape = (len(pairs), 2, TS, TS)
    out_shape = [jax.ShapeDtypeStruct(shape, f32), jax.ShapeDtypeStruct(shape, bf16)]
    if joined is not None:
        out_shape.append(jax.ShapeDtypeStruct((rows, WIDTH), bf16))
    return pl.pallas_call(
        kernel,
        out_shape=out_shape,
        in_specs=[in_vmem] * sum(counts),
        out_specs=[in_vmem] * len(out_shape),
        compiler_params=pltpu.CompilerParams(vmem_limit_bytes=VMEM_LIMIT),
        name="coulomb_pairs",
    )(*[part for n in names for part in blocks[n]])


def sum_cores(own, received):
    pairs = sum(a.shape[0] for a in own)
    rows = WIDTH // NZ

    def kernel(*refs):
        out = refs[-1]
        n = 0
        for mine, theirs in zip(refs[: len(own)], refs[len(own) : -1]):
            count = mine.shape[0]
            total = (mine[...] + theirs[...].astype(f32)).astype(bf16).reshape(count, NZ, rows, TS)
            for k in range(count):
                out[:, (n + k) * rows : (n + k + 1) * rows] = total[k]
            n += count

    return pl.pallas_call(
        kernel,
        out_shape=jax.ShapeDtypeStruct((NZ, pairs * rows, TS), bf16),
        in_specs=[in_vmem] * (2 * len(own)),
        out_specs=in_vmem,
        compiler_params=pltpu.CompilerParams(vmem_limit_bytes=VMEM_LIMIT),
        name="sum_cores",
    )(*own, *received)


def sum_z(parts):
    def kernel(parts_ref, out):
        me = lax.axis_index("pair")
        total = jnp.sum(parts_ref[...].astype(f32), axis=0).reshape(len(PAIRS), NX, PIECE, TS)
        out[...] = jnp.zeros_like(out)
        for d, (first, second) in SENDS:
            both = jnp.concatenate([total[first], total[second]], axis=1)
            out[pl.ds(NX * lax.rem(me + d + NPAIR, NPAIR), NX)] = both.astype(bf16)

    return pl.pallas_call(
        kernel,
        out_shape=jax.ShapeDtypeStruct((NPAIR * NX, 2 * PIECE, TS), bf16),
        in_specs=[in_vmem],
        out_specs=in_vmem,
        compiler_params=pltpu.CompilerParams(vmem_limit_bytes=VMEM_LIMIT),
        name="sum_z",
    )(parts)


def amplitude_copies(parts, denominator):
    rows = len(GETS) * PIECE

    def kernel(parts_ref, denominator_ref, out):
        me = lax.axis_index("pair")
        total = jnp.concatenate(
            [
                jnp.sum(parts_ref[pl.ds(NX * lax.rem(me - d + NPAIR, NPAIR), NX)].astype(f32), axis=0)
                for d, _ in SENDS
            ]
        )
        amplitude = (total / denominator_ref[...]).astype(bf16)
        out[...] = jnp.broadcast_to(amplitude[None], out.shape)

    return pl.pallas_call(
        kernel,
        out_shape=jax.ShapeDtypeStruct((NXZ, rows, TS), bf16),
        in_specs=[in_vmem] * 2,
        out_specs=in_vmem,
        compiler_params=pltpu.CompilerParams(vmem_limit_bytes=VMEM_LIMIT),
        name="amplitude_copies",
    )(parts, denominator)


def gamma_rows(blocks, mine, theirs, scales):
    rows, width = blocks[0][0].shape
    counts = [len(blocks[n]) for n in HELD]

    def kernel(*refs):
        given = list(refs[: sum(counts)])
        block = []
        for count in counts:
            block.append(given[:count])
            given = given[count:]
        own, other, scale, out, matrix = refs[sum(counts) :]
        core = lax.axis_index("core")
        even = lax.rem(lax.axis_index("pair"), 2) == 0
        for pair in range(0, len(ORDER), 2):
            for part, source in ((core, own), (1 - core, other)):
                place = pl.ds(pl.multiple_of(part * TS, TS), TS)
                both = source[:, pair * PIECE : (pair + 2) * PIECE].astype(f32)
                for k in (0, 1):
                    i = pair + k
                    q, transposed = ORDER[i]
                    held = jnp.where(even, HELD.index(held_name(q, 0)), HELD.index(held_name(q, 1)))
                    tiles = both[:, k * PIECE : (k + 1) * PIECE].reshape(2, TS, TS)
                    for h in (0, 1):
                        if transposed:
                            tile = tiles[h].T * scale[2 * i + h : 2 * i + h + 1]
                            matrix[held, h * TS : (h + 1) * TS, place] = tile.astype(bf16)
                        else:
                            tile = tiles[h] * scale[pl.ds(2 * i + part, 1)]
                            matrix[held, place, h * TS : (h + 1) * TS] = tile.astype(bf16)

        for start in range(0, rows, ROWS):
            total = None
            for i, parts in enumerate(block):
                part, offset = divmod(start, rows // len(parts))
                left = parts[part][offset : offset + ROWS]
                term = jnp.dot(left, matrix[i], preferred_element_type=f32)
                total = term if total is None else total + term
            out[start : start + ROWS] = total.astype(bf16)

    return pl.pallas_call(
        kernel,
        out_shape=jax.ShapeDtypeStruct((rows, width), bf16),
        in_specs=[in_vmem] * (sum(counts) + 3),
        out_specs=in_vmem,
        scratch_shapes=[pltpu.VMEM((len(HELD), WIDTH, WIDTH), bf16)],
        compiler_params=pltpu.CompilerParams(vmem_limit_bytes=VMEM_LIMIT),
        name="gamma_rows",
    )(*[part for n in HELD for part in blocks[n]], mine, theirs, scales)


def body(three_index, *energies):
    def swap_a(x):
        return lax.ppermute(x, "pair", SWAP_A)

    def swap_b(x):
        return lax.ppermute(x, "pair", SWAP_B)

    def swap_cores(x):
        return lax.ppermute(x, "core", SWAP_CORES)

    half = three_index.shape[0] // 2
    block = {0: [three_index]}
    block["A", 1] = [swap_a(three_index)]
    block["B", 1] = [swap_b(three_index[:half]), swap_b(three_index[half:])]
    block["B", 2] = [swap_b(block["A", 1][0])]
    block["A", 2] = [swap_a(part) for part in block["B", 1]]

    early, other_early = coulomb_pairs(block, EARLY)
    denominator, scales = tables(*energies)
    other_early, denominator, scales = lax.optimization_barrier((other_early, denominator, scales))
    got_early = swap_cores(other_early)
    late, other_late, joined = coulomb_pairs(block, LATE, ("A", 2))
    got_late = swap_cores(other_late)
    summed = sum_cores((early, late), (got_early, got_late))
    block["A", 2] = [joined]

    b2, a2 = block["B", 2][0], joined
    summed, b2, a2 = lax.optimization_barrier((summed, b2, a2))
    a3, b3 = swap_a(b2), swap_b(a2)
    parts = lax.all_to_all(summed, "z", 0, 0)
    parts = lax.all_to_all(sum_z(parts), ("pair", "x"), 0, 0)
    copies = amplitude_copies(parts, denominator)

    copies, a3, b3 = lax.optimization_barrier((copies, a3, b3))
    b4 = [swap_b(a3[:half]), swap_a(b3[half:])]
    mine = lax.all_to_all(copies, ("z", "x"), 0, 0)
    mine, b4 = lax.optimization_barrier((mine, b4))
    block.update({("B", 2): [b2], ("A", 2): [a2], ("A", 3): [a3], ("B", 3): [b3], ("B", 4): b4})
    return gamma_rows(block, mine, swap_cores(mine), scales)


def solution(mesh):
    grid = Mesh(mesh.devices.reshape(NX, NZ, NCORE, NPAIR), AUX + ("pair",))
    placed = (P(AUX, "pair"), P(), P(), P(), P(), P())
    return jax.shard_map(
        body, mesh=grid, in_specs=placed, out_specs=P(AUX, "pair"), check_vma=False
    )
```

```python
import jax
import jax.numpy as jnp
from jax import lax
from jax.experimental import pallas as pl
from jax.experimental.pallas import tpu as pltpu
from jax.sharding import Mesh, PartitionSpec as P

TS = 128
VT = 157
NT = 16
NX, NZ, NCORE, NPAIR = 4, 8, 2, 8
NXZ = NX * NZ
AUX = ("x", "z", "core")
EARLY = ((0, 0), (0, 1), (-1, 1))
LATE = ((-1, 2), (-2, 2))
PAIRS = EARLY + LATE
WIDTH = 2 * TS
PIECE = WIDTH // NXZ
SENDS = ((0, (0, 1)), (1, (1, 2)), (-1, (2, 3)), (2, (3, 4)))
GETS = tuple((PAIRS[k][0] - d, PAIRS[k][1] - d) for d, pairs in SENDS for k in pairs)
ORDER = tuple((r, False) if c == 0 else (c, True) for r, c in GETS)
ROWS = 224
FETCHED = (("A", 3),)
VMEM_LIMIT = 12 * 1024 * 1024
bf16, f32 = jnp.bfloat16, jnp.float32
in_vmem = pl.BlockSpec(memory_space=pltpu.VMEM)
anywhere = pl.BlockSpec(memory_space=pl.ANY)
in_smem = pl.BlockSpec(memory_space=pltpu.SMEM)


SWAP_A = [(i, i ^ 1) for i in range(NPAIR)]
SWAP_B = [(i, (i + (-1 if i % 2 == 0 else 1)) % NPAIR) for i in range(NPAIR)]
SWAP_CORES = [(0, 1), (1, 0)]
HELD = (0, ("A", 1), ("B", 1), ("A", 2), ("B", 2), ("A", 3), ("B", 3), ("B", 4))


def held_name(relative, parity):
    if relative == 0:
        return 0
    if abs(relative) == 4:
        return ("B", 4)
    return ("A" if (relative > 0) == (parity == 0) else "B", abs(relative))


def tables(occupied_energy, virtual_energy, tile_occupied, tile_virtual, tile_exponent):
    def kernel(occupied, virtual, occupied_of, virtual_of, exponent, denominator, scales):
        me = lax.axis_index("pair")
        core = lax.axis_index("core")
        slot = lax.axis_index("z") * NX + lax.axis_index("x")
        half, first = slot // (NXZ // 2), (slot % (NXZ // 2)) * PIECE

        def tile_of(relative, part):
            return lax.rem(2 * (me + relative + NPAIR) + part, NT)

        def energy(tile):
            return virtual[pl.ds(virtual_of[tile], 1)] - occupied[occupied_of[tile]]

        def scale(tile):
            level = exponent[tile]
            return jnp.where(level == -1, 0.5, jnp.where(level == 1, 2.0, 1.0)).astype(f32)

        lane = lax.broadcasted_iota(jnp.int32, (PIECE, TS), 1)
        chosen = lane == first + lax.broadcasted_iota(jnp.int32, (PIECE, TS), 0)
        for k, (r, c) in enumerate(GETS):
            row, column = tile_of(r, core), tile_of(c, half)
            of_row = jnp.sum(jnp.where(chosen, energy(row), 0.0), axis=1, keepdims=True)
            level = jnp.full((PIECE, TS), scale(row) * scale(column), f32)
            denominator[k * PIECE : (k + 1) * PIECE] = (of_row + energy(column)) / level
        for i, (q, _) in enumerate(ORDER):
            for part in (0, 1):
                n = 2 * i + part
                scales[n : n + 1] = jnp.full((1, TS), scale(tile_of(q, part)), f32)

    return pl.pallas_call(
        kernel,
        out_shape=(
            jax.ShapeDtypeStruct((len(GETS) * PIECE, TS), f32),
            jax.ShapeDtypeStruct((2 * len(ORDER), TS), f32),
        ),
        in_specs=[in_smem, in_vmem, in_smem, in_smem, in_smem],
        out_specs=(in_vmem, in_vmem),
        compiler_params=pltpu.CompilerParams(vmem_limit_bytes=VMEM_LIMIT),
        name="tables",
    )(occupied_energy, virtual_energy.reshape(VT, TS), tile_occupied, tile_virtual, tile_exponent)


def coulomb_pairs(blocks, pairs):
    names = [
        n for n in HELD if n in {held_name(d, parity) for pair in pairs for d in pair for parity in (0, 1)}
    ]
    counts = [len(blocks[n]) for n in names]
    rows = sum(part.shape[0] for part in blocks[names[0]])
    most = max(counts)
    height = rows // most

    def kernel(*refs):
        parts = {}
        given = list(refs[: sum(counts)])
        for n, count in zip(names, counts):
            mine, given = given[:count], given[count:]
            parts[n] = mine if count == most else [
                mine[0].at[i * height : (i + 1) * height] for i in range(most)
            ]
        own, other = refs[sum(counts) :]
        core = lax.axis_index("core")
        me = lax.axis_index("pair")
        for parity in (0, 1):

            @pl.when(lax.rem(me, 2) == parity)
            def _(parity=parity):
                for k, (r, c) in enumerate(pairs):
                    for out, part in ((own, core), (other, 1 - core)):
                        place = pl.ds(pl.multiple_of(part * TS, TS), TS)
                        total = None
                        for left, right in zip(parts[held_name(r, parity)], parts[held_name(c, parity)]):
                            term = lax.dot_general(
                                left[:, place], right[...], (((0,), (0,)), ((), ())), preferred_element_type=f32
                            )
                            total = term if total is None else total + term
                        for h in (0, 1):
                            out[k, h] = total[:, h * TS : (h + 1) * TS].astype(out.dtype)

    shape = (len(pairs), 2, TS, TS)
    out_shape = [jax.ShapeDtypeStruct(shape, f32), jax.ShapeDtypeStruct(shape, bf16)]
    return pl.pallas_call(
        kernel,
        out_shape=out_shape,
        in_specs=[in_vmem] * sum(counts),
        out_specs=[in_vmem] * len(out_shape),
        compiler_params=pltpu.CompilerParams(vmem_limit_bytes=VMEM_LIMIT),
        name="coulomb_pairs",
    )(*[part for n in names for part in blocks[n]])


def sum_cores(own, received):
    pairs = sum(a.shape[0] for a in own)
    rows = WIDTH // NZ

    def kernel(*refs):
        out = refs[-1]
        n = 0
        for mine, theirs in zip(refs[: len(own)], refs[len(own) : -1]):
            count = mine.shape[0]
            total = (mine[...] + theirs[...].astype(f32)).astype(bf16).reshape(count, NZ, rows, TS)
            for k in range(count):
                out[:, (n + k) * rows : (n + k + 1) * rows] = total[k]
            n += count

    return pl.pallas_call(
        kernel,
        out_shape=jax.ShapeDtypeStruct((NZ, pairs * rows, TS), bf16),
        in_specs=[in_vmem] * (2 * len(own)),
        out_specs=in_vmem,
        compiler_params=pltpu.CompilerParams(vmem_limit_bytes=VMEM_LIMIT),
        name="sum_cores",
    )(*own, *received)


def sum_z(parts):
    def kernel(parts_ref, out):
        me = lax.axis_index("pair")
        total = jnp.sum(parts_ref[...].astype(f32), axis=0).reshape(len(PAIRS), NX, PIECE, TS)
        out[...] = jnp.zeros_like(out)
        for d, (first, second) in SENDS:
            both = jnp.concatenate([total[first], total[second]], axis=1)
            out[pl.ds(NX * lax.rem(me + d + NPAIR, NPAIR), NX)] = both.astype(bf16)

    return pl.pallas_call(
        kernel,
        out_shape=jax.ShapeDtypeStruct((NPAIR * NX, 2 * PIECE, TS), bf16),
        in_specs=[in_vmem],
        out_specs=in_vmem,
        compiler_params=pltpu.CompilerParams(vmem_limit_bytes=VMEM_LIMIT),
        name="sum_z",
    )(parts)


def amplitude_copies(parts, denominator):
    rows = len(GETS) * PIECE

    def kernel(parts_ref, denominator_ref, out):
        me = lax.axis_index("pair")
        total = jnp.concatenate(
            [
                jnp.sum(parts_ref[pl.ds(NX * lax.rem(me - d + NPAIR, NPAIR), NX)].astype(f32), axis=0)
                for d, _ in SENDS
            ]
        )
        amplitude = (total / denominator_ref[...]).astype(bf16)
        out[...] = jnp.broadcast_to(amplitude[None], out.shape)

    return pl.pallas_call(
        kernel,
        out_shape=jax.ShapeDtypeStruct((NXZ, rows, TS), bf16),
        in_specs=[in_vmem] * 2,
        out_specs=in_vmem,
        compiler_params=pltpu.CompilerParams(vmem_limit_bytes=VMEM_LIMIT),
        name="amplitude_copies",
    )(parts, denominator)


def gamma_rows(blocks, mine, theirs, scales):
    rows, width = blocks[0][0].shape
    counts = [len(blocks[n]) for n in HELD]

    def kernel(*refs):
        given = list(refs[: sum(counts)])
        block = []
        for count in counts:
            block.append(given[:count])
            given = given[count:]
        own, other, scale, out, matrix, held, arrived = refs[sum(counts) :]
        fetches = []
        for k, name in enumerate(FETCHED):
            i = HELD.index(name)
            fetches.append(pltpu.make_async_copy(block[i][0], held.at[k], arrived.at[k]))
            block[i] = [held.at[k]]
        for fetch in fetches:
            fetch.start()
        core = lax.axis_index("core")
        even = lax.rem(lax.axis_index("pair"), 2) == 0
        for pair in range(0, len(ORDER), 2):
            for part, source in ((core, own), (1 - core, other)):
                place = pl.ds(pl.multiple_of(part * TS, TS), TS)
                both = source[:, pair * PIECE : (pair + 2) * PIECE].astype(f32)
                for k in (0, 1):
                    i = pair + k
                    q, transposed = ORDER[i]
                    held = jnp.where(even, HELD.index(held_name(q, 0)), HELD.index(held_name(q, 1)))
                    tiles = both[:, k * PIECE : (k + 1) * PIECE].reshape(2, TS, TS)
                    for h in (0, 1):
                        if transposed:
                            tile = tiles[h].T * scale[2 * i + h : 2 * i + h + 1]
                            matrix[held, h * TS : (h + 1) * TS, place] = tile.astype(bf16)
                        else:
                            tile = tiles[h] * scale[pl.ds(2 * i + part, 1)]
                            matrix[held, place, h * TS : (h + 1) * TS] = tile.astype(bf16)

        for fetch in fetches:
            fetch.wait()
        for start in range(0, rows, ROWS):
            total = None
            for i, parts in enumerate(block):
                part, offset = divmod(start, rows // len(parts))
                left = parts[part][offset : offset + ROWS]
                term = jnp.dot(left, matrix[i], preferred_element_type=f32)
                total = term if total is None else total + term
            out[start : start + ROWS] = total.astype(bf16)

    return pl.pallas_call(
        kernel,
        out_shape=jax.ShapeDtypeStruct((rows, width), bf16),
        in_specs=[anywhere if n in FETCHED else in_vmem for n in HELD for _ in blocks[n]]
        + [in_vmem] * 3,
        out_specs=in_vmem,
        scratch_shapes=[
            pltpu.VMEM((len(HELD), WIDTH, WIDTH), bf16),
            pltpu.VMEM((len(FETCHED), rows, width), bf16),
            pltpu.SemaphoreType.DMA((len(FETCHED),)),
        ],
        compiler_params=pltpu.CompilerParams(vmem_limit_bytes=VMEM_LIMIT),
        name="gamma_rows",
    )(*[part for n in HELD for part in blocks[n]], mine, theirs, scales)


def body(three_index, *energies):
    def swap_a(x):
        return lax.ppermute(x, "pair", SWAP_A)

    def swap_b(x):
        return lax.ppermute(x, "pair", SWAP_B)

    def swap_cores(x):
        return lax.ppermute(x, "core", SWAP_CORES)

    half = three_index.shape[0] // 2
    block = {0: [three_index]}
    block["A", 1] = [swap_a(three_index)]
    block["B", 1] = [swap_b(three_index[:half]), swap_b(three_index[half:])]
    block["B", 2] = [swap_b(block["A", 1][0])]
    block["A", 2] = [swap_a(part) for part in block["B", 1]]

    early, other_early = coulomb_pairs(block, EARLY)
    denominator, scales = tables(*energies)
    other_early, denominator, scales = lax.optimization_barrier((other_early, denominator, scales))
    got_early = swap_cores(other_early)
    late, other_late = coulomb_pairs(block, LATE)
    got_late = swap_cores(other_late)
    summed = sum_cores((early, late), (got_early, got_late))

    summed, b2, a2 = lax.optimization_barrier((summed, block["B", 2], block["A", 2]))
    a3, b3 = swap_a(b2[0]), swap_b(jnp.concatenate(a2))
    parts = lax.all_to_all(summed, "z", 0, 0)
    parts = lax.all_to_all(sum_z(parts), ("pair", "x"), 0, 0)
    copies = amplitude_copies(parts, denominator)

    copies, a3, b3 = lax.optimization_barrier((copies, a3, b3))
    b4 = [swap_b(a3[:half]), swap_a(b3[half:])]
    mine = lax.all_to_all(copies, ("z", "x"), 0, 0)
    mine, b4 = lax.optimization_barrier((mine, b4))
    block.update({("B", 2): b2, ("A", 2): a2, ("A", 3): [a3], ("B", 3): [b3], ("B", 4): b4})
    return gamma_rows(block, mine, swap_cores(mine), scales)


def solution(mesh):
    grid = Mesh(mesh.devices.reshape(NX, NZ, NCORE, NPAIR), AUX + ("pair",))
    placed = (P(AUX, "pair"), P(), P(), P(), P(), P())
    return jax.shard_map(
        body, mesh=grid, in_specs=placed, out_specs=P(AUX, "pair"), check_vma=False
    )
```

```python
import jax
import jax.numpy as jnp
from jax import lax
from jax.experimental import pallas as pl
from jax.experimental.pallas import tpu as pltpu
from jax.sharding import Mesh, PartitionSpec as P

TS = 128
VT = 157
NT = 16
NX, NZ, NCORE, NPAIR = 4, 8, 2, 8
NXZ = NX * NZ
AUX = ("x", "z", "core")
EARLY = ((0, 0), (0, 1), (-1, 1))
LATE = ((-1, 2), (-2, 2))
PAIRS = EARLY + LATE
WIDTH = 2 * TS
PIECE = WIDTH // NXZ
SENDS = ((0, (0, 1)), (1, (1, 2)), (-1, (2, 3)), (2, (3, 4)))
GETS = tuple((PAIRS[k][0] - d, PAIRS[k][1] - d) for d, pairs in SENDS for k in pairs)
ORDER = tuple((r, False) if c == 0 else (c, True) for r, c in GETS)
ROWS = 224
FETCHED = (("A", 3), ("B", 3))
PARKED = (("A", 1), ("B", 1))
VMEM_LIMIT = 12 * 1024 * 1024
bf16, f32 = jnp.bfloat16, jnp.float32
in_vmem = pl.BlockSpec(memory_space=pltpu.VMEM)
anywhere = pl.BlockSpec(memory_space=pl.ANY)
in_smem = pl.BlockSpec(memory_space=pltpu.SMEM)


SWAP_A = [(i, i ^ 1) for i in range(NPAIR)]
SWAP_B = [(i, (i + (-1 if i % 2 == 0 else 1)) % NPAIR) for i in range(NPAIR)]
SWAP_CORES = [(0, 1), (1, 0)]
HELD = (0, ("A", 1), ("B", 1), ("A", 2), ("B", 2), ("A", 3), ("B", 3), ("B", 4))


def held_name(relative, parity):
    if relative == 0:
        return 0
    if abs(relative) == 4:
        return ("B", 4)
    return ("A" if (relative > 0) == (parity == 0) else "B", abs(relative))


def tables(occupied_energy, virtual_energy, tile_occupied, tile_virtual, tile_exponent):
    def kernel(occupied, virtual, occupied_of, virtual_of, exponent, denominator, scales):
        me = lax.axis_index("pair")
        core = lax.axis_index("core")
        slot = lax.axis_index("z") * NX + lax.axis_index("x")
        half, first = slot // (NXZ // 2), (slot % (NXZ // 2)) * PIECE

        def tile_of(relative, part):
            return lax.rem(2 * (me + relative + NPAIR) + part, NT)

        def energy(tile):
            return virtual[pl.ds(virtual_of[tile], 1)] - occupied[occupied_of[tile]]

        def scale(tile):
            level = exponent[tile]
            return jnp.where(level == -1, 0.5, jnp.where(level == 1, 2.0, 1.0)).astype(f32)

        lane = lax.broadcasted_iota(jnp.int32, (PIECE, TS), 1)
        chosen = lane == first + lax.broadcasted_iota(jnp.int32, (PIECE, TS), 0)
        for k, (r, c) in enumerate(GETS):
            row, column = tile_of(r, core), tile_of(c, half)
            of_row = jnp.sum(jnp.where(chosen, energy(row), 0.0), axis=1, keepdims=True)
            level = jnp.full((PIECE, TS), scale(row) * scale(column), f32)
            denominator[k * PIECE : (k + 1) * PIECE] = (of_row + energy(column)) / level
        for i, (q, _) in enumerate(ORDER):
            for part in (0, 1):
                n = 2 * i + part
                scales[n : n + 1] = jnp.full((1, TS), scale(tile_of(q, part)), f32)

    return pl.pallas_call(
        kernel,
        out_shape=(
            jax.ShapeDtypeStruct((len(GETS) * PIECE, TS), f32),
            jax.ShapeDtypeStruct((2 * len(ORDER), TS), f32),
        ),
        in_specs=[in_smem, in_vmem, in_smem, in_smem, in_smem],
        out_specs=(in_vmem, in_vmem),
        compiler_params=pltpu.CompilerParams(vmem_limit_bytes=VMEM_LIMIT),
        name="tables",
    )(occupied_energy, virtual_energy.reshape(VT, TS), tile_occupied, tile_virtual, tile_exponent)


def coulomb_pairs(blocks, pairs):
    names = [
        n for n in HELD if n in {held_name(d, parity) for pair in pairs for d in pair for parity in (0, 1)}
    ]
    counts = [len(blocks[n]) for n in names]
    rows = sum(part.shape[0] for part in blocks[names[0]])
    most = max(counts)
    height = rows // most

    def kernel(*refs):
        parts = {}
        given = list(refs[: sum(counts)])
        for n, count in zip(names, counts):
            mine, given = given[:count], given[count:]
            parts[n] = mine if count == most else [
                mine[0].at[i * height : (i + 1) * height] for i in range(most)
            ]
        own, other = refs[sum(counts) :]
        core = lax.axis_index("core")
        me = lax.axis_index("pair")
        for parity in (0, 1):

            @pl.when(lax.rem(me, 2) == parity)
            def _(parity=parity):
                for k, (r, c) in enumerate(pairs):
                    for out, part in ((own, core), (other, 1 - core)):
                        place = pl.ds(pl.multiple_of(part * TS, TS), TS)
                        total = None
                        for left, right in zip(parts[held_name(r, parity)], parts[held_name(c, parity)]):
                            term = lax.dot_general(
                                left[:, place], right[...], (((0,), (0,)), ((), ())), preferred_element_type=f32
                            )
                            total = term if total is None else total + term
                        for h in (0, 1):
                            out[k, h] = total[:, h * TS : (h + 1) * TS].astype(out.dtype)

    shape = (len(pairs), 2, TS, TS)
    out_shape = [jax.ShapeDtypeStruct(shape, f32), jax.ShapeDtypeStruct(shape, bf16)]
    return pl.pallas_call(
        kernel,
        out_shape=out_shape,
        in_specs=[in_vmem] * sum(counts),
        out_specs=[in_vmem] * len(out_shape),
        compiler_params=pltpu.CompilerParams(vmem_limit_bytes=VMEM_LIMIT),
        name="coulomb_pairs",
    )(*[part for n in names for part in blocks[n]])


def sum_cores(own, received):
    pairs = sum(a.shape[0] for a in own)
    rows = WIDTH // NZ

    def kernel(*refs):
        out = refs[-1]
        n = 0
        for mine, theirs in zip(refs[: len(own)], refs[len(own) : -1]):
            count = mine.shape[0]
            total = (mine[...] + theirs[...].astype(f32)).astype(bf16).reshape(count, NZ, rows, TS)
            for k in range(count):
                out[:, (n + k) * rows : (n + k + 1) * rows] = total[k]
            n += count

    return pl.pallas_call(
        kernel,
        out_shape=jax.ShapeDtypeStruct((NZ, pairs * rows, TS), bf16),
        in_specs=[in_vmem] * (2 * len(own)),
        out_specs=in_vmem,
        compiler_params=pltpu.CompilerParams(vmem_limit_bytes=VMEM_LIMIT),
        name="sum_cores",
    )(*own, *received)


def sum_z(parts):
    def kernel(parts_ref, out):
        me = lax.axis_index("pair")
        total = jnp.sum(parts_ref[...].astype(f32), axis=0).reshape(len(PAIRS), NX, PIECE, TS)
        out[...] = jnp.zeros_like(out)
        for d, (first, second) in SENDS:
            both = jnp.concatenate([total[first], total[second]], axis=1)
            out[pl.ds(NX * lax.rem(me + d + NPAIR, NPAIR), NX)] = both.astype(bf16)

    return pl.pallas_call(
        kernel,
        out_shape=jax.ShapeDtypeStruct((NPAIR * NX, 2 * PIECE, TS), bf16),
        in_specs=[in_vmem],
        out_specs=in_vmem,
        compiler_params=pltpu.CompilerParams(vmem_limit_bytes=VMEM_LIMIT),
        name="sum_z",
    )(parts)


def amplitude_copies(parts, denominator):
    rows = len(GETS) * PIECE

    def kernel(parts_ref, denominator_ref, out):
        me = lax.axis_index("pair")
        total = jnp.concatenate(
            [
                jnp.sum(parts_ref[pl.ds(NX * lax.rem(me - d + NPAIR, NPAIR), NX)].astype(f32), axis=0)
                for d, _ in SENDS
            ]
        )
        amplitude = (total / denominator_ref[...]).astype(bf16)
        out[...] = jnp.broadcast_to(amplitude[None], out.shape)

    return pl.pallas_call(
        kernel,
        out_shape=jax.ShapeDtypeStruct((NXZ, rows, TS), bf16),
        in_specs=[in_vmem] * 2,
        out_specs=in_vmem,
        compiler_params=pltpu.CompilerParams(vmem_limit_bytes=VMEM_LIMIT),
        name="amplitude_copies",
    )(parts, denominator)


def gamma_rows(blocks, parked, mine, theirs, scales):
    rows, width = blocks[0][0].shape
    counts = [len(blocks[n]) for n in HELD]

    def kernel(*refs):
        given = list(refs[: sum(counts)])
        block = []
        for count in counts:
            block.append(given[:count])
            given = given[count:]
        parked_ref, own, other, scale, out, matrix, held, arrived, sums = refs[sum(counts) :]
        fetches = []
        for k, name in enumerate(PARKED):
            block[HELD.index(name)] = [parked_ref.at[k * rows : (k + 1) * rows]]
        for k, name in enumerate(FETCHED):
            i = HELD.index(name)
            fetches.append(pltpu.make_async_copy(block[i][0], held.at[k], arrived.at[k]))
            block[i] = [held.at[k]]
        for fetch in fetches:
            fetch.start()
        core = lax.axis_index("core")
        even = lax.rem(lax.axis_index("pair"), 2) == 0
        for pair in range(0, len(ORDER), 2):
            for part, source in ((core, own), (1 - core, other)):
                place = pl.ds(pl.multiple_of(part * TS, TS), TS)
                both = source[:, pair * PIECE : (pair + 2) * PIECE].astype(f32)
                for k in (0, 1):
                    i = pair + k
                    q, transposed = ORDER[i]
                    held = jnp.where(even, HELD.index(held_name(q, 0)), HELD.index(held_name(q, 1)))
                    tiles = both[:, k * PIECE : (k + 1) * PIECE].reshape(2, TS, TS)
                    for h in (0, 1):
                        if transposed:
                            tile = tiles[h].T * scale[2 * i + h : 2 * i + h + 1]
                            matrix[held, h * TS : (h + 1) * TS, place] = tile.astype(bf16)
                        else:
                            tile = tiles[h] * scale[pl.ds(2 * i + part, 1)]
                            matrix[held, place, h * TS : (h + 1) * TS] = tile.astype(bf16)

        def product(indices, start):
            total = None
            for i in indices:
                part, offset = divmod(start, rows // len(block[i]))
                left = block[i][part][offset : offset + ROWS]
                term = jnp.dot(left, matrix[i], preferred_element_type=f32)
                total = term if total is None else total + term
            return total

        last = [i for i, name in enumerate(HELD) if name in FETCHED]
        for start in range(0, rows, ROWS):
            sums[start : start + ROWS] = product([i for i in range(len(HELD)) if i not in last], start)
        for fetch in fetches:
            fetch.wait()
        for start in range(0, rows, ROWS):
            total = sums[start : start + ROWS] + product(last, start)
            out[start : start + ROWS] = total.astype(bf16)

    return pl.pallas_call(
        kernel,
        out_shape=jax.ShapeDtypeStruct((rows, width), bf16),
        in_specs=[anywhere if n in FETCHED else in_vmem for n in HELD for _ in blocks[n]]
        + [in_vmem] * 4,
        out_specs=in_vmem,
        scratch_shapes=[
            pltpu.VMEM((len(HELD), WIDTH, WIDTH), bf16),
            pltpu.VMEM((len(FETCHED), rows, width), bf16),
            pltpu.SemaphoreType.DMA((len(FETCHED),)),
            pltpu.VMEM((rows, width), f32),
        ],
        compiler_params=pltpu.CompilerParams(vmem_limit_bytes=VMEM_LIMIT),
        name="gamma_rows",
    )(*[part for n in HELD for part in blocks[n]], parked, mine, theirs, scales)


def body(three_index, *energies):
    def swap_a(x):
        return lax.ppermute(x, "pair", SWAP_A)

    def swap_b(x):
        return lax.ppermute(x, "pair", SWAP_B)

    def swap_cores(x):
        return lax.ppermute(x, "core", SWAP_CORES)

    half = three_index.shape[0] // 2
    block = {0: [three_index]}
    block["A", 1] = [swap_a(three_index)]
    block["B", 1] = [swap_b(three_index[:half]), swap_b(three_index[half:])]
    block["B", 2] = [swap_b(block["A", 1][0])]
    block["A", 2] = [swap_a(part) for part in block["B", 1]]

    early, other_early = coulomb_pairs(block, EARLY)
    denominator, scales = tables(*energies)
    other_early, denominator, scales = lax.optimization_barrier((other_early, denominator, scales))
    got_early = swap_cores(other_early)
    late, other_late = coulomb_pairs(block, LATE)
    got_late = swap_cores(other_late)
    summed = sum_cores((early, late), (got_early, got_late))

    summed, b2, a2, a1, b1 = lax.optimization_barrier(
        (summed, block["B", 2], block["A", 2], block["A", 1], block["B", 1])
    )
    parked = jnp.concatenate(a1 + b1)
    a3, b3 = swap_a(b2[0]), swap_b(jnp.concatenate(a2))
    parts = lax.all_to_all(summed, "z", 0, 0)
    parts, parked = lax.optimization_barrier((parts, parked))
    parts = lax.all_to_all(sum_z(parts), ("pair", "x"), 0, 0)
    copies = amplitude_copies(parts, denominator)

    copies, a3, b3 = lax.optimization_barrier((copies, a3, b3))
    b4 = [swap_b(a3[:half]), swap_a(b3[half:])]
    mine = lax.all_to_all(copies, ("z", "x"), 0, 0)
    mine, b4 = lax.optimization_barrier((mine, b4))
    block.update({("A", 1): [], ("B", 1): [], ("B", 2): b2, ("A", 2): a2, ("A", 3): [a3], ("B", 3): [b3], ("B", 4): b4})
    return gamma_rows(block, parked, mine, swap_cores(mine), scales)


def solution(mesh):
    grid = Mesh(mesh.devices.reshape(NX, NZ, NCORE, NPAIR), AUX + ("pair",))
    placed = (P(AUX, "pair"), P(), P(), P(), P(), P())
    return jax.shard_map(
        body, mesh=grid, in_specs=placed, out_specs=P(AUX, "pair"), check_vma=False
    )
```

```python
import jax
import jax.numpy as jnp
from jax import lax
from jax.experimental import pallas as pl
from jax.experimental.pallas import tpu as pltpu
from jax.sharding import Mesh, PartitionSpec as P

TS = 128
VT = 157
NT = 16
NX, NZ, NCORE, NPAIR = 4, 8, 2, 8
NXZ = NX * NZ
AUX = ("x", "z", "core")
EARLY = ((0, 0), (0, 1), (-1, 1))
LATE = ((-1, 2), (-2, 2))
PAIRS = EARLY + LATE
WIDTH = 2 * TS
PIECE = WIDTH // NXZ
SENDS = ((0, (0, 1)), (1, (1, 2)), (-1, (2, 3)), (2, (3, 4)))
GETS = tuple((PAIRS[k][0] - d, PAIRS[k][1] - d) for d, pairs in SENDS for k in pairs)
ORDER = tuple((r, False) if c == 0 else (c, True) for r, c in GETS)
ROWS = 224
FETCHED = (("A", 3),)
VMEM_LIMIT = 12 * 1024 * 1024
bf16, f32 = jnp.bfloat16, jnp.float32
in_vmem = pl.BlockSpec(memory_space=pltpu.VMEM)
anywhere = pl.BlockSpec(memory_space=pl.ANY)
in_smem = pl.BlockSpec(memory_space=pltpu.SMEM)


SWAP_A = [(i, i ^ 1) for i in range(NPAIR)]
SWAP_B = [(i, (i + (-1 if i % 2 == 0 else 1)) % NPAIR) for i in range(NPAIR)]
SWAP_CORES = [(0, 1), (1, 0)]
HELD = (0, ("A", 1), ("B", 1), ("A", 2), ("B", 2), ("A", 3), ("B", 3), ("B", 4))


def held_name(relative, parity):
    if relative == 0:
        return 0
    if abs(relative) == 4:
        return ("B", 4)
    return ("A" if (relative > 0) == (parity == 0) else "B", abs(relative))


def tables(occupied_energy, virtual_energy, tile_occupied, tile_virtual, tile_exponent):
    def kernel(occupied, virtual, occupied_of, virtual_of, exponent, denominator, scales):
        me = lax.axis_index("pair")
        core = lax.axis_index("core")
        slot = lax.axis_index("z") * NX + lax.axis_index("x")
        half, first = slot // (NXZ // 2), (slot % (NXZ // 2)) * PIECE

        def tile_of(relative, part):
            return lax.rem(2 * (me + relative + NPAIR) + part, NT)

        def energy(tile):
            return virtual[pl.ds(virtual_of[tile], 1)] - occupied[occupied_of[tile]]

        def scale(tile):
            level = exponent[tile]
            return jnp.where(level == -1, 0.5, jnp.where(level == 1, 2.0, 1.0)).astype(f32)

        lane = lax.broadcasted_iota(jnp.int32, (PIECE, TS), 1)
        chosen = lane == first + lax.broadcasted_iota(jnp.int32, (PIECE, TS), 0)
        for k, (r, c) in enumerate(PAIRS):
            row, column = tile_of(r, core), tile_of(c, half)
            of_row = jnp.sum(jnp.where(chosen, energy(row), 0.0), axis=1, keepdims=True)
            level = jnp.full((PIECE, TS), scale(row) * scale(column), f32)
            denominator[k * PIECE : (k + 1) * PIECE] = (of_row + energy(column)) / level
        for i, (q, _) in enumerate(ORDER):
            for part in (0, 1):
                n = 2 * i + part
                scales[n : n + 1] = jnp.full((1, TS), scale(tile_of(q, part)), f32)

    return pl.pallas_call(
        kernel,
        out_shape=(
            jax.ShapeDtypeStruct((len(PAIRS) * PIECE, TS), f32),
            jax.ShapeDtypeStruct((2 * len(ORDER), TS), f32),
        ),
        in_specs=[in_smem, in_vmem, in_smem, in_smem, in_smem],
        out_specs=(in_vmem, in_vmem),
        compiler_params=pltpu.CompilerParams(vmem_limit_bytes=VMEM_LIMIT),
        name="tables",
    )(occupied_energy, virtual_energy.reshape(VT, TS), tile_occupied, tile_virtual, tile_exponent)


def coulomb_pairs(blocks, pairs):
    names = [
        n for n in HELD if n in {held_name(d, parity) for pair in pairs for d in pair for parity in (0, 1)}
    ]
    counts = [len(blocks[n]) for n in names]
    rows = sum(part.shape[0] for part in blocks[names[0]])
    most = max(counts)
    height = rows // most

    def kernel(*refs):
        parts = {}
        given = list(refs[: sum(counts)])
        for n, count in zip(names, counts):
            mine, given = given[:count], given[count:]
            parts[n] = mine if count == most else [
                mine[0].at[i * height : (i + 1) * height] for i in range(most)
            ]
        own, other = refs[sum(counts) :]
        core = lax.axis_index("core")
        me = lax.axis_index("pair")
        for parity in (0, 1):

            @pl.when(lax.rem(me, 2) == parity)
            def _(parity=parity):
                for k, (r, c) in enumerate(pairs):
                    for out, part in ((own, core), (other, 1 - core)):
                        place = pl.ds(pl.multiple_of(part * TS, TS), TS)
                        total = None
                        for left, right in zip(parts[held_name(r, parity)], parts[held_name(c, parity)]):
                            term = lax.dot_general(
                                left[:, place], right[...], (((0,), (0,)), ((), ())), preferred_element_type=f32
                            )
                            total = term if total is None else total + term
                        for h in (0, 1):
                            out[k, h] = total[:, h * TS : (h + 1) * TS].astype(out.dtype)

    shape = (len(pairs), 2, TS, TS)
    out_shape = [jax.ShapeDtypeStruct(shape, f32), jax.ShapeDtypeStruct(shape, bf16)]
    return pl.pallas_call(
        kernel,
        out_shape=out_shape,
        in_specs=[in_vmem] * sum(counts),
        out_specs=[in_vmem] * len(out_shape),
        compiler_params=pltpu.CompilerParams(vmem_limit_bytes=VMEM_LIMIT),
        name="coulomb_pairs",
    )(*[part for n in names for part in blocks[n]])


def sum_cores(own, received):
    count = sum(a.shape[0] for a in own)

    def kernel(*refs):
        parts = []
        for mine, theirs in zip(refs[: len(own)], refs[len(own) : -1]):
            total = (mine[...] + theirs[...].astype(f32)).reshape(-1, NXZ, PIECE, TS)
            parts += [total[k] for k in range(total.shape[0])]
        refs[-1][...] = jnp.concatenate(parts, axis=1).astype(bf16)

    return pl.pallas_call(
        kernel,
        out_shape=jax.ShapeDtypeStruct((NXZ, count * PIECE, TS), bf16),
        in_specs=[in_vmem] * (2 * len(own)),
        out_specs=in_vmem,
        compiler_params=pltpu.CompilerParams(vmem_limit_bytes=VMEM_LIMIT),
        name="sum_cores",
    )(*own, *received)


def amplitude_sends(parts, denominator):
    def kernel(parts_ref, denominator_ref, out):
        me = lax.axis_index("pair")
        total = jnp.sum(parts_ref[...].astype(f32), axis=0) / denominator_ref[...]
        out[...] = jnp.zeros_like(out)
        for d, (first, second) in SENDS:
            both = total[first * PIECE : (second + 1) * PIECE]
            out[lax.rem(me + d + NPAIR, NPAIR)] = both.astype(bf16)

    return pl.pallas_call(
        kernel,
        out_shape=jax.ShapeDtypeStruct((NPAIR, 2 * PIECE, TS), bf16),
        in_specs=[in_vmem] * 2,
        out_specs=in_vmem,
        compiler_params=pltpu.CompilerParams(vmem_limit_bytes=VMEM_LIMIT),
        name="amplitude_sends",
    )(parts, denominator)


def amplitude_copies(received):
    rows = len(GETS) * PIECE

    def kernel(received_ref, out):
        me = lax.axis_index("pair")
        pieces = [received_ref[lax.rem(me - d + NPAIR, NPAIR)] for d, _ in SENDS]
        out[...] = jnp.broadcast_to(jnp.concatenate(pieces)[None], out.shape)

    return pl.pallas_call(
        kernel,
        out_shape=jax.ShapeDtypeStruct((NXZ, rows, TS), bf16),
        in_specs=[in_vmem],
        out_specs=in_vmem,
        compiler_params=pltpu.CompilerParams(vmem_limit_bytes=VMEM_LIMIT),
        name="amplitude_copies",
    )(received)


def gamma_rows(blocks, mine, theirs, scales):
    rows, width = blocks[0][0].shape
    counts = [len(blocks[n]) for n in HELD]

    def kernel(*refs):
        given = list(refs[: sum(counts)])
        block = []
        for count in counts:
            block.append(given[:count])
            given = given[count:]
        own, other, scale, out, matrix, held, arrived, sums = refs[sum(counts) :]
        fetches = []
        for k, name in enumerate(FETCHED):
            i = HELD.index(name)
            fetches.append(pltpu.make_async_copy(block[i][0], held.at[k], arrived.at[k]))
            block[i] = [held.at[k]]
        for fetch in fetches:
            fetch.start()
        core = lax.axis_index("core")
        even = lax.rem(lax.axis_index("pair"), 2) == 0
        for pair in range(0, len(ORDER), 2):
            for part, source in ((core, own), (1 - core, other)):
                place = pl.ds(pl.multiple_of(part * TS, TS), TS)
                both = source[:, pair * PIECE : (pair + 2) * PIECE].astype(f32)
                for k in (0, 1):
                    i = pair + k
                    q, transposed = ORDER[i]
                    held = jnp.where(even, HELD.index(held_name(q, 0)), HELD.index(held_name(q, 1)))
                    tiles = both[:, k * PIECE : (k + 1) * PIECE].reshape(2, TS, TS)
                    for h in (0, 1):
                        if transposed:
                            tile = tiles[h].T * scale[2 * i + h : 2 * i + h + 1]
                            matrix[held, h * TS : (h + 1) * TS, place] = tile.astype(bf16)
                        else:
                            tile = tiles[h] * scale[pl.ds(2 * i + part, 1)]
                            matrix[held, place, h * TS : (h + 1) * TS] = tile.astype(bf16)

        def product(indices, start):
            total = None
            for i in indices:
                part, offset = divmod(start, rows // len(block[i]))
                left = block[i][part][offset : offset + ROWS]
                term = jnp.dot(left, matrix[i], preferred_element_type=f32)
                total = term if total is None else total + term
            return total

        last = [i for i, name in enumerate(HELD) if name in FETCHED]
        for start in range(0, rows, ROWS):
            sums[start : start + ROWS] = product([i for i in range(len(HELD)) if i not in last], start)
        for fetch in fetches:
            fetch.wait()
        for start in range(0, rows, ROWS):
            total = sums[start : start + ROWS] + product(last, start)
            out[start : start + ROWS] = total.astype(bf16)

    return pl.pallas_call(
        kernel,
        out_shape=jax.ShapeDtypeStruct((rows, width), bf16),
        in_specs=[anywhere if n in FETCHED else in_vmem for n in HELD for _ in blocks[n]]
        + [in_vmem] * 3,
        out_specs=in_vmem,
        scratch_shapes=[
            pltpu.VMEM((len(HELD), WIDTH, WIDTH), bf16),
            pltpu.VMEM((len(FETCHED), rows, width), bf16),
            pltpu.SemaphoreType.DMA((len(FETCHED),)),
            pltpu.VMEM((rows, width), f32),
        ],
        compiler_params=pltpu.CompilerParams(vmem_limit_bytes=VMEM_LIMIT),
        name="gamma_rows",
    )(*[part for n in HELD for part in blocks[n]], mine, theirs, scales)


def body(three_index, *energies):
    def swap_a(x):
        return lax.ppermute(x, "pair", SWAP_A)

    def swap_b(x):
        return lax.ppermute(x, "pair", SWAP_B)

    def swap_cores(x):
        return lax.ppermute(x, "core", SWAP_CORES)

    half = three_index.shape[0] // 2
    block = {0: [three_index]}
    block["A", 1] = [swap_a(three_index)]
    block["B", 1] = [swap_b(three_index[:half]), swap_b(three_index[half:])]
    block["B", 2] = [swap_b(block["A", 1][0])]
    block["A", 2] = [swap_a(part) for part in block["B", 1]]

    early, other_early = coulomb_pairs(block, EARLY)
    denominator, scales = tables(*energies)
    other_early, denominator, scales = lax.optimization_barrier((other_early, denominator, scales))
    got_early = swap_cores(other_early)
    late, other_late = coulomb_pairs(block, LATE)
    got_late = swap_cores(other_late)
    summed = sum_cores((early, late), (got_early, got_late))

    summed, b2, a2 = lax.optimization_barrier((summed, block["B", 2], block["A", 2]))
    a3, b3 = swap_a(b2[0]), swap_b(jnp.concatenate(a2))
    parts = lax.all_to_all(summed, ("z", "x"), 0, 0)
    received = lax.all_to_all(amplitude_sends(parts, denominator), "pair", 0, 0)
    copies = amplitude_copies(received)

    copies, a3, b3 = lax.optimization_barrier((copies, a3, b3))
    b4 = [swap_b(a3[:half]), swap_a(b3[half:])]
    mine = lax.all_to_all(copies, ("z", "x"), 0, 0)
    mine, b4 = lax.optimization_barrier((mine, b4))
    block.update({("B", 2): b2, ("A", 2): a2, ("A", 3): [a3], ("B", 3): [b3], ("B", 4): b4})
    return gamma_rows(block, mine, swap_cores(mine), scales)


def solution(mesh):
    grid = Mesh(mesh.devices.reshape(NX, NZ, NCORE, NPAIR), AUX + ("pair",))
    placed = (P(AUX, "pair"), P(), P(), P(), P(), P())
    return jax.shard_map(
        body, mesh=grid, in_specs=placed, out_specs=P(AUX, "pair"), check_vma=False
    )
```

```python
import jax
import jax.numpy as jnp
from jax import lax
from jax.experimental import pallas as pl
from jax.experimental.pallas import tpu as pltpu
from jax.sharding import Mesh, PartitionSpec as P

TS = 128
VT = 157
NT = 16
NX, NZ, NCORE, NPAIR = 4, 8, 2, 8
NXZ = NX * NZ
AUX = ("x", "z", "core")
EARLY = ((0, 0), (0, 1), (-1, 1))
LATE = ((-1, 2), (-2, 2))
PAIRS = EARLY + LATE
WIDTH = 2 * TS
PIECE = WIDTH // NXZ
SENDS = ((0, (0, 1)), (1, (1, 2)), (-1, (2, 3)), (2, (3, 4)))
GETS = tuple((PAIRS[k][0] - d, PAIRS[k][1] - d) for d, pairs in SENDS for k in pairs)
ORDER = tuple((r, False) if c == 0 else (c, True) for r, c in GETS)
ROWS = 224
VMEM_LIMIT = 12 * 1024 * 1024
bf16, f32 = jnp.bfloat16, jnp.float32
in_vmem = pl.BlockSpec(memory_space=pltpu.VMEM)
anywhere = pl.BlockSpec(memory_space=pl.ANY)
in_smem = pl.BlockSpec(memory_space=pltpu.SMEM)


SWAP_A = [(i, i ^ 1) for i in range(NPAIR)]
SWAP_B = [(i, (i + (-1 if i % 2 == 0 else 1)) % NPAIR) for i in range(NPAIR)]
SWAP_CORES = [(0, 1), (1, 0)]
HELD = (0, ("A", 1), ("B", 1), ("A", 2), ("B", 2), ("A", 3), ("B", 3), ("B", 4))


def held_name(relative, parity):
    if relative == 0:
        return 0
    if abs(relative) == 4:
        return ("B", 4)
    return ("A" if (relative > 0) == (parity == 0) else "B", abs(relative))


def tables(occupied_energy, virtual_energy, tile_occupied, tile_virtual, tile_exponent):
    def kernel(occupied, virtual, occupied_of, virtual_of, exponent, denominator, scales):
        me = lax.axis_index("pair")
        core = lax.axis_index("core")
        slot = lax.axis_index("z") * NX + lax.axis_index("x")
        half, first = slot // (NXZ // 2), (slot % (NXZ // 2)) * PIECE

        def tile_of(relative, part):
            return lax.rem(2 * (me + relative + NPAIR) + part, NT)

        def energy(tile):
            return virtual[pl.ds(virtual_of[tile], 1)] - occupied[occupied_of[tile]]

        def scale(tile):
            level = exponent[tile]
            return jnp.where(level == -1, 0.5, jnp.where(level == 1, 2.0, 1.0)).astype(f32)

        lane = lax.broadcasted_iota(jnp.int32, (PIECE, TS), 1)
        chosen = lane == first + lax.broadcasted_iota(jnp.int32, (PIECE, TS), 0)
        for k, (r, c) in enumerate(PAIRS):
            row, column = tile_of(r, core), tile_of(c, half)
            of_row = jnp.sum(jnp.where(chosen, energy(row), 0.0), axis=1, keepdims=True)
            level = jnp.full((PIECE, TS), scale(row) * scale(column), f32)
            denominator[k * PIECE : (k + 1) * PIECE] = (of_row + energy(column)) / level
        for i, (q, _) in enumerate(ORDER):
            for part in (0, 1):
                n = 2 * i + part
                scales[n : n + 1] = jnp.full((1, TS), scale(tile_of(q, part)), f32)

    return pl.pallas_call(
        kernel,
        out_shape=(
            jax.ShapeDtypeStruct((len(PAIRS) * PIECE, TS), f32),
            jax.ShapeDtypeStruct((2 * len(ORDER), TS), f32),
        ),
        in_specs=[in_smem, in_vmem, in_smem, in_smem, in_smem],
        out_specs=(in_vmem, in_vmem),
        compiler_params=pltpu.CompilerParams(vmem_limit_bytes=VMEM_LIMIT),
        name="tables",
    )(occupied_energy, virtual_energy.reshape(VT, TS), tile_occupied, tile_virtual, tile_exponent)


def coulomb_pairs(blocks, pairs):
    names = [
        n for n in HELD if n in {held_name(d, parity) for pair in pairs for d in pair for parity in (0, 1)}
    ]
    counts = [len(blocks[n]) for n in names]
    rows = sum(part.shape[0] for part in blocks[names[0]])
    most = max(counts)
    height = rows // most

    def kernel(*refs):
        parts = {}
        given = list(refs[: sum(counts)])
        for n, count in zip(names, counts):
            mine, given = given[:count], given[count:]
            parts[n] = mine if count == most else [
                mine[0].at[i * height : (i + 1) * height] for i in range(most)
            ]
        own, other = refs[sum(counts) :]
        core = lax.axis_index("core")
        me = lax.axis_index("pair")
        for parity in (0, 1):

            @pl.when(lax.rem(me, 2) == parity)
            def _(parity=parity):
                for k, (r, c) in enumerate(pairs):
                    for out, part in ((own, core), (other, 1 - core)):
                        place = pl.ds(pl.multiple_of(part * TS, TS), TS)
                        total = None
                        for left, right in zip(parts[held_name(r, parity)], parts[held_name(c, parity)]):
                            term = lax.dot_general(
                                left[:, place], right[...], (((0,), (0,)), ((), ())), preferred_element_type=f32
                            )
                            total = term if total is None else total + term
                        for h in (0, 1):
                            out[k, h] = total[:, h * TS : (h + 1) * TS].astype(out.dtype)

    shape = (len(pairs), 2, TS, TS)
    out_shape = [jax.ShapeDtypeStruct(shape, f32), jax.ShapeDtypeStruct(shape, bf16)]
    return pl.pallas_call(
        kernel,
        out_shape=out_shape,
        in_specs=[in_vmem] * sum(counts),
        out_specs=[in_vmem] * len(out_shape),
        compiler_params=pltpu.CompilerParams(vmem_limit_bytes=VMEM_LIMIT),
        name="coulomb_pairs",
    )(*[part for n in names for part in blocks[n]])


def sum_cores(own, received):
    count = sum(a.shape[0] for a in own)

    def kernel(*refs):
        parts = []
        for mine, theirs in zip(refs[: len(own)], refs[len(own) : -1]):
            total = (mine[...] + theirs[...].astype(f32)).reshape(-1, NXZ, PIECE, TS)
            parts += [total[k] for k in range(total.shape[0])]
        refs[-1][...] = jnp.concatenate(parts, axis=1).astype(bf16)

    return pl.pallas_call(
        kernel,
        out_shape=jax.ShapeDtypeStruct((NXZ, count * PIECE, TS), bf16),
        in_specs=[in_vmem] * (2 * len(own)),
        out_specs=in_vmem,
        compiler_params=pltpu.CompilerParams(vmem_limit_bytes=VMEM_LIMIT),
        name="sum_cores",
    )(*own, *received)


def amplitude_sends(parts, denominator):
    def kernel(parts_ref, denominator_ref, out):
        me = lax.axis_index("pair")
        total = jnp.sum(parts_ref[...].astype(f32), axis=0) / denominator_ref[...]
        out[...] = jnp.zeros_like(out)
        for d, (first, second) in SENDS:
            both = total[first * PIECE : (second + 1) * PIECE]
            out[lax.rem(me + d + NPAIR, NPAIR)] = both.astype(bf16)

    return pl.pallas_call(
        kernel,
        out_shape=jax.ShapeDtypeStruct((NPAIR, 2 * PIECE, TS), bf16),
        in_specs=[in_vmem] * 2,
        out_specs=in_vmem,
        compiler_params=pltpu.CompilerParams(vmem_limit_bytes=VMEM_LIMIT),
        name="amplitude_sends",
    )(parts, denominator)


def amplitude_copies(received):
    rows = len(GETS) * PIECE

    def kernel(received_ref, out):
        me = lax.axis_index("pair")
        pieces = [received_ref[lax.rem(me - d + NPAIR, NPAIR)] for d, _ in SENDS]
        out[...] = jnp.broadcast_to(jnp.concatenate(pieces)[None], out.shape)

    return pl.pallas_call(
        kernel,
        out_shape=jax.ShapeDtypeStruct((NXZ, rows, TS), bf16),
        in_specs=[in_vmem],
        out_specs=in_vmem,
        compiler_params=pltpu.CompilerParams(vmem_limit_bytes=VMEM_LIMIT),
        name="amplitude_copies",
    )(received)


def lay_out(source, part, scale, matrix):
    even = lax.rem(lax.axis_index("pair"), 2) == 0
    place = pl.ds(pl.multiple_of(part * TS, TS), TS)
    for pair in range(0, len(ORDER), 2):
        both = source[:, pair * PIECE : (pair + 2) * PIECE].astype(f32)
        for k in (0, 1):
            i = pair + k
            q, transposed = ORDER[i]
            held = jnp.where(even, HELD.index(held_name(q, 0)), HELD.index(held_name(q, 1)))
            tiles = both[:, k * PIECE : (k + 1) * PIECE].reshape(2, TS, TS)
            for h in (0, 1):
                if transposed:
                    tile = tiles[h].T * scale[2 * i + h : 2 * i + h + 1]
                    matrix[held, h * TS : (h + 1) * TS, place] = tile.astype(bf16)
                else:
                    tile = tiles[h] * scale[pl.ds(2 * i + part, 1)]
                    matrix[held, place, h * TS : (h + 1) * TS] = tile.astype(bf16)


def own_half(mine, scales, far):
    def kernel(mine_ref, scale, far_ref, matrix, near, arrived):
        fetch = pltpu.make_async_copy(far_ref, near, arrived)
        fetch.start()
        lay_out(mine_ref, lax.axis_index("core"), scale, matrix)
        fetch.wait()

    return pl.pallas_call(
        kernel,
        out_shape=(
            jax.ShapeDtypeStruct((len(HELD), WIDTH, WIDTH), bf16),
            jax.ShapeDtypeStruct(far.shape, far.dtype),
        ),
        in_specs=[in_vmem, in_vmem, anywhere],
        out_specs=(in_vmem, in_vmem),
        scratch_shapes=[pltpu.SemaphoreType.DMA],
        compiler_params=pltpu.CompilerParams(vmem_limit_bytes=VMEM_LIMIT),
        name="own_half",
    )(mine, scales, far)


def gamma_rows(blocks, half, theirs, scales):
    rows, width = blocks[0][0].shape
    counts = [len(blocks[n]) for n in HELD]

    def kernel(*refs):
        given = list(refs[: sum(counts)])
        block = []
        for count in counts:
            block.append(given[:count])
            given = given[count:]
        _, other, scale, out, matrix = refs[sum(counts) :]
        lay_out(other, 1 - lax.axis_index("core"), scale, matrix)
        for start in range(0, rows, ROWS):
            total = None
            for i, parts in enumerate(block):
                part, offset = divmod(start, rows // len(parts))
                left = parts[part][offset : offset + ROWS]
                term = jnp.dot(left, matrix[i], preferred_element_type=f32)
                total = term if total is None else total + term
            out[start : start + ROWS] = total.astype(bf16)

    return pl.pallas_call(
        kernel,
        out_shape=(
            jax.ShapeDtypeStruct((rows, width), bf16),
            jax.ShapeDtypeStruct(half.shape, half.dtype),
        ),
        in_specs=[in_vmem] * (sum(counts) + 3),
        out_specs=(in_vmem, in_vmem),
        input_output_aliases={sum(counts): 1},
        compiler_params=pltpu.CompilerParams(vmem_limit_bytes=VMEM_LIMIT),
        name="gamma_rows",
    )(*[part for n in HELD for part in blocks[n]], half, theirs, scales)[0]


def body(three_index, *energies):
    def swap_a(x):
        return lax.ppermute(x, "pair", SWAP_A)

    def swap_b(x):
        return lax.ppermute(x, "pair", SWAP_B)

    def swap_cores(x):
        return lax.ppermute(x, "core", SWAP_CORES)

    half = three_index.shape[0] // 2
    block = {0: [three_index]}
    block["A", 1] = [swap_a(three_index)]
    block["B", 1] = [swap_b(three_index[:half]), swap_b(three_index[half:])]
    block["B", 2] = [swap_b(block["A", 1][0])]
    block["A", 2] = [swap_a(part) for part in block["B", 1]]

    early, other_early = coulomb_pairs(block, EARLY)
    denominator, scales = tables(*energies)
    other_early, denominator, scales = lax.optimization_barrier((other_early, denominator, scales))
    got_early = swap_cores(other_early)
    late, other_late = coulomb_pairs(block, LATE)
    got_late = swap_cores(other_late)
    summed = sum_cores((early, late), (got_early, got_late))

    summed, b2, a2 = lax.optimization_barrier((summed, block["B", 2], block["A", 2]))
    a3, b3 = swap_a(b2[0]), swap_b(jnp.concatenate(a2))
    parts = lax.all_to_all(summed, ("z", "x"), 0, 0)
    received = lax.all_to_all(amplitude_sends(parts, denominator), "pair", 0, 0)
    copies = amplitude_copies(received)

    copies, a3, b3 = lax.optimization_barrier((copies, a3, b3))
    b4 = [swap_b(a3[:half]), swap_a(b3[half:])]
    mine = lax.all_to_all(copies, ("z", "x"), 0, 0)
    mine, b4 = lax.optimization_barrier((mine, b4))
    block.update({("B", 2): b2, ("A", 2): a2, ("A", 3): [a3], ("B", 3): [b3], ("B", 4): b4})
    theirs = swap_cores(mine)
    half, a3 = own_half(mine, scales, a3)
    block["A", 3] = [a3]
    return gamma_rows(block, half, theirs, scales)


def solution(mesh):
    grid = Mesh(mesh.devices.reshape(NX, NZ, NCORE, NPAIR), AUX + ("pair",))
    placed = (P(AUX, "pair"), P(), P(), P(), P(), P())
    return jax.shard_map(
        body, mesh=grid, in_specs=placed, out_specs=P(AUX, "pair"), check_vma=False
    )
```

```python
import jax
import jax.numpy as jnp
from jax import lax
from jax.experimental import pallas as pl
from jax.experimental.pallas import tpu as pltpu
from jax.sharding import Mesh, PartitionSpec as P

TS = 128
VT = 157
NT = 16
NX, NZ, NCORE, NPAIR = 4, 8, 2, 8
NXZ = NX * NZ
AUX = ("x", "z", "core")
EARLY = ((0, 0), (0, 1), (-1, 1))
LATE = ((-1, 2), (-2, 2))
PAIRS = EARLY + LATE
WIDTH = 2 * TS
PIECE = WIDTH // NXZ
SENDS = ((0, (0, 1)), (1, (1, 2)), (-1, (2, 3)), (2, (3, 4)))
GETS = tuple((PAIRS[k][0] - d, PAIRS[k][1] - d) for d, pairs in SENDS for k in pairs)
ORDER = tuple((r, False) if c == 0 else (c, True) for r, c in GETS)
ROWS = 224
VMEM_LIMIT = 12 * 1024 * 1024
bf16, f32 = jnp.bfloat16, jnp.float32
in_vmem = pl.BlockSpec(memory_space=pltpu.VMEM)
anywhere = pl.BlockSpec(memory_space=pl.ANY)
in_smem = pl.BlockSpec(memory_space=pltpu.SMEM)


SWAP_A = [(i, i ^ 1) for i in range(NPAIR)]
SWAP_B = [(i, (i + (-1 if i % 2 == 0 else 1)) % NPAIR) for i in range(NPAIR)]
SWAP_CORES = [(0, 1), (1, 0)]
HELD = (0, ("A", 1), ("B", 1), ("A", 2), ("B", 2), ("A", 3), ("B", 3), ("B", 4))


def held_name(relative, parity):
    if relative == 0:
        return 0
    if abs(relative) == 4:
        return ("B", 4)
    return ("A" if (relative > 0) == (parity == 0) else "B", abs(relative))


def tables(occupied_energy, virtual_energy, tile_occupied, tile_virtual, tile_exponent):
    def kernel(occupied, virtual, occupied_of, virtual_of, exponent, denominator, scales):
        me = lax.axis_index("pair")
        core = lax.axis_index("core")
        slot = lax.axis_index("z") * NX + lax.axis_index("x")
        half, first = slot // (NXZ // 2), (slot % (NXZ // 2)) * PIECE

        def tile_of(relative, part):
            return lax.rem(2 * (me + relative + NPAIR) + part, NT)

        def energy(tile):
            return virtual[pl.ds(virtual_of[tile], 1)] - occupied[occupied_of[tile]]

        def scale(tile):
            level = exponent[tile]
            return jnp.where(level == -1, 0.5, jnp.where(level == 1, 2.0, 1.0)).astype(f32)

        lane = lax.broadcasted_iota(jnp.int32, (PIECE, TS), 1)
        chosen = lane == first + lax.broadcasted_iota(jnp.int32, (PIECE, TS), 0)
        for k, (r, c) in enumerate(PAIRS):
            row, column = tile_of(r, core), tile_of(c, half)
            of_row = jnp.sum(jnp.where(chosen, energy(row), 0.0), axis=1, keepdims=True)
            level = jnp.full((PIECE, TS), scale(row) * scale(column), f32)
            denominator[k * PIECE : (k + 1) * PIECE] = (of_row + energy(column)) / level
        for i, (q, _) in enumerate(ORDER):
            for part in (0, 1):
                n = 2 * i + part
                scales[n : n + 1] = jnp.full((1, TS), scale(tile_of(q, part)), f32)

    return pl.pallas_call(
        kernel,
        out_shape=(
            jax.ShapeDtypeStruct((len(PAIRS) * PIECE, TS), f32),
            jax.ShapeDtypeStruct((2 * len(ORDER), TS), f32),
        ),
        in_specs=[in_smem, in_vmem, in_smem, in_smem, in_smem],
        out_specs=(in_vmem, in_vmem),
        compiler_params=pltpu.CompilerParams(vmem_limit_bytes=VMEM_LIMIT),
        name="tables",
    )(occupied_energy, virtual_energy.reshape(VT, TS), tile_occupied, tile_virtual, tile_exponent)


def coulomb_pairs(blocks, pairs):
    names = [
        n for n in HELD if n in {held_name(d, parity) for pair in pairs for d in pair for parity in (0, 1)}
    ]
    counts = [len(blocks[n]) for n in names]
    rows = sum(part.shape[0] for part in blocks[names[0]])
    most = max(counts)
    height = rows // most

    def kernel(*refs):
        parts = {}
        given = list(refs[: sum(counts)])
        for n, count in zip(names, counts):
            mine, given = given[:count], given[count:]
            parts[n] = mine if count == most else [
                mine[0].at[i * height : (i + 1) * height] for i in range(most)
            ]
        own, other = refs[sum(counts) :]
        core = lax.axis_index("core")
        me = lax.axis_index("pair")
        for parity in (0, 1):

            @pl.when(lax.rem(me, 2) == parity)
            def _(parity=parity):
                for k, (r, c) in enumerate(pairs):
                    for out, part in ((own, core), (other, 1 - core)):
                        place = pl.ds(pl.multiple_of(part * TS, TS), TS)
                        total = None
                        for left, right in zip(parts[held_name(r, parity)], parts[held_name(c, parity)]):
                            term = lax.dot_general(
                                left[:, place], right[...], (((0,), (0,)), ((), ())), preferred_element_type=f32
                            )
                            total = term if total is None else total + term
                        for h in (0, 1):
                            out[k, h] = total[:, h * TS : (h + 1) * TS].astype(out.dtype)

    shape = (len(pairs), 2, TS, TS)
    out_shape = [jax.ShapeDtypeStruct(shape, f32), jax.ShapeDtypeStruct(shape, bf16)]
    return pl.pallas_call(
        kernel,
        out_shape=out_shape,
        in_specs=[in_vmem] * sum(counts),
        out_specs=[in_vmem] * len(out_shape),
        compiler_params=pltpu.CompilerParams(vmem_limit_bytes=VMEM_LIMIT),
        name="coulomb_pairs",
    )(*[part for n in names for part in blocks[n]])


def sum_cores(own, received):
    count = sum(a.shape[0] for a in own)

    def kernel(*refs):
        parts = []
        for mine, theirs in zip(refs[: len(own)], refs[len(own) : -1]):
            total = (mine[...] + theirs[...].astype(f32)).reshape(-1, NXZ, PIECE, TS)
            parts += [total[k] for k in range(total.shape[0])]
        refs[-1][...] = jnp.concatenate(parts, axis=1).astype(bf16)

    return pl.pallas_call(
        kernel,
        out_shape=jax.ShapeDtypeStruct((NXZ, count * PIECE, TS), bf16),
        in_specs=[in_vmem] * (2 * len(own)),
        out_specs=in_vmem,
        compiler_params=pltpu.CompilerParams(vmem_limit_bytes=VMEM_LIMIT),
        name="sum_cores",
    )(*own, *received)


def amplitude_sends(parts, denominator):
    def kernel(parts_ref, denominator_ref, out):
        me = lax.axis_index("pair")
        total = jnp.sum(parts_ref[...].astype(f32), axis=0) / denominator_ref[...]
        out[...] = jnp.zeros_like(out)
        for d, (first, second) in SENDS:
            both = total[first * PIECE : (second + 1) * PIECE]
            out[lax.rem(me + d + NPAIR, NPAIR)] = both.astype(bf16)

    return pl.pallas_call(
        kernel,
        out_shape=jax.ShapeDtypeStruct((NPAIR, 2 * PIECE, TS), bf16),
        in_specs=[in_vmem] * 2,
        out_specs=in_vmem,
        compiler_params=pltpu.CompilerParams(vmem_limit_bytes=VMEM_LIMIT),
        name="amplitude_sends",
    )(parts, denominator)


def amplitude_copies(received):
    rows = len(GETS) * PIECE

    def kernel(received_ref, out):
        me = lax.axis_index("pair")
        pieces = [received_ref[lax.rem(me - d + NPAIR, NPAIR)] for d, _ in SENDS]
        out[...] = jnp.broadcast_to(jnp.concatenate(pieces)[None], out.shape)

    return pl.pallas_call(
        kernel,
        out_shape=jax.ShapeDtypeStruct((NXZ, rows, TS), bf16),
        in_specs=[in_vmem],
        out_specs=in_vmem,
        compiler_params=pltpu.CompilerParams(vmem_limit_bytes=VMEM_LIMIT),
        name="amplitude_copies",
    )(received)


def lay_out(source, part, scale, matrix):
    even = lax.rem(lax.axis_index("pair"), 2) == 0
    place = pl.ds(pl.multiple_of(part * TS, TS), TS)
    for pair in range(0, len(ORDER), 2):
        both = source[:, pair * PIECE : (pair + 2) * PIECE].astype(f32)
        for k in (0, 1):
            i = pair + k
            q, transposed = ORDER[i]
            held = jnp.where(even, HELD.index(held_name(q, 0)), HELD.index(held_name(q, 1)))
            tiles = both[:, k * PIECE : (k + 1) * PIECE].reshape(2, TS, TS)
            for h in (0, 1):
                if transposed:
                    tile = tiles[h].T * scale[2 * i + h : 2 * i + h + 1]
                    matrix[held, h * TS : (h + 1) * TS, place] = tile.astype(bf16)
                else:
                    tile = tiles[h] * scale[pl.ds(2 * i + part, 1)]
                    matrix[held, place, h * TS : (h + 1) * TS] = tile.astype(bf16)


def own_half(mine, scales, far):
    def kernel(mine_ref, scale, *refs):
        sources, (matrix, near, arrived) = refs[: len(far)], refs[len(far) :]
        fetches = []
        start = 0
        for k, source in enumerate(sources):
            place = near.at[start : start + source.shape[0]]
            fetches.append(pltpu.make_async_copy(source, place, arrived.at[k]))
            start += source.shape[0]
        for fetch in fetches:
            fetch.start()
        lay_out(mine_ref, lax.axis_index("core"), scale, matrix)
        for fetch in fetches:
            fetch.wait()

    rows = sum(part.shape[0] for part in far)
    return pl.pallas_call(
        kernel,
        out_shape=(
            jax.ShapeDtypeStruct((len(HELD), WIDTH, WIDTH), bf16),
            jax.ShapeDtypeStruct((rows, WIDTH), bf16),
        ),
        in_specs=[in_vmem, in_vmem] + [anywhere] * len(far),
        out_specs=(in_vmem, in_vmem),
        scratch_shapes=[pltpu.SemaphoreType.DMA((len(far),))],
        compiler_params=pltpu.CompilerParams(vmem_limit_bytes=VMEM_LIMIT),
        name="own_half",
    )(mine, scales, *far)


def gamma_rows(blocks, half, theirs, scales):
    rows, width = blocks[0][0].shape
    counts = [len(blocks[n]) for n in HELD]

    def kernel(*refs):
        given = list(refs[: sum(counts)])
        block = []
        for count in counts:
            block.append(given[:count])
            given = given[count:]
        _, other, scale, out, matrix = refs[sum(counts) :]
        lay_out(other, 1 - lax.axis_index("core"), scale, matrix)
        for start in range(0, rows, ROWS):
            total = None
            for i, parts in enumerate(block):
                part, offset = divmod(start, rows // len(parts))
                left = parts[part][offset : offset + ROWS]
                term = jnp.dot(left, matrix[i], preferred_element_type=f32)
                total = term if total is None else total + term
            out[start : start + ROWS] = total.astype(bf16)

    return pl.pallas_call(
        kernel,
        out_shape=(
            jax.ShapeDtypeStruct((rows, width), bf16),
            jax.ShapeDtypeStruct(half.shape, half.dtype),
        ),
        in_specs=[in_vmem] * (sum(counts) + 3),
        out_specs=(in_vmem, in_vmem),
        input_output_aliases={sum(counts): 1},
        compiler_params=pltpu.CompilerParams(vmem_limit_bytes=VMEM_LIMIT),
        name="gamma_rows",
    )(*[part for n in HELD for part in blocks[n]], half, theirs, scales)[0]


def body(three_index, *energies):
    def swap_a(x):
        return lax.ppermute(x, "pair", SWAP_A)

    def swap_b(x):
        return lax.ppermute(x, "pair", SWAP_B)

    def swap_cores(x):
        return lax.ppermute(x, "core", SWAP_CORES)

    half = three_index.shape[0] // 2
    block = {0: [three_index]}
    block["A", 1] = [swap_a(three_index)]
    block["B", 1] = [swap_b(three_index[:half]), swap_b(three_index[half:])]
    block["B", 2] = [swap_b(block["A", 1][0])]
    block["A", 2] = [swap_a(part) for part in block["B", 1]]

    early, other_early = coulomb_pairs(block, EARLY)
    denominator, scales = tables(*energies)
    other_early, denominator, scales = lax.optimization_barrier((other_early, denominator, scales))
    got_early = swap_cores(other_early)
    late, other_late = coulomb_pairs(block, LATE)
    got_late = swap_cores(other_late)
    summed = sum_cores((early, late), (got_early, got_late))

    summed, b2, a2 = lax.optimization_barrier((summed, block["B", 2], block["A", 2]))
    a3, b3 = swap_a(b2[0]), [swap_b(part) for part in a2]
    parts = lax.all_to_all(summed, ("z", "x"), 0, 0)
    received = lax.all_to_all(amplitude_sends(parts, denominator), "pair", 0, 0)
    copies = amplitude_copies(received)

    copies, a3, b3 = lax.optimization_barrier((copies, a3, b3))
    b4 = [swap_b(a3[:half]), swap_a(b3[1])]
    mine = lax.all_to_all(copies, ("z", "x"), 0, 0)
    mine, b4 = lax.optimization_barrier((mine, b4))
    block.update({("B", 2): b2, ("A", 2): a2, ("A", 3): [a3], ("B", 3): b3, ("B", 4): b4})
    theirs = swap_cores(mine)
    own, near = own_half(mine, scales, b3)
    block["B", 3] = [near]
    return gamma_rows(block, own, theirs, scales)


def solution(mesh):
    grid = Mesh(mesh.devices.reshape(NX, NZ, NCORE, NPAIR), AUX + ("pair",))
    placed = (P(AUX, "pair"), P(), P(), P(), P(), P())
    return jax.shard_map(
        body, mesh=grid, in_specs=placed, out_specs=P(AUX, "pair"), check_vma=False
    )
```

```python
import jax
import jax.numpy as jnp
from jax import lax
from jax.experimental import pallas as pl
from jax.experimental.pallas import tpu as pltpu
from jax.sharding import Mesh, PartitionSpec as P

TS = 128
VT = 157
NT = 16
NX, NZ, NCORE, NPAIR = 4, 8, 2, 8
NXZ = NX * NZ
AUX = ("x", "z", "core")
EARLY = ((0, 0), (0, 1), (-1, 1))
LATE = ((-1, 2), (-2, 2))
PAIRS = EARLY + LATE
WIDTH = 2 * TS
PIECE = WIDTH // NXZ
SENDS = ((0, (0, 1)), (1, (1, 2)), (-1, (2, 3)), (2, (3, 4)))
GETS = tuple((PAIRS[k][0] - d, PAIRS[k][1] - d) for d, pairs in SENDS for k in pairs)
ORDER = tuple((r, False) if c == 0 else (c, True) for r, c in GETS)
ROWS = 448
VMEM_LIMIT = 12 * 1024 * 1024
bf16, f32 = jnp.bfloat16, jnp.float32
in_vmem = pl.BlockSpec(memory_space=pltpu.VMEM)
anywhere = pl.BlockSpec(memory_space=pl.ANY)
in_smem = pl.BlockSpec(memory_space=pltpu.SMEM)


SWAP_A = [(i, i ^ 1) for i in range(NPAIR)]
SWAP_B = [(i, (i + (-1 if i % 2 == 0 else 1)) % NPAIR) for i in range(NPAIR)]
SWAP_CORES = [(0, 1), (1, 0)]
HELD = (0, ("A", 1), ("B", 1), ("A", 2), ("B", 2), ("A", 3), ("B", 3), ("B", 4))


def held_name(relative, parity):
    if relative == 0:
        return 0
    if abs(relative) == 4:
        return ("B", 4)
    return ("A" if (relative > 0) == (parity == 0) else "B", abs(relative))


def tables(occupied_energy, virtual_energy, tile_occupied, tile_virtual, tile_exponent):
    def kernel(occupied, virtual, occupied_of, virtual_of, exponent, denominator, scales):
        me = lax.axis_index("pair")
        core = lax.axis_index("core")
        slot = lax.axis_index("z") * NX + lax.axis_index("x")
        half, first = slot // (NXZ // 2), (slot % (NXZ // 2)) * PIECE

        def tile_of(relative, part):
            return lax.rem(2 * (me + relative + NPAIR) + part, NT)

        def energy(tile):
            return virtual[pl.ds(virtual_of[tile], 1)] - occupied[occupied_of[tile]]

        def scale(tile):
            level = exponent[tile]
            return jnp.where(level == -1, 0.5, jnp.where(level == 1, 2.0, 1.0)).astype(f32)

        lane = lax.broadcasted_iota(jnp.int32, (PIECE, TS), 1)
        chosen = lane == first + lax.broadcasted_iota(jnp.int32, (PIECE, TS), 0)
        for k, (r, c) in enumerate(PAIRS):
            row, column = tile_of(r, core), tile_of(c, half)
            of_row = jnp.sum(jnp.where(chosen, energy(row), 0.0), axis=1, keepdims=True)
            level = jnp.full((PIECE, TS), scale(row) * scale(column), f32)
            denominator[k * PIECE : (k + 1) * PIECE] = (of_row + energy(column)) / level
        for i, (q, _) in enumerate(ORDER):
            for part in (0, 1):
                n = 2 * i + part
                scales[n : n + 1] = jnp.full((1, TS), scale(tile_of(q, part)), f32)

    return pl.pallas_call(
        kernel,
        out_shape=(
            jax.ShapeDtypeStruct((len(PAIRS) * PIECE, TS), f32),
            jax.ShapeDtypeStruct((2 * len(ORDER), TS), f32),
        ),
        in_specs=[in_smem, in_vmem, in_smem, in_smem, in_smem],
        out_specs=(in_vmem, in_vmem),
        compiler_params=pltpu.CompilerParams(vmem_limit_bytes=VMEM_LIMIT),
        name="tables",
    )(occupied_energy, virtual_energy.reshape(VT, TS), tile_occupied, tile_virtual, tile_exponent)


def coulomb_pairs(blocks, pairs):
    names = [
        n for n in HELD if n in {held_name(d, parity) for pair in pairs for d in pair for parity in (0, 1)}
    ]
    counts = [len(blocks[n]) for n in names]
    rows = sum(part.shape[0] for part in blocks[names[0]])
    most = max(counts)
    height = rows // most

    def kernel(*refs):
        parts = {}
        given = list(refs[: sum(counts)])
        for n, count in zip(names, counts):
            mine, given = given[:count], given[count:]
            parts[n] = mine if count == most else [
                mine[0].at[i * height : (i + 1) * height] for i in range(most)
            ]
        own, other = refs[sum(counts) :]
        core = lax.axis_index("core")
        me = lax.axis_index("pair")
        for parity in (0, 1):

            @pl.when(lax.rem(me, 2) == parity)
            def _(parity=parity):
                for k, (r, c) in enumerate(pairs):
                    for out, part in ((own, core), (other, 1 - core)):
                        place = pl.ds(pl.multiple_of(part * TS, TS), TS)
                        total = None
                        for left, right in zip(parts[held_name(r, parity)], parts[held_name(c, parity)]):
                            term = lax.dot_general(
                                left[:, place], right[...], (((0,), (0,)), ((), ())), preferred_element_type=f32
                            )
                            total = term if total is None else total + term
                        for h in (0, 1):
                            out[k, h] = total[:, h * TS : (h + 1) * TS].astype(out.dtype)

    shape = (len(pairs), 2, TS, TS)
    out_shape = [jax.ShapeDtypeStruct(shape, f32), jax.ShapeDtypeStruct(shape, bf16)]
    return pl.pallas_call(
        kernel,
        out_shape=out_shape,
        in_specs=[in_vmem] * sum(counts),
        out_specs=[in_vmem] * len(out_shape),
        compiler_params=pltpu.CompilerParams(vmem_limit_bytes=VMEM_LIMIT),
        name="coulomb_pairs",
    )(*[part for n in names for part in blocks[n]])


def sum_cores(own, received):
    count = sum(a.shape[0] for a in own)

    def kernel(*refs):
        parts = []
        for mine, theirs in zip(refs[: len(own)], refs[len(own) : -1]):
            total = (mine[...] + theirs[...].astype(f32)).reshape(-1, NXZ, PIECE, TS)
            parts += [total[k] for k in range(total.shape[0])]
        refs[-1][...] = jnp.concatenate(parts, axis=1).astype(bf16)

    return pl.pallas_call(
        kernel,
        out_shape=jax.ShapeDtypeStruct((NXZ, count * PIECE, TS), bf16),
        in_specs=[in_vmem] * (2 * len(own)),
        out_specs=in_vmem,
        compiler_params=pltpu.CompilerParams(vmem_limit_bytes=VMEM_LIMIT),
        name="sum_cores",
    )(*own, *received)


def amplitude_sends(parts, denominator):
    def kernel(parts_ref, denominator_ref, out):
        me = lax.axis_index("pair")
        total = jnp.sum(parts_ref[...].astype(f32), axis=0) / denominator_ref[...]
        out[...] = jnp.zeros_like(out)
        for d, (first, second) in SENDS:
            both = total[first * PIECE : (second + 1) * PIECE]
            out[lax.rem(me + d + NPAIR, NPAIR)] = both.astype(bf16)

    return pl.pallas_call(
        kernel,
        out_shape=jax.ShapeDtypeStruct((NPAIR, 2 * PIECE, TS), bf16),
        in_specs=[in_vmem] * 2,
        out_specs=in_vmem,
        compiler_params=pltpu.CompilerParams(vmem_limit_bytes=VMEM_LIMIT),
        name="amplitude_sends",
    )(parts, denominator)


def amplitude_copies(received):
    rows = len(GETS) * PIECE

    def kernel(received_ref, out):
        me = lax.axis_index("pair")
        pieces = [received_ref[lax.rem(me - d + NPAIR, NPAIR)] for d, _ in SENDS]
        out[...] = jnp.broadcast_to(jnp.concatenate(pieces)[None], out.shape)

    return pl.pallas_call(
        kernel,
        out_shape=jax.ShapeDtypeStruct((NXZ, rows, TS), bf16),
        in_specs=[in_vmem],
        out_specs=in_vmem,
        compiler_params=pltpu.CompilerParams(vmem_limit_bytes=VMEM_LIMIT),
        name="amplitude_copies",
    )(received)


def lay_out(source, part, scale, matrix):
    even = lax.rem(lax.axis_index("pair"), 2) == 0
    place = pl.ds(pl.multiple_of(part * TS, TS), TS)
    for pair in range(0, len(ORDER), 2):
        both = source[:, pair * PIECE : (pair + 2) * PIECE].astype(f32)
        for k in (0, 1):
            i = pair + k
            q, transposed = ORDER[i]
            held = jnp.where(even, HELD.index(held_name(q, 0)), HELD.index(held_name(q, 1)))
            tiles = both[:, k * PIECE : (k + 1) * PIECE].reshape(2, TS, TS)
            for h in (0, 1):
                if transposed:
                    tile = tiles[h].T * scale[2 * i + h : 2 * i + h + 1]
                    matrix[held, h * TS : (h + 1) * TS, place] = tile.astype(bf16)
                else:
                    tile = tiles[h] * scale[pl.ds(2 * i + part, 1)]
                    matrix[held, place, h * TS : (h + 1) * TS] = tile.astype(bf16)


def own_half(mine, scales, far):
    def kernel(mine_ref, scale, *refs):
        sources, (matrix, near, arrived) = refs[: len(far)], refs[len(far) :]
        fetches = []
        start = 0
        for k, source in enumerate(sources):
            place = near.at[start : start + source.shape[0]]
            fetches.append(pltpu.make_async_copy(source, place, arrived.at[k]))
            start += source.shape[0]
        for fetch in fetches:
            fetch.start()
        lay_out(mine_ref, lax.axis_index("core"), scale, matrix)
        for fetch in fetches:
            fetch.wait()

    rows = sum(part.shape[0] for part in far)
    return pl.pallas_call(
        kernel,
        out_shape=(
            jax.ShapeDtypeStruct((len(HELD), WIDTH, WIDTH), bf16),
            jax.ShapeDtypeStruct((rows, WIDTH), bf16),
        ),
        in_specs=[in_vmem, in_vmem] + [anywhere] * len(far),
        out_specs=(in_vmem, in_vmem),
        scratch_shapes=[pltpu.SemaphoreType.DMA((len(far),))],
        compiler_params=pltpu.CompilerParams(vmem_limit_bytes=VMEM_LIMIT),
        name="own_half",
    )(mine, scales, *far)


def gamma_rows(blocks, half, theirs, scales):
    rows, width = blocks[0][0].shape
    counts = [len(blocks[n]) for n in HELD]

    def kernel(*refs):
        given = list(refs[: sum(counts)])
        block = []
        for count in counts:
            block.append(given[:count])
            given = given[count:]
        _, other, scale, out, matrix = refs[sum(counts) :]
        lay_out(other, 1 - lax.axis_index("core"), scale, matrix)
        for start in range(0, rows, ROWS):
            total = None
            for i, parts in enumerate(block):
                part, offset = divmod(start, rows // len(parts))
                left = parts[part][offset : offset + ROWS]
                term = jnp.dot(left, matrix[i], preferred_element_type=f32)
                total = term if total is None else total + term
            out[start : start + ROWS] = total.astype(bf16)

    return pl.pallas_call(
        kernel,
        out_shape=(
            jax.ShapeDtypeStruct((rows, width), bf16),
            jax.ShapeDtypeStruct(half.shape, half.dtype),
        ),
        in_specs=[in_vmem] * (sum(counts) + 3),
        out_specs=(in_vmem, in_vmem),
        input_output_aliases={sum(counts): 1},
        compiler_params=pltpu.CompilerParams(vmem_limit_bytes=VMEM_LIMIT),
        name="gamma_rows",
    )(*[part for n in HELD for part in blocks[n]], half, theirs, scales)[0]


def body(three_index, *energies):
    def swap_a(x):
        return lax.ppermute(x, "pair", SWAP_A)

    def swap_b(x):
        return lax.ppermute(x, "pair", SWAP_B)

    def swap_cores(x):
        return lax.ppermute(x, "core", SWAP_CORES)

    half = three_index.shape[0] // 2
    block = {0: [three_index]}
    block["A", 1] = [swap_a(three_index)]
    block["B", 1] = [swap_b(three_index[:half]), swap_b(three_index[half:])]
    block["B", 2] = [swap_b(block["A", 1][0])]
    block["A", 2] = [swap_a(part) for part in block["B", 1]]

    early, other_early = coulomb_pairs(block, EARLY)
    denominator, scales = tables(*energies)
    other_early, denominator, scales = lax.optimization_barrier((other_early, denominator, scales))
    got_early = swap_cores(other_early)
    late, other_late = coulomb_pairs(block, LATE)
    got_late = swap_cores(other_late)
    summed = sum_cores((early, late), (got_early, got_late))

    summed, b2, a2 = lax.optimization_barrier((summed, block["B", 2], block["A", 2]))
    a3, b3 = swap_a(b2[0]), [swap_b(part) for part in a2]
    parts = lax.all_to_all(summed, ("z", "x"), 0, 0)
    received = lax.all_to_all(amplitude_sends(parts, denominator), "pair", 0, 0)
    copies = amplitude_copies(received)

    copies, a3, b3 = lax.optimization_barrier((copies, a3, b3))
    b4 = [swap_b(a3[:half]), swap_a(b3[1])]
    mine = lax.all_to_all(copies, ("z", "x"), 0, 0)
    mine, b4 = lax.optimization_barrier((mine, b4))
    block.update({("B", 2): b2, ("A", 2): a2, ("A", 3): [a3], ("B", 3): b3, ("B", 4): b4})
    theirs = swap_cores(mine)
    own, near = own_half(mine, scales, b3)
    block["B", 3] = [near]
    return gamma_rows(block, own, theirs, scales)


def solution(mesh):
    grid = Mesh(mesh.devices.reshape(NX, NZ, NCORE, NPAIR), AUX + ("pair",))
    placed = (P(AUX, "pair"), P(), P(), P(), P(), P())
    return jax.shard_map(
        body, mesh=grid, in_specs=placed, out_specs=P(AUX, "pair"), check_vma=False
    )
```

```python
import jax
import jax.numpy as jnp
from jax import lax
from jax.experimental import pallas as pl
from jax.experimental.pallas import tpu as pltpu
from jax.sharding import Mesh, PartitionSpec as P

TS = 128
VT = 157
NT = 16
NX, NZ, NCORE, NPAIR = 4, 8, 2, 8
NXZ = NX * NZ
AUX = ("x", "z", "core")
EARLY = ((0, 0), (0, 1), (-1, 1))
LATE = ((-1, 2), (-2, 2))
PAIRS = EARLY + LATE
WIDTH = 2 * TS
PIECE = WIDTH // NXZ
SENDS = ((0, (0, 1)), (1, (1, 2)), (-1, (2, 3)), (2, (3, 4)))
GETS = tuple((PAIRS[k][0] - d, PAIRS[k][1] - d) for d, pairs in SENDS for k in pairs)
ORDER = tuple((r, False) if c == 0 else (c, True) for r, c in GETS)
ROWS = 224
VMEM_LIMIT = 12 * 1024 * 1024
bf16, f32 = jnp.bfloat16, jnp.float32
in_vmem = pl.BlockSpec(memory_space=pltpu.VMEM)
anywhere = pl.BlockSpec(memory_space=pl.ANY)
in_smem = pl.BlockSpec(memory_space=pltpu.SMEM)


SWAP_A = [(i, i ^ 1) for i in range(NPAIR)]
SWAP_B = [(i, (i + (-1 if i % 2 == 0 else 1)) % NPAIR) for i in range(NPAIR)]
SWAP_CORES = [(0, 1), (1, 0)]
HELD = (0, ("A", 1), ("B", 1), ("A", 2), ("B", 2), ("A", 3), ("B", 3), ("B", 4))


def held_name(relative, parity):
    if relative == 0:
        return 0
    if abs(relative) == 4:
        return ("B", 4)
    return ("A" if (relative > 0) == (parity == 0) else "B", abs(relative))


def tables(occupied_energy, virtual_energy, tile_occupied, tile_virtual, tile_exponent):
    def kernel(occupied, virtual, occupied_of, virtual_of, exponent, denominator, scales):
        me = lax.axis_index("pair")
        core = lax.axis_index("core")
        slot = lax.axis_index("z") * NX + lax.axis_index("x")
        half, first = slot // (NXZ // 2), (slot % (NXZ // 2)) * PIECE

        def tile_of(relative, part):
            return lax.rem(2 * (me + relative + NPAIR) + part, NT)

        def energy(tile):
            return virtual[pl.ds(virtual_of[tile], 1)] - occupied[occupied_of[tile]]

        def scale(tile):
            level = exponent[tile]
            return jnp.where(level == -1, 0.5, jnp.where(level == 1, 2.0, 1.0)).astype(f32)

        lane = lax.broadcasted_iota(jnp.int32, (PIECE, TS), 1)
        chosen = lane == first + lax.broadcasted_iota(jnp.int32, (PIECE, TS), 0)
        for k, (r, c) in enumerate(PAIRS):
            row, column = tile_of(r, core), tile_of(c, half)
            of_row = jnp.sum(jnp.where(chosen, energy(row), 0.0), axis=1, keepdims=True)
            level = jnp.full((PIECE, TS), scale(row) * scale(column), f32)
            denominator[k * PIECE : (k + 1) * PIECE] = (of_row + energy(column)) / level
        for i, (q, _) in enumerate(ORDER):
            for part in (0, 1):
                n = 2 * i + part
                scales[n : n + 1] = jnp.full((1, TS), scale(tile_of(q, part)), f32)

    return pl.pallas_call(
        kernel,
        out_shape=(
            jax.ShapeDtypeStruct((len(PAIRS) * PIECE, TS), f32),
            jax.ShapeDtypeStruct((2 * len(ORDER), TS), f32),
        ),
        in_specs=[in_smem, in_vmem, in_smem, in_smem, in_smem],
        out_specs=(in_vmem, in_vmem),
        compiler_params=pltpu.CompilerParams(vmem_limit_bytes=VMEM_LIMIT),
        name="tables",
    )(occupied_energy, virtual_energy.reshape(VT, TS), tile_occupied, tile_virtual, tile_exponent)


def coulomb_pairs(blocks, pairs):
    names = [
        n for n in HELD if n in {held_name(d, parity) for pair in pairs for d in pair for parity in (0, 1)}
    ]
    counts = [len(blocks[n]) for n in names]
    rows = sum(part.shape[0] for part in blocks[names[0]])
    most = max(counts)
    height = rows // most

    def kernel(*refs):
        parts = {}
        given = list(refs[: sum(counts)])
        for n, count in zip(names, counts):
            mine, given = given[:count], given[count:]
            parts[n] = mine if count == most else [
                mine[0].at[i * height : (i + 1) * height] for i in range(most)
            ]
        own, other = refs[sum(counts) :]
        core = lax.axis_index("core")
        me = lax.axis_index("pair")
        for parity in (0, 1):

            @pl.when(lax.rem(me, 2) == parity)
            def _(parity=parity):
                for k, (r, c) in enumerate(pairs):
                    for out, part in ((own, core), (other, 1 - core)):
                        place = pl.ds(pl.multiple_of(part * TS, TS), TS)
                        total = None
                        for left, right in zip(parts[held_name(r, parity)], parts[held_name(c, parity)]):
                            term = lax.dot_general(
                                left[:, place], right[...], (((0,), (0,)), ((), ())), preferred_element_type=f32
                            )
                            total = term if total is None else total + term
                        for h in (0, 1):
                            out[k, h] = total[:, h * TS : (h + 1) * TS].astype(out.dtype)

    shape = (len(pairs), 2, TS, TS)
    out_shape = [jax.ShapeDtypeStruct(shape, f32), jax.ShapeDtypeStruct(shape, bf16)]
    return pl.pallas_call(
        kernel,
        out_shape=out_shape,
        in_specs=[in_vmem] * sum(counts),
        out_specs=[in_vmem] * len(out_shape),
        compiler_params=pltpu.CompilerParams(vmem_limit_bytes=VMEM_LIMIT),
        name="coulomb_pairs",
    )(*[part for n in names for part in blocks[n]])


def sum_cores(own, received):
    count = sum(a.shape[0] for a in own)

    def kernel(*refs):
        parts = []
        for mine, theirs in zip(refs[: len(own)], refs[len(own) : -1]):
            total = (mine[...] + theirs[...].astype(f32)).reshape(-1, NXZ, PIECE, TS)
            parts += [total[k] for k in range(total.shape[0])]
        refs[-1][...] = jnp.concatenate(parts, axis=1).astype(bf16)

    return pl.pallas_call(
        kernel,
        out_shape=jax.ShapeDtypeStruct((NXZ, count * PIECE, TS), bf16),
        in_specs=[in_vmem] * (2 * len(own)),
        out_specs=in_vmem,
        compiler_params=pltpu.CompilerParams(vmem_limit_bytes=VMEM_LIMIT),
        name="sum_cores",
    )(*own, *received)


def amplitude_sends(parts, denominator):
    def kernel(parts_ref, denominator_ref, out):
        me = lax.axis_index("pair")
        total = jnp.sum(parts_ref[...].astype(f32), axis=0) / denominator_ref[...]
        out[...] = jnp.zeros_like(out)
        for d, (first, second) in SENDS:
            both = total[first * PIECE : (second + 1) * PIECE]
            out[lax.rem(me + d + NPAIR, NPAIR)] = both.astype(bf16)

    return pl.pallas_call(
        kernel,
        out_shape=jax.ShapeDtypeStruct((NPAIR, 2 * PIECE, TS), bf16),
        in_specs=[in_vmem] * 2,
        out_specs=in_vmem,
        compiler_params=pltpu.CompilerParams(vmem_limit_bytes=VMEM_LIMIT),
        name="amplitude_sends",
    )(parts, denominator)


def amplitude_copies(received):
    rows = len(GETS) * PIECE

    def kernel(received_ref, out):
        me = lax.axis_index("pair")
        pieces = [received_ref[lax.rem(me - d + NPAIR, NPAIR)] for d, _ in SENDS]
        out[...] = jnp.broadcast_to(jnp.concatenate(pieces)[None], out.shape)

    return pl.pallas_call(
        kernel,
        out_shape=jax.ShapeDtypeStruct((NXZ, rows, TS), bf16),
        in_specs=[in_vmem],
        out_specs=in_vmem,
        compiler_params=pltpu.CompilerParams(vmem_limit_bytes=VMEM_LIMIT),
        name="amplitude_copies",
    )(received)


def lay_out(source, part, scale, matrix):
    even = lax.rem(lax.axis_index("pair"), 2) == 0
    place = pl.ds(pl.multiple_of(part * TS, TS), TS)
    for pair in range(0, len(ORDER), 2):
        both = source[:, pair * PIECE : (pair + 2) * PIECE].astype(f32)
        for k in (0, 1):
            i = pair + k
            q, transposed = ORDER[i]
            held = jnp.where(even, HELD.index(held_name(q, 0)), HELD.index(held_name(q, 1)))
            tiles = both[:, k * PIECE : (k + 1) * PIECE].reshape(2, TS, TS)
            for h in (0, 1):
                if transposed:
                    tile = tiles[h].T * scale[2 * i + h : 2 * i + h + 1]
                    matrix[held, h * TS : (h + 1) * TS, place] = tile.astype(bf16)
                else:
                    tile = tiles[h] * scale[pl.ds(2 * i + part, 1)]
                    matrix[held, place, h * TS : (h + 1) * TS] = tile.astype(bf16)


def own_half(mine, scales, far):
    def kernel(mine_ref, scale, *refs):
        sources, (matrix, near, arrived) = refs[: len(far)], refs[len(far) :]
        fetches = []
        start = 0
        for k, source in enumerate(sources):
            place = near.at[start : start + source.shape[0]]
            fetches.append(pltpu.make_async_copy(source, place, arrived.at[k]))
            start += source.shape[0]
        for fetch in fetches:
            fetch.start()
        lay_out(mine_ref, lax.axis_index("core"), scale, matrix)
        for fetch in fetches:
            fetch.wait()

    rows = sum(part.shape[0] for part in far)
    return pl.pallas_call(
        kernel,
        out_shape=(
            jax.ShapeDtypeStruct((len(HELD), WIDTH, WIDTH), bf16),
            jax.ShapeDtypeStruct((rows, WIDTH), bf16),
        ),
        in_specs=[in_vmem, in_vmem] + [anywhere] * len(far),
        out_specs=(in_vmem, in_vmem),
        scratch_shapes=[pltpu.SemaphoreType.DMA((len(far),))],
        compiler_params=pltpu.CompilerParams(vmem_limit_bytes=VMEM_LIMIT),
        name="own_half",
    )(mine, scales, *far)


def gamma_rows(blocks, half, theirs, scales):
    rows, width = blocks[0][0].shape
    counts = [len(blocks[n]) for n in HELD]

    def kernel(*refs):
        given = list(refs[: sum(counts)])
        block = []
        for count in counts:
            block.append(given[:count])
            given = given[count:]
        _, other, scale, out, matrix = refs[sum(counts) :]
        lay_out(other, 1 - lax.axis_index("core"), scale, matrix)
        for start in range(0, rows, ROWS):
            total = None
            for i, parts in enumerate(block):
                part, offset = divmod(start, rows // len(parts))
                left = parts[part][offset : offset + ROWS]
                term = jnp.dot(left, matrix[i], preferred_element_type=f32)
                total = term if total is None else total + term
            out[start : start + ROWS] = total.astype(bf16)

    return pl.pallas_call(
        kernel,
        out_shape=(
            jax.ShapeDtypeStruct((rows, width), bf16),
            jax.ShapeDtypeStruct(half.shape, half.dtype),
        ),
        in_specs=[in_vmem] * (sum(counts) + 3),
        out_specs=(in_vmem, in_vmem),
        input_output_aliases={sum(counts): 1},
        compiler_params=pltpu.CompilerParams(vmem_limit_bytes=VMEM_LIMIT),
        name="gamma_rows",
    )(*[part for n in HELD for part in blocks[n]], half, theirs, scales)[0]


def body(three_index, *energies):
    def swap_a(x):
        return lax.ppermute(x, "pair", SWAP_A)

    def swap_b(x):
        return lax.ppermute(x, "pair", SWAP_B)

    def swap_cores(x):
        return lax.ppermute(x, "core", SWAP_CORES)

    half = three_index.shape[0] // 2
    block = {0: [three_index]}
    block["A", 1] = [swap_a(three_index)]
    block["B", 1] = [swap_b(three_index[:half]), swap_b(three_index[half:])]
    a1 = block["A", 1][0]
    block["B", 2] = [swap_b(a1[:half]), swap_b(a1[half:])]
    block["A", 2] = [swap_a(part) for part in block["B", 1]]

    early, other_early = coulomb_pairs(block, EARLY)
    denominator, scales = tables(*energies)
    other_early, denominator, scales = lax.optimization_barrier((other_early, denominator, scales))
    got_early = swap_cores(other_early)
    late, other_late = coulomb_pairs(block, LATE)
    got_late = swap_cores(other_late)
    summed = sum_cores((early, late), (got_early, got_late))

    summed, b2, a2 = lax.optimization_barrier((summed, block["B", 2], block["A", 2]))
    a3, b3 = [swap_a(part) for part in b2], [swap_b(part) for part in a2]
    parts = lax.all_to_all(summed, ("z", "x"), 0, 0)
    received = lax.all_to_all(amplitude_sends(parts, denominator), "pair", 0, 0)
    copies = amplitude_copies(received)

    copies, a3, b3 = lax.optimization_barrier((copies, a3, b3))
    b4 = [swap_b(a3[0]), swap_a(b3[1])]
    mine = lax.all_to_all(copies, ("z", "x"), 0, 0)
    mine, b4 = lax.optimization_barrier((mine, b4))
    block.update({("B", 2): b2, ("A", 2): a2, ("A", 3): a3, ("B", 3): b3, ("B", 4): b4})
    theirs = swap_cores(mine)
    own, near = own_half(mine, scales, b3)
    block["B", 3] = [near]
    return gamma_rows(block, own, theirs, scales)


def solution(mesh):
    grid = Mesh(mesh.devices.reshape(NX, NZ, NCORE, NPAIR), AUX + ("pair",))
    placed = (P(AUX, "pair"), P(), P(), P(), P(), P())
    return jax.shard_map(
        body, mesh=grid, in_specs=placed, out_specs=P(AUX, "pair"), check_vma=False
    )
```

```python
import jax
import jax.numpy as jnp
from jax import lax
from jax.experimental import pallas as pl
from jax.experimental.pallas import tpu as pltpu
from jax.sharding import Mesh, PartitionSpec as P

TS = 128
VT = 157
NT = 16
NX, NZ, NCORE, NPAIR = 4, 8, 2, 8
NXZ = NX * NZ
AUX = ("x", "z", "core")
EARLY = ((0, 0), (0, 1), (-1, 1))
LATE = ((-1, 2), (-2, 2))
PAIRS = EARLY + LATE
WIDTH = 2 * TS
PIECE = WIDTH // NXZ
SENDS = ((0, (0, 1)), (1, (1, 2)), (-1, (2, 3)), (2, (3, 4)))
GETS = tuple((PAIRS[k][0] - d, PAIRS[k][1] - d) for d, pairs in SENDS for k in pairs)
ORDER = tuple((r, False) if c == 0 else (c, True) for r, c in GETS)
ROWS = 224
VMEM_LIMIT = 12 * 1024 * 1024
bf16, f32 = jnp.bfloat16, jnp.float32
in_vmem = pl.BlockSpec(memory_space=pltpu.VMEM)
anywhere = pl.BlockSpec(memory_space=pl.ANY)
in_smem = pl.BlockSpec(memory_space=pltpu.SMEM)


SWAP_A = [(i, i ^ 1) for i in range(NPAIR)]
SWAP_B = [(i, (i + (-1 if i % 2 == 0 else 1)) % NPAIR) for i in range(NPAIR)]
SWAP_CORES = [(0, 1), (1, 0)]
HELD = (0, ("A", 1), ("B", 1), ("A", 2), ("B", 2), ("A", 3), ("B", 3), ("B", 4))


def held_name(relative, parity):
    if relative == 0:
        return 0
    if abs(relative) == 4:
        return ("B", 4)
    return ("A" if (relative > 0) == (parity == 0) else "B", abs(relative))


def tables(occupied_energy, virtual_energy, tile_occupied, tile_virtual, tile_exponent):
    def kernel(occupied, virtual, occupied_of, virtual_of, exponent, denominator, scales):
        me = lax.axis_index("pair")
        core = lax.axis_index("core")
        slot = lax.axis_index("z") * NX + lax.axis_index("x")
        half, first = slot // (NXZ // 2), (slot % (NXZ // 2)) * PIECE

        def tile_of(relative, part):
            return lax.rem(2 * (me + relative + NPAIR) + part, NT)

        def energy(tile):
            return virtual[pl.ds(virtual_of[tile], 1)] - occupied[occupied_of[tile]]

        def scale(tile):
            level = exponent[tile]
            return jnp.where(level == -1, 0.5, jnp.where(level == 1, 2.0, 1.0)).astype(f32)

        lane = lax.broadcasted_iota(jnp.int32, (PIECE, TS), 1)
        chosen = lane == first + lax.broadcasted_iota(jnp.int32, (PIECE, TS), 0)
        for k, (r, c) in enumerate(PAIRS):
            row, column = tile_of(r, core), tile_of(c, half)
            of_row = jnp.sum(jnp.where(chosen, energy(row), 0.0), axis=1, keepdims=True)
            level = jnp.full((PIECE, TS), scale(row) * scale(column), f32)
            denominator[k * PIECE : (k + 1) * PIECE] = (of_row + energy(column)) / level
        for i, (q, _) in enumerate(ORDER):
            for part in (0, 1):
                n = 2 * i + part
                scales[n : n + 1] = jnp.full((1, TS), scale(tile_of(q, part)), f32)

    return pl.pallas_call(
        kernel,
        out_shape=(
            jax.ShapeDtypeStruct((len(PAIRS) * PIECE, TS), f32),
            jax.ShapeDtypeStruct((2 * len(ORDER), TS), f32),
        ),
        in_specs=[in_smem, in_vmem, in_smem, in_smem, in_smem],
        out_specs=(in_vmem, in_vmem),
        compiler_params=pltpu.CompilerParams(vmem_limit_bytes=VMEM_LIMIT),
        name="tables",
    )(occupied_energy, virtual_energy.reshape(VT, TS), tile_occupied, tile_virtual, tile_exponent)


def coulomb_pairs(blocks, pairs):
    names = [
        n for n in HELD if n in {held_name(d, parity) for pair in pairs for d in pair for parity in (0, 1)}
    ]
    counts = [len(blocks[n]) for n in names]
    rows = sum(part.shape[0] for part in blocks[names[0]])
    most = max(counts)
    height = rows // most

    def kernel(*refs):
        parts = {}
        given = list(refs[: sum(counts)])
        for n, count in zip(names, counts):
            mine, given = given[:count], given[count:]
            parts[n] = mine if count == most else [
                mine[0].at[i * height : (i + 1) * height] for i in range(most)
            ]
        own, other = refs[sum(counts) :]
        core = lax.axis_index("core")
        me = lax.axis_index("pair")
        for parity in (0, 1):

            @pl.when(lax.rem(me, 2) == parity)
            def _(parity=parity):
                for k, (r, c) in enumerate(pairs):
                    for out, part in ((own, core), (other, 1 - core)):
                        place = pl.ds(pl.multiple_of(part * TS, TS), TS)
                        total = None
                        for left, right in zip(parts[held_name(r, parity)], parts[held_name(c, parity)]):
                            term = lax.dot_general(
                                left[:, place], right[...], (((0,), (0,)), ((), ())), preferred_element_type=f32
                            )
                            total = term if total is None else total + term
                        for h in (0, 1):
                            out[k, h] = total[:, h * TS : (h + 1) * TS].astype(out.dtype)

    shape = (len(pairs), 2, TS, TS)
    out_shape = [jax.ShapeDtypeStruct(shape, f32), jax.ShapeDtypeStruct(shape, bf16)]
    return pl.pallas_call(
        kernel,
        out_shape=out_shape,
        in_specs=[in_vmem] * sum(counts),
        out_specs=[in_vmem] * len(out_shape),
        compiler_params=pltpu.CompilerParams(vmem_limit_bytes=VMEM_LIMIT),
        name="coulomb_pairs",
    )(*[part for n in names for part in blocks[n]])


def sum_cores(own, received):
    count = sum(a.shape[0] for a in own)

    def kernel(*refs):
        parts = []
        for mine, theirs in zip(refs[: len(own)], refs[len(own) : -1]):
            total = (mine[...] + theirs[...].astype(f32)).reshape(-1, NXZ, PIECE, TS)
            parts += [total[k] for k in range(total.shape[0])]
        refs[-1][...] = jnp.concatenate(parts, axis=1).astype(bf16)

    return pl.pallas_call(
        kernel,
        out_shape=jax.ShapeDtypeStruct((NXZ, count * PIECE, TS), bf16),
        in_specs=[in_vmem] * (2 * len(own)),
        out_specs=in_vmem,
        compiler_params=pltpu.CompilerParams(vmem_limit_bytes=VMEM_LIMIT),
        name="sum_cores",
    )(*own, *received)


def amplitude_sends(parts, denominator):
    def kernel(parts_ref, denominator_ref, out):
        me = lax.axis_index("pair")
        total = jnp.sum(parts_ref[...].astype(f32), axis=0) / denominator_ref[...]
        out[...] = jnp.zeros_like(out)
        for d, (first, second) in SENDS:
            both = total[first * PIECE : (second + 1) * PIECE]
            out[lax.rem(me + d + NPAIR, NPAIR)] = both.astype(bf16)

    return pl.pallas_call(
        kernel,
        out_shape=jax.ShapeDtypeStruct((NPAIR, 2 * PIECE, TS), bf16),
        in_specs=[in_vmem] * 2,
        out_specs=in_vmem,
        compiler_params=pltpu.CompilerParams(vmem_limit_bytes=VMEM_LIMIT),
        name="amplitude_sends",
    )(parts, denominator)


def amplitude_copies(received):
    rows = len(GETS) * PIECE

    def kernel(received_ref, out):
        me = lax.axis_index("pair")
        pieces = [received_ref[lax.rem(me - d + NPAIR, NPAIR)] for d, _ in SENDS]
        out[...] = jnp.broadcast_to(jnp.concatenate(pieces)[None], out.shape)

    return pl.pallas_call(
        kernel,
        out_shape=jax.ShapeDtypeStruct((NXZ, rows, TS), bf16),
        in_specs=[in_vmem],
        out_specs=in_vmem,
        compiler_params=pltpu.CompilerParams(vmem_limit_bytes=VMEM_LIMIT),
        name="amplitude_copies",
    )(received)


def lay_out(source, part, scale, matrix):
    even = lax.rem(lax.axis_index("pair"), 2) == 0
    place = pl.ds(pl.multiple_of(part * TS, TS), TS)
    for pair in range(0, len(ORDER), 2):
        both = source[:, pair * PIECE : (pair + 2) * PIECE].astype(f32)
        for k in (0, 1):
            i = pair + k
            q, transposed = ORDER[i]
            held = jnp.where(even, HELD.index(held_name(q, 0)), HELD.index(held_name(q, 1)))
            tiles = both[:, k * PIECE : (k + 1) * PIECE].reshape(2, TS, TS)
            for h in (0, 1):
                if transposed:
                    tile = tiles[h].T * scale[2 * i + h : 2 * i + h + 1]
                    matrix[held, h * TS : (h + 1) * TS, place] = tile.astype(bf16)
                else:
                    tile = tiles[h] * scale[pl.ds(2 * i + part, 1)]
                    matrix[held, place, h * TS : (h + 1) * TS] = tile.astype(bf16)


def own_half(mine, scales, far):
    def kernel(mine_ref, scale, *refs):
        sources, (matrix, near, arrived) = refs[: len(far)], refs[len(far) :]
        fetches = []
        start = 0
        for k, source in enumerate(sources):
            place = near.at[start : start + source.shape[0]]
            fetches.append(pltpu.make_async_copy(source, place, arrived.at[k]))
            start += source.shape[0]
        for fetch in fetches:
            fetch.start()
        lay_out(mine_ref, lax.axis_index("core"), scale, matrix)
        for fetch in fetches:
            fetch.wait()

    rows = sum(part.shape[0] for part in far)
    return pl.pallas_call(
        kernel,
        out_shape=(
            jax.ShapeDtypeStruct((len(HELD), WIDTH, WIDTH), bf16),
            jax.ShapeDtypeStruct((rows, WIDTH), bf16),
        ),
        in_specs=[in_vmem, in_vmem] + [anywhere] * len(far),
        out_specs=(in_vmem, in_vmem),
        scratch_shapes=[pltpu.SemaphoreType.DMA((len(far),))],
        compiler_params=pltpu.CompilerParams(vmem_limit_bytes=VMEM_LIMIT),
        name="own_half",
    )(mine, scales, *far)


def gamma_rows(blocks, half, theirs, scales):
    rows, width = blocks[0][0].shape
    counts = [len(blocks[n]) for n in HELD]

    def kernel(*refs):
        given = list(refs[: sum(counts)])
        block = []
        for count in counts:
            block.append(given[:count])
            given = given[count:]
        _, other, scale, out, matrix, held, sent = refs[sum(counts) :]
        sends = []
        lay_out(other, 1 - lax.axis_index("core"), scale, matrix)
        for start in range(0, rows, ROWS):
            total = None
            for i, parts in enumerate(block):
                part, offset = divmod(start, rows // len(parts))
                left = parts[part][offset : offset + ROWS]
                term = jnp.dot(left, matrix[i], preferred_element_type=f32)
                total = term if total is None else total + term
            here = slice(start, start + ROWS)
            held[here] = total.astype(bf16)
            sends.append(pltpu.make_async_copy(held.at[here], out.at[here], sent.at[len(sends)]))
            sends[-1].start()
        for send in sends:
            send.wait()

    return pl.pallas_call(
        kernel,
        out_shape=(
            jax.ShapeDtypeStruct((rows, width), bf16),
            jax.ShapeDtypeStruct(half.shape, half.dtype),
        ),
        in_specs=[in_vmem] * (sum(counts) + 3),
        out_specs=(anywhere, in_vmem),
        scratch_shapes=[
            pltpu.VMEM((rows, width), bf16),
            pltpu.SemaphoreType.DMA((rows // ROWS,)),
        ],
        input_output_aliases={sum(counts): 1},
        compiler_params=pltpu.CompilerParams(vmem_limit_bytes=VMEM_LIMIT),
        name="gamma_rows",
    )(*[part for n in HELD for part in blocks[n]], half, theirs, scales)[0]


def body(three_index, *energies):
    def swap_a(x):
        return lax.ppermute(x, "pair", SWAP_A)

    def swap_b(x):
        return lax.ppermute(x, "pair", SWAP_B)

    def swap_cores(x):
        return lax.ppermute(x, "core", SWAP_CORES)

    half = three_index.shape[0] // 2
    block = {0: [three_index]}
    block["A", 1] = [swap_a(three_index)]
    block["B", 1] = [swap_b(three_index[:half]), swap_b(three_index[half:])]
    block["B", 2] = [swap_b(block["A", 1][0])]
    block["A", 2] = [swap_a(part) for part in block["B", 1]]

    early, other_early = coulomb_pairs(block, EARLY)
    denominator, scales = tables(*energies)
    other_early, denominator, scales = lax.optimization_barrier((other_early, denominator, scales))
    got_early = swap_cores(other_early)
    late, other_late = coulomb_pairs(block, LATE)
    got_late = swap_cores(other_late)
    summed = sum_cores((early, late), (got_early, got_late))

    summed, b2, a2 = lax.optimization_barrier((summed, block["B", 2], block["A", 2]))
    a3, b3 = swap_a(b2[0]), [swap_b(part) for part in a2]
    parts = lax.all_to_all(summed, ("z", "x"), 0, 0)
    received = lax.all_to_all(amplitude_sends(parts, denominator), "pair", 0, 0)
    copies = amplitude_copies(received)

    copies, a3, b3 = lax.optimization_barrier((copies, a3, b3))
    b4 = [swap_b(a3[:half]), swap_a(b3[1])]
    mine = lax.all_to_all(copies, ("z", "x"), 0, 0)
    mine, b4 = lax.optimization_barrier((mine, b4))
    block.update({("B", 2): b2, ("A", 2): a2, ("A", 3): [a3], ("B", 3): b3, ("B", 4): b4})
    theirs = swap_cores(mine)
    own, near = own_half(mine, scales, b3)
    block["B", 3] = [near]
    return gamma_rows(block, own, theirs, scales)


def solution(mesh):
    grid = Mesh(mesh.devices.reshape(NX, NZ, NCORE, NPAIR), AUX + ("pair",))
    placed = (P(AUX, "pair"), P(), P(), P(), P(), P())
    return jax.shard_map(
        body, mesh=grid, in_specs=placed, out_specs=P(AUX, "pair"), check_vma=False
    )
```

```python
import jax
import jax.numpy as jnp
from jax import lax
from jax.experimental import pallas as pl
from jax.experimental.pallas import tpu as pltpu
from jax.sharding import Mesh, PartitionSpec as P

TS = 128
VT = 157
NT = 16
NX, NZ, NCORE, NPAIR = 4, 8, 2, 8
NXZ = NX * NZ
AUX = ("x", "z", "core")
EARLY = ((0, 0), (0, 1), (-1, 1))
LATE = ((-1, 2), (-2, 2))
PAIRS = EARLY + LATE
WIDTH = 2 * TS
PIECE = WIDTH // NXZ
SENDS = ((0, (0, 1)), (1, (1, 2)), (-1, (2, 3)), (2, (3, 4)))
GETS = tuple((PAIRS[k][0] - d, PAIRS[k][1] - d) for d, pairs in SENDS for k in pairs)
ORDER = tuple((r, False) if c == 0 else (c, True) for r, c in GETS)
ROWS = 224
VMEM_LIMIT = 12 * 1024 * 1024
bf16, f32 = jnp.bfloat16, jnp.float32
in_vmem = pl.BlockSpec(memory_space=pltpu.VMEM)
anywhere = pl.BlockSpec(memory_space=pl.ANY)
in_smem = pl.BlockSpec(memory_space=pltpu.SMEM)


SWAP_A = [(i, i ^ 1) for i in range(NPAIR)]
SWAP_B = [(i, (i + (-1 if i % 2 == 0 else 1)) % NPAIR) for i in range(NPAIR)]
SWAP_CORES = [(0, 1), (1, 0)]
HELD = (0, ("A", 1), ("B", 1), ("A", 2), ("B", 2), ("A", 3), ("B", 3), ("B", 4))


def held_name(relative, parity):
    if relative == 0:
        return 0
    if abs(relative) == 4:
        return ("B", 4)
    return ("A" if (relative > 0) == (parity == 0) else "B", abs(relative))


def tables(occupied_energy, virtual_energy, tile_occupied, tile_virtual, tile_exponent):
    def kernel(occupied, virtual, occupied_of, virtual_of, exponent, denominator, scales):
        me = lax.axis_index("pair")
        core = lax.axis_index("core")
        slot = lax.axis_index("z") * NX + lax.axis_index("x")
        half, first = slot // (NXZ // 2), (slot % (NXZ // 2)) * PIECE

        def tile_of(relative, part):
            return lax.rem(2 * (me + relative + NPAIR) + part, NT)

        def energy(tile):
            return virtual[pl.ds(virtual_of[tile], 1)] - occupied[occupied_of[tile]]

        def scale(tile):
            level = exponent[tile]
            return jnp.where(level == -1, 0.5, jnp.where(level == 1, 2.0, 1.0)).astype(f32)

        lane = lax.broadcasted_iota(jnp.int32, (PIECE, TS), 1)
        chosen = lane == first + lax.broadcasted_iota(jnp.int32, (PIECE, TS), 0)
        for k, (r, c) in enumerate(PAIRS):
            row, column = tile_of(r, core), tile_of(c, half)
            of_row = jnp.sum(jnp.where(chosen, energy(row), 0.0), axis=1, keepdims=True)
            level = jnp.full((PIECE, TS), scale(row) * scale(column), f32)
            denominator[k * PIECE : (k + 1) * PIECE] = (of_row + energy(column)) / level
        for i, (q, _) in enumerate(ORDER):
            for part in (0, 1):
                n = 2 * i + part
                scales[n : n + 1] = jnp.full((1, TS), scale(tile_of(q, part)), f32)

    return pl.pallas_call(
        kernel,
        out_shape=(
            jax.ShapeDtypeStruct((len(PAIRS) * PIECE, TS), f32),
            jax.ShapeDtypeStruct((2 * len(ORDER), TS), f32),
        ),
        in_specs=[in_smem, in_vmem, in_smem, in_smem, in_smem],
        out_specs=(in_vmem, in_vmem),
        compiler_params=pltpu.CompilerParams(vmem_limit_bytes=VMEM_LIMIT),
        name="tables",
    )(occupied_energy, virtual_energy.reshape(VT, TS), tile_occupied, tile_virtual, tile_exponent)


def coulomb_pairs(blocks, pairs):
    names = [
        n for n in HELD if n in {held_name(d, parity) for pair in pairs for d in pair for parity in (0, 1)}
    ]
    counts = [len(blocks[n]) for n in names]
    rows = sum(part.shape[0] for part in blocks[names[0]])
    most = max(counts)
    height = rows // most

    def kernel(*refs):
        parts = {}
        given = list(refs[: sum(counts)])
        for n, count in zip(names, counts):
            mine, given = given[:count], given[count:]
            parts[n] = mine if count == most else [
                mine[0].at[i * height : (i + 1) * height] for i in range(most)
            ]
        own, other = refs[sum(counts) :]
        core = lax.axis_index("core")
        me = lax.axis_index("pair")
        for parity in (0, 1):

            @pl.when(lax.rem(me, 2) == parity)
            def _(parity=parity):
                for k, (r, c) in enumerate(pairs):
                    for out, part in ((own, core), (other, 1 - core)):
                        place = pl.ds(pl.multiple_of(part * TS, TS), TS)
                        total = None
                        for left, right in zip(parts[held_name(r, parity)], parts[held_name(c, parity)]):
                            term = lax.dot_general(
                                left[:, place], right[...], (((0,), (0,)), ((), ())), preferred_element_type=f32
                            )
                            total = term if total is None else total + term
                        for h in (0, 1):
                            out[k, h] = total[:, h * TS : (h + 1) * TS].astype(out.dtype)

    shape = (len(pairs), 2, TS, TS)
    out_shape = [jax.ShapeDtypeStruct(shape, f32), jax.ShapeDtypeStruct(shape, bf16)]
    return pl.pallas_call(
        kernel,
        out_shape=out_shape,
        in_specs=[in_vmem] * sum(counts),
        out_specs=[in_vmem] * len(out_shape),
        compiler_params=pltpu.CompilerParams(vmem_limit_bytes=VMEM_LIMIT),
        name="coulomb_pairs",
    )(*[part for n in names for part in blocks[n]])


def sum_cores(own, received):
    count = sum(a.shape[0] for a in own)

    def kernel(*refs):
        parts = []
        for mine, theirs in zip(refs[: len(own)], refs[len(own) : -1]):
            total = (mine[...] + theirs[...].astype(f32)).reshape(-1, NXZ, PIECE, TS)
            parts += [total[k] for k in range(total.shape[0])]
        refs[-1][...] = jnp.concatenate(parts, axis=1).astype(bf16)

    return pl.pallas_call(
        kernel,
        out_shape=jax.ShapeDtypeStruct((NXZ, count * PIECE, TS), bf16),
        in_specs=[in_vmem] * (2 * len(own)),
        out_specs=in_vmem,
        compiler_params=pltpu.CompilerParams(vmem_limit_bytes=VMEM_LIMIT),
        name="sum_cores",
    )(*own, *received)


def amplitude_sends(parts, denominator):
    def kernel(parts_ref, denominator_ref, out):
        me = lax.axis_index("pair")
        total = jnp.sum(parts_ref[...].astype(f32), axis=0) / denominator_ref[...]
        out[...] = jnp.zeros_like(out)
        for d, (first, second) in SENDS:
            both = total[first * PIECE : (second + 1) * PIECE]
            out[lax.rem(me + d + NPAIR, NPAIR)] = both.astype(bf16)

    return pl.pallas_call(
        kernel,
        out_shape=jax.ShapeDtypeStruct((NPAIR, 2 * PIECE, TS), bf16),
        in_specs=[in_vmem] * 2,
        out_specs=in_vmem,
        compiler_params=pltpu.CompilerParams(vmem_limit_bytes=VMEM_LIMIT),
        name="amplitude_sends",
    )(parts, denominator)


def amplitude_copies(received):
    rows = len(GETS) * PIECE

    def kernel(received_ref, out):
        me = lax.axis_index("pair")
        pieces = [received_ref[lax.rem(me - d + NPAIR, NPAIR)] for d, _ in SENDS]
        out[...] = jnp.broadcast_to(jnp.concatenate(pieces)[None], out.shape)

    return pl.pallas_call(
        kernel,
        out_shape=jax.ShapeDtypeStruct((NXZ, rows, TS), bf16),
        in_specs=[in_vmem],
        out_specs=in_vmem,
        compiler_params=pltpu.CompilerParams(vmem_limit_bytes=VMEM_LIMIT),
        name="amplitude_copies",
    )(received)


def lay_out(source, part, scale, matrix):
    even = lax.rem(lax.axis_index("pair"), 2) == 0
    place = pl.ds(pl.multiple_of(part * TS, TS), TS)
    for pair in range(0, len(ORDER), 2):
        both = source[:, pair * PIECE : (pair + 2) * PIECE].astype(f32)
        for k in (0, 1):
            i = pair + k
            q, transposed = ORDER[i]
            held = jnp.where(even, HELD.index(held_name(q, 0)), HELD.index(held_name(q, 1)))
            tiles = both[:, k * PIECE : (k + 1) * PIECE].reshape(2, TS, TS)
            for h in (0, 1):
                if transposed:
                    tile = tiles[h].T * scale[2 * i + h : 2 * i + h + 1]
                    matrix[held, h * TS : (h + 1) * TS, place] = tile.astype(bf16)
                else:
                    tile = tiles[h] * scale[pl.ds(2 * i + part, 1)]
                    matrix[held, place, h * TS : (h + 1) * TS] = tile.astype(bf16)


def own_half(mine, scales, far):
    def kernel(mine_ref, scale, *refs):
        sources, (matrix, near, arrived) = refs[: len(far)], refs[len(far) :]
        fetches = []
        start = 0
        for k, source in enumerate(sources):
            place = near.at[start : start + source.shape[0]]
            fetches.append(pltpu.make_async_copy(source, place, arrived.at[k]))
            start += source.shape[0]
        for fetch in fetches:
            fetch.start()
        lay_out(mine_ref, lax.axis_index("core"), scale, matrix)
        for fetch in fetches:
            fetch.wait()

    rows = sum(part.shape[0] for part in far)
    return pl.pallas_call(
        kernel,
        out_shape=(
            jax.ShapeDtypeStruct((len(HELD), WIDTH, WIDTH), bf16),
            jax.ShapeDtypeStruct((rows, WIDTH), bf16),
        ),
        in_specs=[in_vmem, in_vmem] + [anywhere] * len(far),
        out_specs=(in_vmem, in_vmem),
        scratch_shapes=[pltpu.SemaphoreType.DMA((len(far),))],
        compiler_params=pltpu.CompilerParams(vmem_limit_bytes=VMEM_LIMIT),
        name="own_half",
    )(mine, scales, *far)


def gamma_rows(blocks, half, theirs, scales):
    rows, width = blocks[0][0].shape
    counts = [len(blocks[n]) for n in HELD]

    def kernel(*refs):
        given = list(refs[: sum(counts)])
        block = []
        for count in counts:
            block.append(given[:count])
            given = given[count:]
        _, other, scale, out, matrix, held, sent = refs[sum(counts) :]
        sends = []
        lay_out(other, 1 - lax.axis_index("core"), scale, matrix)
        for start in range(0, rows, ROWS):
            total = None
            for i, parts in enumerate(block):
                part, offset = divmod(start, rows // len(parts))
                left = parts[part][offset : offset + ROWS]
                term = jnp.dot(left, matrix[i], preferred_element_type=f32)
                total = term if total is None else total + term
            here = slice(start, start + ROWS)
            held[here] = total.astype(bf16)
            sends.append(pltpu.make_async_copy(held.at[here], out.at[here], sent.at[len(sends)]))
            sends[-1].start()
        for send in sends:
            send.wait()

    return pl.pallas_call(
        kernel,
        out_shape=(
            jax.ShapeDtypeStruct((rows, width), bf16),
            jax.ShapeDtypeStruct(half.shape, half.dtype),
        ),
        in_specs=[in_vmem] * (sum(counts) + 3),
        out_specs=(anywhere, in_vmem),
        scratch_shapes=[
            pltpu.VMEM((rows, width), bf16),
            pltpu.SemaphoreType.DMA((rows // ROWS,)),
        ],
        input_output_aliases={sum(counts): 1},
        compiler_params=pltpu.CompilerParams(vmem_limit_bytes=VMEM_LIMIT),
        name="gamma_rows",
    )(*[part for n in HELD for part in blocks[n]], half, theirs, scales)[0]


def body(three_index, *energies):
    def swap_a(x):
        return lax.ppermute(x, "pair", SWAP_A)

    def swap_b(x):
        return lax.ppermute(x, "pair", SWAP_B)

    def swap_cores(x):
        return lax.ppermute(x, "core", SWAP_CORES)

    half = three_index.shape[0] // 2
    block = {0: [three_index]}
    block["A", 1] = [swap_a(three_index)]
    block["B", 1] = [swap_b(three_index[:half]), swap_b(three_index[half:])]
    block["B", 2] = [swap_b(block["A", 1][0])]
    block["A", 2] = [swap_a(part) for part in block["B", 1]]

    early, other_early = coulomb_pairs(block, EARLY)
    denominator, scales = tables(*energies)
    other_early, denominator, scales = lax.optimization_barrier((other_early, denominator, scales))
    got_early = swap_cores(other_early)
    late, other_late = coulomb_pairs(block, LATE)
    got_late = swap_cores(other_late)
    summed = sum_cores((early, late), (got_early, got_late))

    summed, b2, a2 = lax.optimization_barrier((summed, block["B", 2], block["A", 2]))
    a3, b3 = swap_a(b2[0]), [None, swap_b(a2[1])]
    parts = lax.all_to_all(summed, ("z", "x"), 0, 0)
    received = lax.all_to_all(amplitude_sends(parts, denominator), "pair", 0, 0)
    copies = amplitude_copies(received)

    copies, a3, b3[1], a2 = lax.optimization_barrier((copies, a3, b3[1], a2))
    b3[0] = swap_b(a2[0])
    b4 = [swap_b(a3[:half]), swap_a(b3[1])]
    mine = lax.all_to_all(copies, ("z", "x"), 0, 0)
    mine, b4, b3 = lax.optimization_barrier((mine, b4, b3))
    block.update({("B", 2): b2, ("A", 2): a2, ("A", 3): [a3], ("B", 3): b3, ("B", 4): b4})
    theirs = swap_cores(mine)
    own, near = own_half(mine, scales, b3)
    block["B", 3] = [near]
    return gamma_rows(block, own, theirs, scales)


def solution(mesh):
    grid = Mesh(mesh.devices.reshape(NX, NZ, NCORE, NPAIR), AUX + ("pair",))
    placed = (P(AUX, "pair"), P(), P(), P(), P(), P())
    return jax.shard_map(
        body, mesh=grid, in_specs=placed, out_specs=P(AUX, "pair"), check_vma=False
    )
```
